32 devices in a mesh: dp: 8 (over z, x), mp: 4 (over y, core).
Axes of the slice: x: 2, y: 2, z: 4, core: 2. Of those that a mesh axis runs over, the one named last changes fastest.
Arguments:
- time_in: bfloat16 [8, 336, 384], P('dp', 'mp'), may hold values from -6 to 6
- spec_in: bfloat16 [8, 2048, 384], P('dp', 'mp'), may hold values from -6 to 6
- rate_flags: int32 [8], P('dp'), may hold values 0 or 1
- band_limits: int32 [8], P('dp'), may hold values from 1 to 8
- time_cot: bfloat16 [8, 336, 384], P('dp', 'mp'), may hold values from -6 to 6
- spec_cot: bfloat16 [8, 2048, 384], P('dp', 'mp'), may hold values from -6 to 6
- attn_in: float32 [4, 3, 384, 384], P(None, None, 'mp'), may hold values from -0.3125 to 0.3125
- attn_out: float32 [4, 384, 384], P(None, 'mp'), may hold values from -3.6742346 to 3.6742346
- ffn_in: float32 [384, 1536], P(None, 'mp'), may hold values from -0.3125 to 0.3125
- ffn_out: float32 [1536, 384], P('mp'), may hold values from -0.30618622 to 0.30618622
- small: float32 [19, 384], replicated, may hold values from -1.2 to 1.5
- attn_in_m: float32 [4, 3, 384, 384], P(None, None, 'mp'), may hold values from -0.03125 to 0.03125
- attn_in_v: float32 [4, 3, 384, 384], P(None, None, 'mp'), may hold values from 0.00014832611 to 0.00059330446
- attn_out_m: float32 [4, 384, 384], P(None, 'mp'), may hold values from -0.01171875 to 0.01171875
- attn_out_v: float32 [4, 384, 384], P(None, 'mp'), may hold values from 1.1279552e-05 to 4.511821e-05
- ffn_in_m: float32 [384, 1536], P(None, 'mp'), may hold values from -0.03125 to 0.03125
- ffn_in_v: float32 [384, 1536], P(None, 'mp'), may hold values from 0.00014832611 to 0.00059330446
- ffn_out_m: float32 [1536, 384], P('mp'), may hold values from -0.01171875 to 0.01171875
- ffn_out_v: float32 [1536, 384], P('mp'), may hold values from 1.1279552e-05 to 4.511821e-05
- small_m: float32 [19, 384], replicated, may hold values from -0.03125 to 0.03125
- small_v: float32 [19, 384], replicated, may hold values from 0.00014832611 to 0.00059330446
Outputs:
- time_out: float32 [8, 336, 384], P('dp', 'mp')
- spec_out: float32 [8, 2048, 384], P('dp', 'mp')
- time_grad: float32 [8, 336, 384], P('dp', 'mp')
- spec_grad: float32 [8, 2048, 384], P('dp', 'mp')
- grad_norm: float32 [], replicated
- attn_in_new: float32 [4, 3, 384, 384], P(None, None, 'mp')
- attn_in_m_new: float32 [4, 3, 384, 384], P(None, None, 'mp')
- attn_in_v_new: float32 [4, 3, 384, 384], P(None, None, 'mp')
- attn_out_new: float32 [4, 384, 384], P(None, 'mp')
- attn_out_m_new: float32 [4, 384, 384], P(None, 'mp')
- attn_out_v_new: float32 [4, 384, 384], P(None, 'mp')
- ffn_in_new: float32 [384, 1536], P(None, 'mp')
- ffn_in_m_new: float32 [384, 1536], P(None, 'mp')
- ffn_in_v_new: float32 [384, 1536], P(None, 'mp')
- ffn_out_new: float32 [1536, 384], P('mp')
- ffn_out_m_new: float32 [1536, 384], P('mp')
- ffn_out_v_new: float32 [1536, 384], P('mp')
- small_new: float32 [19, 384], replicated
- small_m_new: float32 [19, 384], replicated
- small_v_new: float32 [19, 384], replicated
- shift_gradient: float32 [384], replicated
The draws below stay inside these ranges and needn't reach their ends.
All inputs are finite; a program needn't handle non-finite values. No bound on the sum of `rate_flags` on one device may be relied on, other than what follows from the above.
Results may differ from the reference program's by a relative error of at most 0.025.
Values may be sent and summed in bfloat16 or wider, within the bound.
A program may use at most 192 MiB of HBM per device.

```python
import math
import jax
import jax.numpy as jnp
from jax import lax

D = 384
HEADS = 8
HD = 48
FF = 1536
LT = 336
FBINS = 8
FRAMES = 256
LF = 2048
ITEMS = 8
NSMALL = 19
STEP = 10


def draw_attn_out(key, part):
    key = jax.random.fold_in(key, 11)
    position = jnp.arange(D, dtype=jnp.float32) / (D - 1)
    rise_rows = 1.0 + 2.0 * position
    base_draw = jax.random.truncated_normal(key, -4.0, 4.0, (4, D, D), jnp.float32)
    return base_draw * (6.0 / math.sqrt(D)) * rise_rows[None, :, None]


def draw_ffn_out(key, part):
    key = jax.random.fold_in(key, 12)
    position = jnp.arange(FF, dtype=jnp.float32) / (FF - 1)
    rise_rows = 1.0 + 2.0 * position
    base_draw = jax.random.truncated_normal(key, -4.0, 4.0, (FF, D), jnp.float32)
    return base_draw * (1.0 / math.sqrt(FF)) * rise_rows[:, None]


def draw_small(key, part):
    key = jax.random.fold_in(key, 13)
    first_key, second_key = jax.random.split(key)
    uniform_part = jax.random.uniform(first_key, (NSMALL, D), jnp.float32)
    normal_part = jax.random.truncated_normal(second_key, -4.0, 4.0, (NSMALL, D), jnp.float32)
    row_index = jnp.arange(NSMALL, dtype=jnp.int32)[:, None]
    gains = 0.6 + 0.8 * uniform_part
    shifts = 0.3 * normal_part
    scales = 0.5 + uniform_part
    return jnp.where(row_index >= 14, scales, jnp.where(row_index % 2 == 0, gains, shifts))


def plant(drawn, rng, low, high):
    shape = drawn.shape
    place = [jax.random.randint(jax.random.fold_in(rng, axis), (), 0, shape[axis]) for axis in range(len(shape))]
    drawn = drawn.at[tuple(place)].set(low)
    longest = shape.index(max(shape))
    place[longest] = (place[longest] + 1) % shape[longest]
    return drawn.at[tuple(place)].set(high)


def shard_levels(stream_key, dims, pieces, low, top_value):
    gain, own = 1.0, jax.random.fold_in(stream_key, 6)
    for dim, shards_of in pieces:
        steps = jnp.exp(jax.random.uniform(jax.random.fold_in(own, dim), (shards_of,), jnp.float32, low / len(pieces), top_value / len(pieces)))
        gain = gain * jnp.repeat(steps, dims[dim] // shards_of).reshape([-1 if axis == dim else 1 for axis in range(len(dims))])
    return gain


def scatter_about(rng, extent, scale, reach, cuts=(), kind=jnp.bfloat16):
    values = scale * jax.random.normal(rng, extent, jnp.float32)
    if cuts:
        values = values * shard_levels(rng, extent, cuts, -0.22, 0.18)
    return jnp.clip(values, -reach, reach).astype(kind)


def setup_inputs(seed: int = 0) -> dict:
    keys = jax.random.split(jax.random.key(seed), 22)
    return {
        "time_in": scatter_about(keys[0], (ITEMS, LT, D), 1.0, 6.0, ((0, 8), (1, 4))),
        "spec_in": scatter_about(keys[1], (ITEMS, LF, D), 1.0, 6.0, ((0, 8), (1, 4))),
        "rate_flags": plant((jax.random.randint(keys[2], (ITEMS,), 0, 2) < 1).astype(jnp.int32), jax.random.fold_in(keys[2], 1), 0, 1),
        "band_limits": plant(jax.random.randint(keys[3], (ITEMS,), 1, FBINS + 1), jax.random.fold_in(keys[3], 1), 1, FBINS).astype(jnp.int32),
        "time_cot": scatter_about(keys[4], (ITEMS, LT, D), 1.0, 6.0, ((0, 8), (1, 4))),
        "spec_cot": scatter_about(keys[5], (ITEMS, LF, D), 1.0, 6.0, ((0, 8), (1, 4))),
        "attn_in": scatter_about(keys[6], (4, 3, D, D), D ** -0.5, 0.3125, ((2, 4),), jnp.float32),
        "attn_out": draw_attn_out(jax.random.fold_in(keys[21], 71), 0),
        "ffn_in": scatter_about(keys[8], (D, FF), D ** -0.5, 0.3125, ((1, 4),), jnp.float32),
        "ffn_out": draw_ffn_out(jax.random.fold_in(keys[21], 71), 0),
        "small": draw_small(jax.random.fold_in(keys[21], 71), 0),
        "attn_in_m": scatter_about(keys[11], (4, 3, D, D), (11.1 * (16 * D * D + 2 * D * FF + NSMALL * D) ** -0.5), 0.03125, ((2, 4),), jnp.float32),
        "attn_in_v": jnp.clip(jnp.exp(math.log(0.00059330446) - 1.3862944 * jax.random.uniform(keys[12], (4, 3, D, D), jnp.float32) ** shard_levels(keys[12], (4, 3, D, D), ((2, 4),), -0.2, 0.2)), 0.00014832611, 0.00059330446),
        "attn_out_m": scatter_about(keys[13], (4, D, D), (3.7 * (16 * D * D + 2 * D * FF + NSMALL * D) ** -0.5), 0.01171875, ((1, 4),), jnp.float32),
        "attn_out_v": jnp.clip(jnp.exp(math.log(4.511820952757262e-05) - 1.3862944 * jax.random.uniform(keys[14], (4, D, D), jnp.float32) ** shard_levels(keys[14], (4, D, D), ((1, 4),), -0.2, 0.2)), 1.1279552381893154e-05, 4.511820952757262e-05),
        "ffn_in_m": scatter_about(keys[15], (D, FF), (11.1 * (16 * D * D + 2 * D * FF + NSMALL * D) ** -0.5), 0.03125, ((1, 4),), jnp.float32),
        "ffn_in_v": jnp.clip(jnp.exp(math.log(0.00059330446) - 1.3862944 * jax.random.uniform(keys[16], (D, FF), jnp.float32) ** shard_levels(keys[16], (D, FF), ((1, 4),), -0.2, 0.2)), 0.00014832611, 0.00059330446),
        "ffn_out_m": scatter_about(keys[17], (FF, D), (3.7 * (16 * D * D + 2 * D * FF + NSMALL * D) ** -0.5), 0.01171875, ((0, 4),), jnp.float32),
        "ffn_out_v": jnp.clip(jnp.exp(math.log(4.511820952757262e-05) - 1.3862944 * jax.random.uniform(keys[18], (FF, D), jnp.float32) ** shard_levels(keys[18], (FF, D), ((0, 4),), -0.2, 0.2)), 1.1279552381893154e-05, 4.511820952757262e-05),
        "small_m": scatter_about(keys[19], (NSMALL, D), (11.1 * (16 * D * D + 2 * D * FF + NSMALL * D) ** -0.5), 0.03125, (), jnp.float32),
        "small_v": jnp.clip(jnp.exp(jax.random.uniform(keys[20], (NSMALL, D), jnp.float32, math.log(0.00014832611), math.log(0.00059330446))), 0.00014832611, 0.00059330446),
    }


@jax.custom_vjp
def low(v):
    return lax.optimization_barrier(v.astype(jnp.bfloat16)).astype(jnp.float32)

@jax.custom_vjp
def low_back(v):
    return v

def low_keep(v):
    return (low(v), None)

def low_pass(kept, grad):
    return (grad,)

def back_keep(v):
    return (v, None)

def back_low(kept, grad):
    return (low(grad),)
low.defvjp(low_keep, low_pass)
low_back.defvjp(back_keep, back_low)
norm_eps = 1e-05
clip_level = 100.0
beta_first = 0.9
beta_second = 0.95
adam_eps = 1e-08
decay_matrix = 0.1
rate_matrix = 0.05
rate_output = 0.5
rate_small = 0.5
masked_score = -1000000000.0

def both_ways(values):
    return low(low_back(values))

def product(left, right):
    return jnp.dot(left, right, precision=lax.Precision.HIGHEST, preferred_element_type=jnp.float32)

def layer_norm(stream, small, row):
    center = stream - lax.optimization_barrier(jnp.mean(stream, axis=-1, keepdims=True))
    spread = lax.optimization_barrier(jnp.mean(center * center, axis=-1, keepdims=True))
    return center * lax.rsqrt(spread + norm_eps) * small[row] + small[row + 1]

def attention(queries_in, keys_in, w_in, w_out, live_keys):
    queries = both_ways(product(queries_in, w_in[0].T))
    key_rows = both_ways(product(keys_in, w_in[1].T))
    values = both_ways(product(keys_in, w_in[2].T))
    rows_q = queries.shape[0]
    rows_k = key_rows.shape[0]
    query_heads = queries.reshape(rows_q, HEADS, HD)
    key_heads = key_rows.reshape(rows_k, HEADS, HD)
    value_heads = values.reshape(rows_k, HEADS, HD)
    raw_score = low_back(jnp.einsum('qhd,khd->hqk', query_heads, key_heads, precision=lax.Precision.HIGHEST))
    scores = raw_score * HD ** (-0.5)
    scores = jnp.where(live_keys[None, None, :] > 0, scores, masked_score)
    peak_score = lax.optimization_barrier(jnp.max(scores, axis=-1, keepdims=True))
    exponent = jnp.exp(scores - peak_score)
    shares = exponent / lax.optimization_barrier(jnp.sum(exponent, axis=-1, keepdims=True))
    mixed = jnp.einsum('hqk,khd->qhd', low(shares), value_heads, precision=lax.Precision.HIGHEST)
    mixed = both_ways(mixed.reshape(rows_q, D))
    return low_back(product(mixed, w_out))

def feed_forward(stream, small, w_first, w_second):
    normed = low(layer_norm(stream, small, 12))
    hidden = low_back(product(normed, w_first))
    active = low(jax.nn.gelu(hidden, approximate=False))
    return low_back(product(active, w_second))

def layer(attn_in, attn_out, ffn_in, ffn_out, small, time_zero, spec_zero, live_keys):
    w_in = low(attn_in)
    w_out = low(attn_out)
    w_first = low(ffn_in)
    w_second = low(ffn_out)
    all_keys = jnp.ones((time_zero.shape[0],), jnp.int32)
    normed_time = low(layer_norm(time_zero, small, 0))
    time_one = time_zero + small[14] * attention(normed_time, normed_time, w_in[0], w_out[0], all_keys)
    normed_spec = low(layer_norm(spec_zero, small, 2))
    spec_one = spec_zero + small[15] * attention(normed_spec, normed_spec, w_in[1], w_out[1], live_keys)
    time_two = time_one + small[16] * attention(low(layer_norm(time_one, small, 4)), low(layer_norm(spec_one, small, 6)), w_in[2], w_out[2], live_keys)
    spec_two = spec_one + small[17] * attention(low(layer_norm(spec_one, small, 8)), low(layer_norm(time_one, small, 10)), w_in[3], w_out[3], all_keys)
    time_three = time_two + small[18] * feed_forward(time_two, small, w_first, w_second)
    spec_three = spec_two + small[18] * feed_forward(spec_two, small, w_first, w_second)
    return (time_three, spec_three)

def adam_update(weight, first_moment, second_moment, gradient, step_rate, decay_rate):
    first_new = beta_first * first_moment + (1.0 - beta_first) * gradient
    second_new = beta_second * second_moment + (1.0 - beta_second) * gradient * gradient
    first_fix = 1.0 - beta_first ** STEP
    second_fix = 1.0 - beta_second ** STEP
    direction = first_new / first_fix / (jnp.sqrt(second_new / second_fix) + adam_eps)
    return (weight - step_rate * (direction + decay_rate * weight), first_new, second_new)

def reference(time_in, spec_in, rate_flags, band_limits, time_cot, spec_cot, attn_in, attn_out, ffn_in, ffn_out, small, attn_in_m, attn_in_v, attn_out_m, attn_out_v, ffn_in_m, ffn_in_v, ffn_out_m, ffn_out_v, small_m, small_v):
    weights = (attn_in, attn_out, ffn_in, ffn_out, small)
    key_bins = jnp.arange(spec_in.shape[1], dtype=jnp.int32) // FRAMES

    def one_item(totals, entry_data):
        time_part, spec_part, rate_flag, band_limit, time_dy, spec_dy = entry_data
        live_keys = jnp.maximum((key_bins < band_limit).astype(jnp.int32), (rate_flag == 0).astype(jnp.int32))

        def run_layer(w_a, w_b, w_c, w_d, w_e, time_arg, spec_arg):
            return layer(w_a, w_b, w_c, w_d, w_e, time_arg, spec_arg, live_keys)
        results, pullback = jax.vjp(run_layer, attn_in, attn_out, ffn_in, ffn_out, small, time_part.astype(jnp.float32), spec_part.astype(jnp.float32))
        gradients = pullback((time_dy.astype(jnp.float32), spec_dy.astype(jnp.float32)))
        totals = tuple((running + gradients[index] for index, running in enumerate(totals)))
        return (totals, (results[0], results[1], gradients[5], gradients[6]))
    empty_sums = tuple((jnp.zeros_like(weight) for weight in weights))
    totals, stacked = lax.scan(one_item, empty_sums, (time_in, spec_in, rate_flags, band_limits, time_cot, spec_cot))
    time_out, spec_out, time_grad, spec_grad = stacked
    squares = jnp.sum(totals[0] * totals[0]) + jnp.sum(totals[1] * totals[1]) + jnp.sum(totals[2] * totals[2])
    squares = squares + jnp.sum(totals[3] * totals[3]) + jnp.sum(totals[4] * totals[4])
    grad_norm = jnp.sqrt(squares)
    factor = jnp.minimum(1.0, clip_level / grad_norm)
    moments = ((attn_in_m, attn_in_v), (attn_out_m, attn_out_v), (ffn_in_m, ffn_in_v), (ffn_out_m, ffn_out_v))
    rates = (rate_matrix, rate_output, rate_matrix, rate_matrix)
    updated = []
    for index in range(4):
        updated.append(adam_update(weights[index], moments[index][0], moments[index][1], totals[index] * factor, rates[index], decay_matrix))
    small_clipped = totals[4] * factor
    small_new, small_m_new, small_v_new = adam_update(small, small_m, small_v, small_clipped, rate_small, 0.0)
    shift_gradient = small_clipped[13]
    return (time_out, spec_out, time_grad, spec_grad, grad_norm, updated[0][0], updated[0][1], updated[0][2], updated[1][0], updated[1][1], updated[1][2], updated[2][0], updated[2][1], updated[2][2], updated[3][0], updated[3][1], updated[3][2], small_new, small_m_new, small_v_new, shift_gradient)
```

```python
import functools
import math

import jax
import jax.numpy as jnp
from jax import lax
from jax.experimental import pallas as pl
from jax.experimental.pallas import tpu as pltpu
from jax.sharding import PartitionSpec as P

HD = 48
HP = 64
LANES = 128
FRAMES = 256
STEP = 10
BF = jnp.bfloat16
F32 = jnp.float32
NN = ((1,), (0,))
NT = ((1,), (1,))
TN = ((0,), (0,))
MESH = pl.DeviceIdType.MESH

norm_eps = 1e-05
clip_level = 100.0
beta_first = 0.9
beta_second = 0.95
adam_eps = 1e-08
decay_matrix = 0.1
rate_matrix = 0.05
rate_output = 0.5
rate_small = 0.5
masked_score = -1000000000.0
score_scale = HD ** (-0.5)
log_two = math.log(2.0)
query_scale = score_scale / log_two
vmem_limit = 58 * 2**20
AUX = HD
MASK_ROW = HD + 3
norm_rows = ((0, 0, 0), (2, 2, 2), (4, 6, 6), (8, 10, 10))


def mul(left, right, dims):
    return lax.dot_general(left, right, (dims, ((), ())), preferred_element_type=F32)


def dma(*shape):
    return pltpu.SemaphoreType.DMA(shape)


def vmem():
    return pl.BlockSpec(memory_space=pltpu.VMEM)


def shape_of(shape, kind):
    return jax.ShapeDtypeStruct(shape, kind)


def call(kernel, name, outs, args, scratch=(), collective=None, flops=0):
    extra = {} if collective is None else {"collective_id": collective, "has_side_effects": True}
    return pl.pallas_call(
        kernel,
        name=name,
        out_shape=outs,
        in_specs=[vmem()] * len(args),
        out_specs=tuple(vmem() for _ in outs),
        scratch_shapes=list(scratch),
        compiler_params=pltpu.CompilerParams(vmem_limit_bytes=vmem_limit, **extra),
        cost_estimate=pl.CostEstimate(flops=flops, bytes_accessed=4_000_000, transcendentals=0),
    )(*args)


def places():
    me = lax.axis_index("mp")
    mate = me + 1 - 2 * lax.rem(me, 2)
    across = lax.rem(me + 2, 4)
    far = lax.rem(mate + 2, 4)
    return me, mate, across, far


def greet(others):
    barrier = pltpu.get_barrier_semaphore()
    for other in others:
        pl.semaphore_signal(barrier, inc=1, device_id={"mp": other}, device_id_type=MESH)
    pl.semaphore_wait(barrier, len(others))


def push(source, target, send, recv, device):
    copy = pltpu.make_async_remote_copy(
        source, target, send, recv, device_id={"mp": device}, device_id_type=MESH
    )
    copy.start()
    return copy


def gather_start(refs, sems):
    me, mate, across, far = places()
    first = [push(ref.at[me], ref.at[me], sems.at[0, n], sems.at[1, n], across) for n, ref in enumerate(refs)]
    second = [push(ref.at[me], ref.at[me], sems.at[2, n], sems.at[3, n], mate) for n, ref in enumerate(refs)]
    return first, second


def gather_finish(refs, sems, started):
    me, mate, across, far = places()
    first, second = started
    third = []
    for n, ref in enumerate(refs):
        first[n].wait_recv()
        third.append(push(ref.at[across], ref.at[across], sems.at[4, n], sems.at[5, n], mate))
    for copy in first:
        copy.wait_send()
    for copy in second + third:
        copy.wait()


def exchange(source, target, sems):
    me, mate, across, far = places()
    copies = [
        push(source.at[other], target.at[me], sems.at[0, n], sems.at[1, n], other)
        for n, other in enumerate((across, far, mate))
    ]
    target[me] = source[me]
    for copy in copies:
        copy.wait()


def reduce_scatter(source, held, sems):
    me, mate, across, far = places()
    near_far = push(source.at[far], held.at[0], sems.at[0, 0], sems.at[1, 0], mate)
    near = push(source.at[mate], held.at[1], sems.at[0, 1], sems.at[1, 1], mate)
    near_far.wait()
    held[2] = (source[across].astype(F32) + held[0].astype(F32)).astype(BF)
    cross = push(held.at[2], held.at[3], sems.at[0, 2], sems.at[1, 2], across)
    near.wait()
    total = source[me].astype(F32) + held[1].astype(F32)
    cross.wait()
    return total + held[3].astype(F32)


def norm_parts(stream):
    center = stream - jnp.mean(stream, axis=0, keepdims=True)
    scale_inv = lax.rsqrt(jnp.mean(center * center, axis=0, keepdims=True) + norm_eps)
    return center * scale_inv, scale_inv


def norm_back(unit, scale_inv, scaled):
    return scale_inv * (
        scaled
        - jnp.mean(scaled, axis=0, keepdims=True)
        - unit * jnp.mean(scaled * unit, axis=0, keepdims=True)
    )


def enter_kernel(time_ref, spec_ref, time_x, spec_x, time_all, spec_all, sems):
    me, mate, across, far = places()
    greet((mate, across))
    for source, stream, whole in ((time_ref, time_x, time_all), (spec_ref, spec_x, spec_all)):
        columns = source[...].astype(F32).T
        stream[...] = columns
        whole[me] = norm_parts(columns)[0].astype(BF)
    refs = (time_all, spec_all)
    gather_finish(refs, sems, gather_start(refs, sems))


def add_branch(mixed, w_out, scale, stream):
    return stream + scale * mul(w_out, mixed, TN)


def middle_kernel(
    rows, mixed_ref, out_t, out_f, cols, time_x, spec_x,
    mixed_all, time_y, spec_y, time_all, spec_all, sems, sems_two,
):
    me, mate, across, far = places()
    greet((mate, across, far))
    exchange(mixed_ref, mixed_all, sems_two)
    mixed = mixed_all[...].reshape(-1, mixed_all.shape[2])
    value = jnp.concatenate(
        [
            add_branch(mixed[:, :LANES], out_t[...], cols[:, rows[0] : rows[0] + 1], time_x[...]),
            add_branch(mixed[:, LANES:], out_f[...], cols[:, rows[1] : rows[1] + 1], spec_x[...]),
        ],
        axis=1,
    )
    time_y[...] = value[:, :LANES]
    spec_y[...] = value[:, LANES:]
    unit = norm_parts(value)[0].astype(BF)
    time_all[me] = unit[:, :LANES]
    spec_all[me] = unit[:, LANES:]
    refs = (time_all, spec_all)
    gather_finish(refs, sems, gather_start(refs, sems))


def gelu_pair(values):
    share = 0.5 * (1.0 + lax.erf(values * (2.0**-0.5)))
    slope = share + values * (jnp.exp(-0.5 * values * values) * ((2.0 * math.pi) ** -0.5))
    return values * share, slope


def turn_kernel(
    mixed_ref, out_t, out_f, w_first, w_second, cols, time_x, spec_x, time_dy, spec_dy,
    time_out, spec_out, time_d, spec_d, grads, smalls, grad_mixed, mixed_all, outgoing, sems, sems_two,
):
    me, mate, across, far = places()
    greet((mate, across, far))
    exchange(mixed_ref, mixed_all, sems)
    mixed = mixed_all[...].reshape(-1, mixed_all.shape[2])
    gain, shift, scale = cols[:, 12:13], cols[:, 13:14], cols[:, 18:19]
    first, second = w_first[...], w_second[...]
    group = mixed_all.shape[0]
    hidden_part = first.shape[1] // group
    stream = jnp.concatenate(
        [
            add_branch(mixed[:, :LANES], out_t[...], cols[:, 16:17], time_x[...]),
            add_branch(mixed[:, LANES:], out_f[...], cols[:, 17:18], spec_x[...]),
        ],
        axis=1,
    )
    upstream = jnp.concatenate([time_dy[...].astype(F32).T, spec_dy[...].astype(F32).T], axis=1)
    unit, scale_inv = norm_parts(stream)
    normed = (unit * gain + shift).astype(BF)
    hidden = mul(first, normed, TN)
    active, slope = gelu_pair(hidden)
    active = active.astype(BF)
    branch = mul(second, active, TN)
    result = stream + scale * branch
    time_out[...] = result[:, :LANES].T
    spec_out[...] = result[:, LANES:].T
    grad_branch = (scale * upstream).astype(BF)
    grad_hidden = (mul(second, grad_branch, NN) * slope).astype(BF)
    grad_normed = mul(first, grad_hidden, NN)
    smalls[:, 0:1] = jnp.sum(grad_normed * unit, axis=1, keepdims=True)
    smalls[:, 1:2] = jnp.sum(grad_normed, axis=1, keepdims=True)
    smalls[:, 2:3] = jnp.sum(upstream * branch, axis=1, keepdims=True)
    grad_first = mul(normed, grad_hidden, NT).astype(BF)
    grad_second = mul(active, grad_branch, NT).astype(BF)
    for n in range(group):
        part = slice(n * hidden_part, (n + 1) * hidden_part)
        grads[n, :hidden_part] = grad_first[:, part]
        grads[n, hidden_part : 2 * hidden_part] = grad_second[part]
    grad_stream = upstream + norm_back(unit, scale_inv, grad_normed * gain)
    time_d[...] = grad_stream[:, :LANES]
    spec_d[...] = grad_stream[:, LANES:]
    branches_back(
        grad_stream, mixed, (out_t[...], out_f[...]), (cols[:, 16:17], cols[:, 17:18]),
        grads, 2 * hidden_part, outgoing,
    )
    exchange(outgoing, grad_mixed, sems_two)


def branches_back(grad_stream, mixed, outs, scales, grads, start, outgoing):
    group = outgoing.shape[0]
    width = mixed.shape[0] // group
    for n, lanes in enumerate((slice(0, LANES), slice(LANES, None))):
        upstream = grad_stream[:, lanes]
        grad_out = mul(mixed[:, lanes], upstream.astype(BF), NT).astype(BF)
        grad_mix = mul(outs[n], (scales[n] * upstream).astype(BF), NN).astype(BF)
        for g in range(group):
            part = slice(g * width, (g + 1) * width)
            grads[g, start + n * width : start + (n + 1) * width] = grad_out[part]
            outgoing[g, :, lanes] = grad_mix[part]


def back_middle_kernel(
    rows, terms, mixed_all, out_t, out_f, cols, time_x, spec_x, time_d, spec_d,
    time_e, spec_e, grads, grad_mixed, outgoing, held, sems, sems_two,
):
    me, mate, across, far = places()
    greet((mate, across, far))
    total = reduce_scatter(terms, held, sems)
    mixed = mixed_all[...].reshape(-1, mixed_all.shape[2])
    stream = jnp.concatenate([time_x[...], spec_x[...]], axis=1)
    unit, scale_inv = norm_parts(stream)
    grad_stream = jnp.concatenate([time_d[...], spec_d[...]], axis=1) + norm_back(unit, scale_inv, total)
    time_e[...] = grad_stream[:, :LANES]
    spec_e[...] = grad_stream[:, LANES:]
    scales = tuple(cols[:, row : row + 1] for row in rows)
    branches_back(grad_stream, mixed, (out_t[...], out_f[...]), scales, grads, 0, outgoing)
    exchange(outgoing, grad_mixed, sems_two)


def leave_kernel(terms, time_x, spec_x, time_d, spec_d, time_grad, spec_grad, held, sems):
    me, mate, across, far = places()
    greet((mate, across))
    total = reduce_scatter(terms, held, sems)
    stream = jnp.concatenate([time_x[...], spec_x[...]], axis=1)
    unit, scale_inv = norm_parts(stream)
    grad_stream = jnp.concatenate([time_d[...], spec_d[...]], axis=1) + norm_back(unit, scale_inv, total)
    time_grad[...] = grad_stream[:, :LANES].T
    spec_grad[...] = grad_stream[:, LANES:].T


def attend_blocks(block, keys, queries, values, score, write):
    count = queries.shape[1] // block
    rows_k = keys.shape[0]
    row = lax.broadcasted_iota(jnp.int32, (LANES, block), 0)

    def make(n, head):
        lanes = pl.ds(pl.multiple_of(n * block, LANES), block)
        query = queries[:, lanes]
        own = (row < HP) if head == 0 else (row >= HP)
        score[head, :rows_k, :] = mul(keys[...], jnp.where(own, query, jnp.zeros_like(query)), NN)

    def finish(n, head):
        held = score[head, :rows_k, :]
        peak = jnp.max(held, axis=0, keepdims=True)
        shares = jnp.exp2(held - peak).astype(BF)
        mixed = mul(values[head * HP : (head + 1) * HP, :], shares, NN)
        total = mixed[AUX : AUX + 1, :]
        write(n, head, (mixed[:HD] * (1.0 / total)).astype(BF), peak + jnp.log2(total))

    make(0, 0)

    def step(n, carry):
        make(n, 1)
        finish(n, 0)
        make(jnp.minimum(n + 1, count - 1), 0)
        finish(n, 1)
        return carry

    lax.fori_loop(0, count, step, 0)


def attend_kernel(
    cross, live, time_all, spec_all, w_t, w_f, b_t, b_f, bias,
    mixed, qt, kt, vt, qf, kf, vf, kt_rows, vt_rows, kf_rows, vf_rows, total_t, total_f, score,
):
    group, _, block_f = spec_all.shape
    block_t = time_all.shape[2]
    row_t = lax.broadcasted_iota(jnp.int32, (LANES, block_t), 0)
    lane_t = lax.broadcasted_iota(jnp.int32, (LANES, block_t), 1)
    row_f = lax.broadcasted_iota(jnp.int32, (LANES, block_f), 0)
    dead_t = jnp.where(lane_t < live, 0.0, masked_score)
    mask_t = (row_t == MASK_ROW) | (row_t == MASK_ROW + HP)
    mask_f = (row_f == MASK_ROW) | (row_f == MASK_ROW + HP)
    kept = kt_rows.shape[0] // group
    for n in range(group):
        lanes = slice(n * block_f, (n + 1) * block_f)
        made = mul(w_f[...], spec_all[n], NN) + b_f[...]
        qf[:, lanes] = made[:LANES].astype(BF)
        key = (made[LANES : 2 * LANES] + jnp.where(mask_f, bias[:, lanes], 0.0)).astype(BF)
        value = made[2 * LANES :].astype(BF)
        kf[:, lanes], vf[:, lanes] = key, value
        kf_rows[lanes, :], vf_rows[lanes, :] = key.T, value.T
        lanes = slice(n * block_t, (n + 1) * block_t)
        made = mul(w_t[...], time_all[n], NN) + b_t[...]
        qt[:, lanes] = made[:LANES].astype(BF)
        key = (made[LANES : 2 * LANES] + jnp.where(mask_t, dead_t, 0.0)).astype(BF)
        value = made[2 * LANES :].astype(BF)
        lanes = slice(n * kept, (n + 1) * kept)
        kt_rows[lanes, :], vt_rows[lanes, :] = key.T[:kept], value.T[:kept]
    kt[...] = kt_rows[...].T
    vt[...] = vt_rows[...].T

    def write_time(n, head, value, total):
        for g in range(group):
            mixed[g, head * HD : (head + 1) * HD, :block_t] = value[:, g * block_t : (g + 1) * block_t]
        total_t[head : head + 1, :] = total

    def write_spec(n, head, value, total):
        mixed[n, head * HD : (head + 1) * HD, block_t:] = value
        total_f[head : head + 1, pl.ds(pl.multiple_of(n * block_f, LANES), block_f)] = total

    keys, values = ((kf_rows, kt_rows), (vf, vt)) if cross else ((kt_rows, kf_rows), (vt, vf))
    attend_blocks(qt.shape[1], keys[0], qt, values[0], score, write_time)
    attend_blocks(block_f, keys[1], qf, values[1], score, write_spec)


def split_three(value):
    high = value.astype(BF)
    rest = value - high.astype(F32)
    middle = rest.astype(BF)
    return high, middle, (rest - middle.astype(F32)).astype(BF)


def with_rows(body, head, parts):
    row = lax.broadcasted_iota(jnp.int32, body.shape, 0) - head * HP
    out = jnp.where((row >= 0) & (row < HP), body.astype(F32), 0.0)
    for n, part in enumerate(parts):
        out = jnp.where(row == AUX + n, part.astype(F32), out)
    return out.astype(BF)


def back_blocks(block, keys_rows, keys, values_rows, queries, upstream, grad_q, grad_k, grad_v):
    count = queries.shape[2] // block
    rows_k = keys_rows.shape[0]
    grad_k[:, :rows_k] = jnp.zeros((LANES, rows_k), F32)
    grad_v[:, :rows_k] = jnp.zeros((LANES, rows_k), F32)

    def step(n, carry):
        lanes = pl.ds(pl.multiple_of(n * block, LANES), block)
        for head in range(2):
            own = slice(head * HP, (head + 1) * HP)
            shares = jnp.exp2(mul(keys_rows[...], queries[head, :, lanes], NN))
            inner = mul(values_rows[...], upstream[head, :, lanes], NN)
            grad_score = (shares * inner).astype(BF)
            shares = shares.astype(BF)
            grad_q[own, lanes] = (mul(keys[own, :], grad_score, NN) * score_scale).astype(BF)
            grad_k[own, :rows_k] += mul(queries[head, own, lanes], grad_score, NT)
            grad_v[own, :rows_k] += mul(upstream[head, own, lanes], shares, NT)
        return carry

    lax.fori_loop(0, count, step, 0)


def attend_back_kernel(
    cross, time_all, spec_all, wt_t, wt_f, grad_mixed, mixed,
    qt, kt, vt, qf, kf, vf, kt_rows, vt_rows, kf_rows, vf_rows, total_t, total_f,
    terms, grads, sums, ds_t, ds_f, query, upstream, grad_k, grad_v,
):
    group, _, block_f = spec_all.shape
    block_t = time_all.shape[2]
    kept = kt_rows.shape[0] // group

    def prepare(q, total, first, lanes_in, block):
        size = q.shape[1]
        for head in range(2):
            query[head, :, :size] = with_rows(q[...], head, split_three(-total[head : head + 1, :]))
            rows = slice(head * HD, (head + 1) * HD)
            for g in range(group):
                part = grad_mixed[g, rows, lanes_in]
                inner = jnp.sum(
                    part.astype(F32) * mixed[g, rows, lanes_in].astype(F32), axis=0, keepdims=True
                )
                padded = jnp.concatenate(
                    [part, *split_three(-inner), jnp.zeros((HP - HD - 3, block), BF)], axis=0
                )
                other = jnp.zeros((HP, block), BF)
                both = [padded, other] if head == 0 else [other, padded]
                upstream[head, :, g * block : (g + 1) * block] = jnp.concatenate(both, axis=0)

    def spread(dst, base, source):
        turned = source.T
        for g in range(group):
            part = turned[g * kept : (g + 1) * kept]
            part = jnp.concatenate([part, jnp.zeros((block_t - kept, LANES), F32)], axis=0)
            dst[base : base + LANES, g * block_t : (g + 1) * block_t] = part.T.astype(BF)

    def store_keys(time_keys):
        if time_keys:
            size = kt_rows.shape[0]
            spread(ds_t, LANES, grad_k[:, :size] * log_two)
            spread(ds_t, 2 * LANES, grad_v[:, :size])
        else:
            ds_f[LANES : 2 * LANES, :] = (grad_k[...] * log_two).astype(BF)
            ds_f[2 * LANES :, :] = grad_v[...].astype(BF)

    time_side, spec_side = (kt_rows, kt, vt_rows), (kf_rows, kf, vf_rows)
    if cross:
        time_side, spec_side = spec_side, time_side
    size_t = qt.shape[1]
    prepare(qt, total_t, 0, slice(0, block_t), block_t)
    back_blocks(
        size_t, *time_side, query.at[:, :, :size_t], upstream.at[:, :, :size_t], ds_t, grad_k, grad_v
    )
    store_keys(not cross)
    prepare(qf, total_f, 1, slice(block_t, None), block_f)
    back_blocks(block_f, *spec_side, query, upstream, ds_f, grad_k, grad_v)
    store_keys(cross)

    for n, (ds, whole, weight, block) in enumerate(
        ((ds_t, time_all, wt_t, block_t), (ds_f, spec_all, wt_f, block_f))
    ):
        lanes_out = slice(0, block_t) if n == 0 else slice(block_t, None)
        total = None
        for g in range(group):
            part = ds[:, g * block : (g + 1) * block]
            terms[g, :, lanes_out] = mul(weight[...], part, NN).astype(BF)
            product = mul(part, whole[g], NT)
            total = product if total is None else total + product
        sums[n] = jnp.broadcast_to(jnp.sum(ds[...].astype(F32), axis=1, keepdims=True), sums.shape[1:])
        for piece in range(6):
            grads[n, piece * HD : (piece + 1) * HD] = total[piece * HP : piece * HP + HD].astype(BF)


def adam_update(weight, first_moment, second_moment, gradient, step_rate, decay_rate):
    first_new = beta_first * first_moment + (1.0 - beta_first) * gradient
    second_new = beta_second * second_moment + (1.0 - beta_second) * gradient * gradient
    first_fix = 1.0 - beta_first**STEP
    second_fix = 1.0 - beta_second**STEP
    direction = first_new / first_fix / (jnp.sqrt(second_new / second_fix) + adam_eps)
    return (weight - step_rate * (direction + decay_rate * weight), first_new, second_new)


def pad_heads(value):
    shape = value.shape
    heads = shape[2] // HD
    value = value.reshape(shape[:2] + (heads, HD) + shape[3:])
    value = jnp.pad(value, ((0, 0),) * 3 + ((0, HP - HD),) + ((0, 0),) * (len(shape) - 3))
    return value.reshape(shape[:2] + (heads * HP,) + shape[3:])


def by_stream(value, cross):
    picks = (((2, 0), (3, 1), (3, 2)), ((3, 0), (2, 1), (2, 2))) if cross else (
        ((0, 0), (0, 1), (0, 2)), ((1, 0), (1, 1), (1, 2)))
    return [jnp.concatenate([value[i, n] for i, n in pick], axis=0) for pick in picks]


def shards(
    time_in, spec_in, rate_flags, band_limits, time_cot, spec_cot, attn_in, attn_out, ffn_in, ffn_out, small,
    attn_in_m, attn_in_v, attn_out_m, attn_out_v, ffn_in_m, ffn_in_v, ffn_out_m, ffn_out_v, small_m, small_v,
):
    group = lax.axis_size("mp")
    live = time_in.shape[1]
    kept = -(-live // 16) * 16
    block_t, block_f = LANES, spec_in.shape[1]
    width = time_in.shape[2]
    local = attn_in.shape[2]
    hidden_part = ffn_in.shape[1]
    lanes = block_t + block_f
    size_t, size_f, rows_t = group * block_t, group * block_f, group * kept

    def padded(value):
        return jnp.pad(value[0], ((0, block_t - live), (0, 0)))

    gains = jnp.stack([jnp.stack([small[r] for r in rows]) for rows in norm_rows])
    shifts = jnp.stack([jnp.stack([small[r + 1] for r in rows]) for rows in norm_rows])
    folded = attn_in * gains[:, :, None, :]
    offsets = jnp.sum(attn_in * shifts[:, :, None, :], axis=3)
    scaling = jnp.array([query_scale, 1.0, 1.0], F32)
    spare = jnp.zeros((3, HP), F32)
    spare = spare.at[0, MASK_ROW].set(1.0).at[1, AUX : AUX + 3].set(1.0).at[2, AUX : AUX + 3].set(1.0)
    spare = jnp.tile(spare, (1, 2))[None]
    forward = pad_heads((folded * scaling[:, None, None]).astype(BF))
    backward = pad_heads(folded.astype(BF))
    offsets = (pad_heads(offsets * scaling[:, None]) + spare)[..., None]
    w_out = lax.all_gather(attn_out.astype(BF), "mp", axis=1, tiled=True)
    w_first = lax.all_gather(ffn_in.astype(BF), "mp", axis=1, tiled=True)
    w_second = lax.all_gather(ffn_out.astype(BF), "mp", axis=0, tiled=True)
    cols = jnp.pad(small, ((0, 24 - small.shape[0]), (0, 0))).T
    bins = jnp.arange(size_f, dtype=jnp.int32) // FRAMES
    open_keys = (rate_flags[0] == 0) | (bins < band_limits[0])
    bias = jnp.where(open_keys, 0.0, masked_score).astype(F32)[None]

    whole = (shape_of((group, width, block_t), BF), shape_of((group, width, block_f), BF))
    stream = (shape_of((width, block_t), F32), shape_of((width, block_f), F32))
    mix = shape_of((group, local, lanes), BF)

    def attend(cross, time_all, spec_all, name):
        forward_t, forward_f = by_stream(forward, cross)
        offset_t, offset_f = by_stream(offsets, cross)
        outs = (mix,) + tuple(
            shape_of(s, BF)
            for s in (
                [(LANES, size_t)] + [(LANES, rows_t)] * 2 + [(LANES, size_f)] * 3 + [(rows_t, LANES)] * 2 + [(size_f, LANES)] * 2
            )
        ) + (shape_of((2, size_t), F32), shape_of((2, size_f), F32))
        return call(
            functools.partial(attend_kernel, cross, live), name, outs,
            (time_all, spec_all, forward_t, forward_f, offset_t, offset_f, bias),
            [pltpu.VMEM((2, size_f, max(size_t, block_f)), F32)],
        )

    def attend_back(cross, time_all, spec_all, grad_mixed, kept_values, name):
        back_t, back_f = (part.T for part in by_stream(backward, cross))
        outs = (
            shape_of((group, width, lanes), BF), shape_of((2, 3 * local, width), BF),
            shape_of((2, 3 * LANES, LANES), F32),
        )
        return call(
            functools.partial(attend_back_kernel, cross), name, outs,
            (time_all, spec_all, back_t, back_f, grad_mixed) + kept_values,
            [
                pltpu.VMEM((3 * LANES, size_t), BF), pltpu.VMEM((3 * LANES, size_f), BF),
                pltpu.VMEM((2, LANES, size_f), BF), pltpu.VMEM((2, LANES, size_f), BF),
                pltpu.VMEM((LANES, size_f), F32), pltpu.VMEM((LANES, size_f), F32),
            ],
        )

    time_zero, spec_zero, time_all, spec_all = call(
        enter_kernel, "enter", stream + whole, (padded(time_in), spec_in[0]), [dma(6, 2)], 0
    )
    kept_ab = attend(False, time_all, spec_all, "attend_self")
    mixed_ab, time_one, spec_one, time_all_one, spec_all_one = call(
        functools.partial(middle_kernel, (14, 15)), "middle", (mix,) + stream + whole,
        (kept_ab[0], w_out[0], w_out[1], cols, time_zero, spec_zero), [dma(6, 2), dma(2, 3)], 1,
    )
    kept_cd = attend(True, time_all_one, spec_all_one, "attend_cross")
    time_out, spec_out, time_d, spec_d, grads_turn, smalls, grad_mixed_cd, _ = call(
        turn_kernel, "turn",
        (
            shape_of((block_t, width), F32), shape_of((block_f, width), F32)) + stream + (
            shape_of((group, 2 * hidden_part + 2 * local, width), BF), shape_of((width, LANES), F32), mix, mix,
        ),
        (
            kept_cd[0], w_out[2], w_out[3], w_first, w_second, cols, time_one, spec_one,
            padded(time_cot), spec_cot[0],
        ),
        [pltpu.VMEM(mix.shape, BF), dma(2, 3), dma(2, 3)], 2,
    )

    terms_cd, grads_cd, sums_cd = attend_back(True, time_all_one, spec_all_one, grad_mixed_cd, kept_cd, "back_cross")
    time_e, spec_e, grads_out, grad_mixed_ab = call(
        functools.partial(back_middle_kernel, (14, 15)), "back_middle",
        stream + (shape_of((group, 2 * local, width), BF), mix),
        (terms_cd, mixed_ab, w_out[0], w_out[1], cols, time_one, spec_one, time_d, spec_d),
        [pltpu.VMEM(mix.shape, BF), pltpu.VMEM((4, width, lanes), BF), dma(2, 3), dma(2, 3)], 3,
    )
    terms_ab, grads_ab, sums_ab = attend_back(False, time_all, spec_all, grad_mixed_ab, kept_ab, "back_self")
    time_grad, spec_grad = call(
        leave_kernel, "leave", (shape_of((block_t, width), F32), shape_of((block_f, width), F32)),
        (terms_ab, time_zero, spec_zero, time_e, spec_e),
        [pltpu.VMEM((4, width, lanes), BF), dma(2, 3)], 4,
    )

    def both(value):
        part = lax.psum_scatter(value, "mp", scatter_dimension=0, tiled=True)[0]
        return lax.psum(part, "dp").astype(F32)

    turn_sum = both(grads_turn)
    out_sum = both(grads_out)
    cd_sum = lax.psum(grads_cd, "dp").astype(F32).reshape(2, 3, local, width)
    ab_sum = lax.psum(grads_ab, "dp").astype(F32).reshape(2, 3, local, width)
    row_sums = jnp.stack([sums_ab[:, :, 0], sums_cd[:, :, 0]]).reshape(2, 2, 3, 2, HP)[..., :HD]
    row_sums = lax.psum(row_sums.reshape(2, 2, 3, local), "dp")
    small_turn = lax.psum(smalls[:, :3], ("dp", "mp"))
    plain = jnp.stack([ab_sum[0], ab_sum[1], jnp.stack([cd_sum[0, 0], cd_sum[1, 1], cd_sum[1, 2]]),
                       jnp.stack([cd_sum[1, 0], cd_sum[0, 1], cd_sum[0, 2]])])
    rows = row_sums.reshape(4, 3, local)
    rows = jnp.stack([rows[0], rows[1], jnp.stack([rows[2, 0], rows[3, 1], rows[3, 2]]),
                      jnp.stack([rows[3, 0], rows[2, 1], rows[2, 2]])])
    grad_a = plain * gains[:, :, None, :] + rows[..., None] * shifts[:, :, None, :]
    gain_terms = jnp.sum(attn_in * plain, axis=2)
    shift_terms = jnp.sum(attn_in * rows[..., None], axis=2)
    out_plain = jnp.concatenate(
        [out_sum.reshape(2, local, width), turn_sum[2 * hidden_part :].reshape(2, local, width)]
    )
    grad_b = out_plain * small[14:18][:, None, :]
    scale_terms = jnp.sum(attn_out * out_plain, axis=1)
    grad_c, grad_d = turn_sum[:hidden_part], turn_sum[hidden_part : 2 * hidden_part]
    summed = (grad_a, grad_b, grad_c, grad_d)
    pairs = []
    for index, picks in enumerate((((0, 0), (0, 1), (0, 2)), ((1, 0), (1, 1), (1, 2)), ((2, 0),), ((2, 1), (2, 2)), ((3, 0),), ((3, 1), (3, 2)))):
        pairs.append(sum(gain_terms[i, n] for i, n in picks))
        pairs.append(sum(shift_terms[i, n] for i, n in picks))
    local_squares = sum(jnp.sum(g * g) for g in summed)
    packed = jnp.concatenate(
        [jnp.stack(pairs), scale_terms, jnp.broadcast_to(local_squares, (1, width))]
    )
    packed = lax.psum(packed, "mp")
    grad_small = jnp.concatenate([packed[:12], small_turn[:, :2].T, packed[12:16], small_turn[:, 2:3].T])
    squares = packed[16, 0] + jnp.sum(grad_small * grad_small)
    grad_norm = jnp.sqrt(squares)
    factor = jnp.minimum(1.0, clip_level / grad_norm)
    weights = (attn_in, attn_out, ffn_in, ffn_out)
    moments = (
        (attn_in_m, attn_in_v), (attn_out_m, attn_out_v), (ffn_in_m, ffn_in_v), (ffn_out_m, ffn_out_v),
    )
    rates = (rate_matrix, rate_output, rate_matrix, rate_matrix)
    updated = []
    for index in range(4):
        updated.extend(
            adam_update(
                weights[index], *moments[index], summed[index] * factor, rates[index], decay_matrix
            )
        )
    small_clipped = grad_small * factor
    updated.extend(adam_update(small, small_m, small_v, small_clipped, rate_small, 0.0))
    return (
        time_out[None, :live], spec_out[None], time_grad[None, :live], spec_grad[None], grad_norm,
        *updated, small_clipped[13],
    )


def solution(mesh):
    tokens, copied = P("dp", "mp", None), P()
    a, b, c, d = P(None, None, "mp", None), P(None, "mp", None), P(None, "mp"), P("mp", None)
    return jax.shard_map(
        shards,
        mesh=mesh,
        in_specs=(
            tokens, tokens, P("dp"), P("dp"), tokens, tokens, a, b, c, d, copied,
            a, a, b, b, c, c, d, d, copied, copied,
        ),
        out_specs=(
            tokens, tokens, tokens, tokens, copied,
            a, a, a, b, b, b, c, c, c, d, d, d, copied, copied, copied, copied,
        ),
        check_vma=False,
    )
```

```python
import functools
import math

import jax
import jax.numpy as jnp
from jax import lax
from jax.experimental import pallas as pl
from jax.experimental.pallas import tpu as pltpu
from jax.sharding import PartitionSpec as P

HD = 48
HP = 64
LANES = 128
FRAMES = 256
STEP = 10
BF = jnp.bfloat16
F32 = jnp.float32
NN = ((1,), (0,))
NT = ((1,), (1,))
TN = ((0,), (0,))
MESH = pl.DeviceIdType.MESH

norm_eps = 1e-05
clip_level = 100.0
beta_first = 0.9
beta_second = 0.95
adam_eps = 1e-08
decay_matrix = 0.1
rate_matrix = 0.05
rate_output = 0.5
rate_small = 0.5
masked_score = -1000000000.0
score_scale = HD ** (-0.5)
log_two = math.log(2.0)
query_scale = score_scale / log_two
vmem_limit = 58 * 2**20
AUX = HD
MASK_ROW = HD + 3
norm_rows = ((0, 0, 0), (2, 2, 2), (4, 6, 6), (8, 10, 10))


def mul(left, right, dims):
    return lax.dot_general(left, right, (dims, ((), ())), preferred_element_type=F32)


def dma(*shape):
    return pltpu.SemaphoreType.DMA(shape)


def vmem():
    return pl.BlockSpec(memory_space=pltpu.VMEM)


def shape_of(shape, kind):
    return jax.ShapeDtypeStruct(shape, kind)


def call(kernel, name, outs, args, scratch, collective, specs=None):
    return pl.pallas_call(
        kernel,
        name=name,
        out_shape=outs,
        in_specs=[(specs or {}).get(n, vmem()) for n in range(len(args))],
        out_specs=tuple(vmem() for _ in outs),
        scratch_shapes=list(scratch),
        compiler_params=pltpu.CompilerParams(
            vmem_limit_bytes=vmem_limit, collective_id=collective, has_side_effects=True
        ),
    )(*args)


def places():
    me = lax.axis_index("mp")
    mate = me + 1 - 2 * lax.rem(me, 2)
    across = lax.rem(me + 2, 4)
    far = lax.rem(mate + 2, 4)
    return me, mate, across, far


def greet(others, partners=()):
    barrier = pltpu.get_barrier_semaphore()
    for other in others:
        pl.semaphore_signal(barrier, inc=1, device_id={"mp": other}, device_id_type=MESH)
    for partner in partners:
        pl.semaphore_signal(barrier, inc=1, device_id={"dp": partner}, device_id_type=MESH)
    pl.semaphore_wait(barrier, len(others) + len(partners))


def push_to(source, target, send, recv, device):
    copy = pltpu.make_async_remote_copy(
        source, target, send, recv, device_id=device, device_id_type=MESH
    )
    copy.start()
    return copy


def push(source, target, send, recv, device):
    return push_to(source, target, send, recv, {"mp": device})


def gather_start(refs, sems):
    me, mate, across, far = places()
    first = [push(ref.at[me], ref.at[me], sems.at[0, n], sems.at[1, n], across) for n, ref in enumerate(refs)]
    second = [push(ref.at[me], ref.at[me], sems.at[2, n], sems.at[3, n], mate) for n, ref in enumerate(refs)]
    return first, second


def gather_finish(refs, sems, started):
    me, mate, across, far = places()
    first, second = started
    third = []
    for n, ref in enumerate(refs):
        first[n].wait_recv()
        third.append(push(ref.at[across], ref.at[across], sems.at[4, n], sems.at[5, n], mate))
    for copy in first:
        copy.wait_send()
    for copy in second + third:
        copy.wait()


def exchange(sources, targets, sems):
    me, mate, across, far = places()
    copies = []
    for source, target, sem in zip(sources, targets, sems):
        for n, other in enumerate((across, far, mate)):
            copies.append(push(source.at[other], target.at[me], sem.at[0, n], sem.at[1, n], other))
    for source, target in zip(sources, targets):
        target[me] = source[me]
    for copy in copies:
        copy.wait()


class Scatter:
    def __init__(self, source, held, sems):
        self.source, self.held, self.sems = source, held, sems
        self.stage = 0

    def start(self):
        me, mate, across, far = places()
        send, recv = self.sems.at[0], self.sems.at[1]
        self.one = push(self.source.at[far], self.held.at[0], send.at[0], recv.at[0], mate)
        self.two = push(self.source.at[mate], self.held.at[1], send.at[1], recv.at[1], mate)

    def middle(self):
        if self.stage:
            return
        self.stage = 1
        me, mate, across, far = places()
        self.one.wait()
        self.held[2] = (self.source[across].astype(F32) + self.held[0].astype(F32)).astype(BF)
        self.cross = push(self.held.at[2], self.held.at[3], self.sems.at[0, 2], self.sems.at[1, 2], across)

    def finish(self):
        me, mate, across, far = places()
        self.two.wait()
        total = self.source[me].astype(F32) + self.held[1].astype(F32)
        self.cross.wait()
        return total + self.held[3].astype(F32)


def norm_parts(stream):
    center = stream - jnp.mean(stream, axis=0, keepdims=True)
    scale_inv = lax.rsqrt(jnp.mean(center * center, axis=0, keepdims=True) + norm_eps)
    return center * scale_inv, scale_inv


def norm_back(unit, scale_inv, scaled):
    return scale_inv * (
        scaled
        - jnp.mean(scaled, axis=0, keepdims=True)
        - unit * jnp.mean(scaled * unit, axis=0, keepdims=True)
    )


def attend_blocks(block, keys, queries, values, score, write):
    count = queries.shape[1] // block
    rows_k = keys.shape[0]
    row = lax.broadcasted_iota(jnp.int32, (LANES, block), 0)

    def make(n, head):
        lanes = pl.ds(pl.multiple_of(n * block, LANES), block)
        query = queries[:, lanes]
        own = (row < HP) if head == 0 else (row >= HP)
        score[head, :rows_k, :] = mul(keys[...], jnp.where(own, query, jnp.zeros_like(query)), NN)

    def finish(n, head):
        held = score[head, :rows_k, :]
        peak = jnp.max(held, axis=0, keepdims=True)
        shares = jnp.exp2(held - peak).astype(BF)
        mixed = mul(values[head * HP : (head + 1) * HP, :], shares, NN)
        total = mixed[AUX : AUX + 1, :]
        write(n, head, (mixed[:HD] * (1.0 / total)).astype(BF), peak + jnp.log2(total))

    make(0, 0)

    def step(n, carry):
        make(n, 1)
        finish(n, 0)
        make(jnp.minimum(n + 1, count - 1), 0)
        finish(n, 1)
        return carry

    lax.fori_loop(0, count, step, 0)


def split_three(value):
    high = value.astype(BF)
    rest = value - high.astype(F32)
    middle = rest.astype(BF)
    return high, middle, (rest - middle.astype(F32)).astype(BF)


def with_rows(body, head, parts):
    row = lax.broadcasted_iota(jnp.int32, body.shape, 0) - head * HP
    out = jnp.where((row >= 0) & (row < HP), body.astype(F32), 0.0)
    for n, part in enumerate(parts):
        out = jnp.where(row == AUX + n, part.astype(F32), out)
    return out.astype(BF)


def back_blocks(block, keys_rows, keys, values_rows, queries, upstream, grad_q, grad_k, grad_v, between):
    count = queries.shape[2] // block
    rows_k = keys_rows.shape[0]
    grad_k[:, :rows_k] = jnp.zeros((LANES, rows_k), F32)
    grad_v[:, :rows_k] = jnp.zeros((LANES, rows_k), F32)

    def step(n, carry):
        lanes = pl.ds(pl.multiple_of(n * block, LANES), block)
        for head in range(2):
            own = slice(head * HP, (head + 1) * HP)
            shares = jnp.exp2(mul(keys_rows[...], queries[head, :, lanes], NN))
            inner = mul(values_rows[...], upstream[head, :, lanes], NN)
            grad_score = (shares * inner).astype(BF)
            shares = shares.astype(BF)
            grad_q[own, lanes] = (mul(keys[own, :], grad_score, NN) * score_scale).astype(BF)
            grad_k[own, :rows_k] += mul(queries[head, own, lanes], grad_score, NT)
            grad_v[own, :rows_k] += mul(upstream[head, own, lanes], shares, NT)
        return carry

    if between is None:
        lax.fori_loop(0, count, step, 0)
    else:
        for n in range(count):
            lax.fori_loop(n, n + 1, step, 0)
            between()


class Sum:
    def __init__(self, buffer, stage, whole, sems, parts):
        self.buffer, self.stage, self.whole, self.sems = buffer, stage, whole, sems
        self.index = lax.axis_index("dp")
        self.state = []
        held = 0
        for first, rows, bits in parts:
            places = []
            for bit in bits:
                rows_now = rows >> (len(places) + 1)
                places.append(held)
                held += rows_now
            self.state.append([first, rows, bits, places])
        self.steps = 2 * len(parts[0][2])
        self.at = 0
        self.copies = []

    def bit(self, value):
        mine = lax.rem(self.index // value, 2)
        return mine, self.index + value * (1 - 2 * mine)

    def rows(self, ref, first, count):
        return ref.at[pl.ds(pl.multiple_of(first, 16), count)]

    def start(self):
        half = self.steps // 2
        self.copies = []
        for n, (first, rows, bits, places) in enumerate(self.state):
            send, recv = self.sems.at[0, n, self.at], self.sems.at[1, n, self.at]
            if self.at < half:
                mine, partner = self.bit(bits[self.at])
                count = rows // 2
                source = self.rows(self.buffer, first + (1 - mine) * count, count)
                target = self.stage.at[pl.ds(places[self.at], count)]
            else:
                mine, partner = self.bit(bits[self.steps - 1 - self.at])
                source = target = self.rows(self.whole, first, rows)
            self.copies.append(push_to(source, target, send, recv, {"dp": partner}))

    def finish(self):
        half = self.steps // 2
        for n, copy in enumerate(self.copies):
            copy.wait()
            first, rows, bits, places = self.state[n]
            if self.at < half:
                mine, partner = self.bit(bits[self.at])
                count = rows // 2
                first = first + mine * count
                here = pl.ds(pl.multiple_of(first, 16), count)
                there = pl.ds(places[self.at], count)
                target = self.buffer if self.at < half - 1 else self.whole
                target[here, :] = (
                    self.buffer[here, :].astype(F32) + self.stage[there, :].astype(F32)
                ).astype(BF)
                self.state[n][:2] = [first, count]
            else:
                mine, partner = self.bit(bits[self.steps - 1 - self.at])
                self.state[n][:2] = [first - mine * rows, 2 * rows]
        self.at += 1

    def advance(self):
        if self.copies:
            self.finish()
            self.copies = []
        if self.at < self.steps:
            self.start()

    def complete(self):
        while self.at < self.steps:
            self.advance()


def bit_orders(size):
    bits = [1 << n for n in range(size.bit_length() - 1)]
    return bits, bits[1:2] + bits[:1] + bits[2:]


def sum_rows(count, size):
    tile = 32 * size
    return -(-count // tile) * tile


def sum_parts(rows, size):
    one, two = bit_orders(size)
    return ((0, rows // 2, one), (rows // 2, rows // 2, two))


def picks_of(cross):
    if cross:
        return ((2, 0), (3, 1), (3, 2)), ((3, 0), (2, 1), (2, 2))
    return ((0, 0), (0, 1), (0, 2)), ((1, 0), (1, 1), (1, 2))


def fold_weights(cross, attn_in, small, forward, offsets, backward):
    width = attn_in.shape[3]
    for stream, picks in enumerate(picks_of(cross)):
        blocks = []
        for block, (index, group) in enumerate(picks):
            row = norm_rows[index][group]
            weight = attn_in[index, group]
            folded = weight * small[row : row + 1, :]
            offset = jnp.sum(weight * small[row + 1 : row + 2, :], axis=1, keepdims=True)
            factor = query_scale if group == 0 else 1.0
            ones = (MASK_ROW,) if group == 0 else (AUX, AUX + 1, AUX + 2)
            spare = lax.broadcasted_iota(jnp.int32, (HP - HD, 1), 0) + HD
            marks = jnp.zeros((HP - HD, 1), F32)
            for one in ones:
                marks = jnp.where(spare == one, 1.0, marks)
            for head in range(2):
                rows = slice(head * HD, (head + 1) * HD)
                start = block * LANES + head * HP
                forward[stream, start : start + HD, :] = (folded[rows] * factor).astype(BF)
                forward[stream, start + HD : start + HP, :] = jnp.zeros((HP - HD, width), BF)
                offsets[stream, start : start + HD, :] = offset[rows] * factor
                offsets[stream, start + HD : start + HP, :] = marks
                blocks += [folded[rows], jnp.zeros((HP - HD, width), F32)]
        backward[stream] = jnp.concatenate(blocks, axis=0).T.astype(BF)


def project(cross, live, time_all, spec_all, forward, offsets, bias, kept):
    qt, kt, vt, qf, kf, vf, kt_rows, vt_rows, kf_rows, vf_rows = kept
    group, _, block_f = spec_all.shape
    block_t = time_all.shape[2]
    row_t = lax.broadcasted_iota(jnp.int32, (LANES, block_t), 0)
    lane_t = lax.broadcasted_iota(jnp.int32, (LANES, block_t), 1)
    row_f = lax.broadcasted_iota(jnp.int32, (LANES, block_f), 0)
    dead_t = jnp.where(lane_t < live, 0.0, masked_score)
    mask_t = (row_t == MASK_ROW) | (row_t == MASK_ROW + HP)
    mask_f = (row_f == MASK_ROW) | (row_f == MASK_ROW + HP)
    count = kt_rows.shape[0] // group
    for n in range(group):
        lanes = slice(n * block_f, (n + 1) * block_f)
        made = mul(forward[1], spec_all[n], NN) + offsets[1]
        qf[:, lanes] = made[:LANES].astype(BF)
        key = (made[LANES : 2 * LANES] + jnp.where(mask_f, bias[:, lanes], 0.0)).astype(BF)
        value = made[2 * LANES :].astype(BF)
        kf[:, lanes], vf[:, lanes] = key, value
        kf_rows[lanes, :], vf_rows[lanes, :] = key.T, value.T
        lanes = slice(n * block_t, (n + 1) * block_t)
        made = mul(forward[0], time_all[n], NN) + offsets[0]
        qt[:, lanes] = made[:LANES].astype(BF)
        key = (made[LANES : 2 * LANES] + jnp.where(mask_t, dead_t, 0.0)).astype(BF)
        value = made[2 * LANES :].astype(BF)
        lanes = slice(n * count, (n + 1) * count)
        kt_rows[lanes, :], vt_rows[lanes, :] = key.T[:count], value.T[:count]
    kt[...] = kt_rows[...].T
    vt[...] = vt_rows[...].T


def attend(cross, kept, totals, mixed, score):
    qt, kt, vt, qf, kf, vf, kt_rows, vt_rows, kf_rows, vf_rows = kept
    mix_t, mix_f = mixed
    total_t, total_f = totals
    group, _, block_t = mix_t.shape
    block_f = mix_f.shape[2]

    def write_time(n, head, value, total):
        for g in range(group):
            mix_t[g, head * HD : (head + 1) * HD, :] = value[:, g * block_t : (g + 1) * block_t]
        total_t[head : head + 1, :] = total

    def write_spec(n, head, value, total):
        mix_f[n, head * HD : (head + 1) * HD, :] = value
        total_f[head : head + 1, pl.ds(pl.multiple_of(n * block_f, LANES), block_f)] = total

    keys, values = ((kf_rows, kt_rows), (vf, vt)) if cross else ((kt_rows, kf_rows), (vt, vf))
    attend_blocks(qt.shape[1], keys[0], qt, values[0], score, write_time)
    attend_blocks(block_f, keys[1], qf, values[1], score, write_spec)


def first_kernel(
    live, time_in, spec_in, flags, limits, attn_in, attn_out, ffn_in, small,
    time_x, spec_x, time_all, spec_all, mix_t, mix_f, all_t, all_f, *rest,
):
    kept, totals = rest[:10], rest[10:12]
    forward_two, offsets_two, backward, w_out, w_first, bias, cols = rest[12:19]
    forward, offsets, rows_t, score, sems, sems_w, sems_t, sems_f = rest[19:]
    me, mate, across, far = places()
    greet((mate, across, far))
    rows_t[...] = jnp.zeros_like(rows_t)
    rows_t[:live, :] = time_in[0].astype(F32)
    for source, stream, whole in ((rows_t[...], time_x, time_all), (spec_in[0].astype(F32), spec_x, spec_all)):
        columns = source.T
        stream[...] = columns
        whole[me] = norm_parts(columns)[0].astype(BF)
    refs = (time_all, spec_all)
    started = gather_start(refs, sems)
    w_out[me] = attn_out[...].astype(BF)
    w_first[me] = ffn_in[...].astype(BF)
    fold_weights(False, attn_in, small, forward, offsets, backward.at[0])
    fold_weights(True, attn_in, small, forward_two, offsets_two, backward.at[1])
    cols[...] = jnp.concatenate(
        [small[...], jnp.zeros((LANES - small.shape[0], small.shape[1]), F32)], axis=0
    ).T
    bins = lax.broadcasted_iota(jnp.int32, bias.shape, 1) // FRAMES
    bias[...] = jnp.where((bins < limits[0]) | (flags[0] == 0), 0.0, masked_score)
    gather_finish(refs, sems, started)
    weights = (w_out, w_first)
    started = gather_start(weights, sems_w)
    project(False, live, time_all, spec_all, forward, offsets, bias, kept)
    attend(False, kept, totals, (mix_t, mix_f), score)
    exchange((mix_t, mix_f), (all_t, all_f), (sems_t, sems_f))
    gather_finish(weights, sems_w, started)


def whole_weight(w_out, index):
    part = w_out[:, index]
    return part.reshape(-1, part.shape[2])


def joined(mixed):
    part = mixed[...]
    return part.reshape(-1, part.shape[2])


def add_branch(mixed, w_out, scale, stream):
    return stream + scale * mul(w_out, mixed, TN)


def second_kernel(
    live, time_x, spec_x, in_t, in_f, w_out, cols, forward, offsets, bias, ffn_out,
    time_y, spec_y, time_all, spec_all, mix_t, mix_f, all_t, all_f, *rest,
):
    kept, totals, w_second = rest[:10], rest[10:12], rest[12]
    score, sems, sems_w, sems_t, sems_f = rest[13:]
    me, mate, across, far = places()
    greet((mate, across, far))
    time_y[...] = add_branch(joined(in_t), whole_weight(w_out, 0), cols[:, 14:15], time_x[...])
    time_all[me] = norm_parts(time_y[...])[0].astype(BF)
    spec_y[...] = add_branch(joined(in_f), whole_weight(w_out, 1), cols[:, 15:16], spec_x[...])
    spec_all[me] = norm_parts(spec_y[...])[0].astype(BF)
    refs = (time_all, spec_all)
    started = gather_start(refs, sems)
    w_second[me] = ffn_out[...].astype(BF)
    gather_finish(refs, sems, started)
    started = gather_start((w_second,), sems_w)
    project(True, live, time_all, spec_all, forward, offsets, bias, kept)
    attend(True, kept, totals, (mix_t, mix_f), score)
    exchange((mix_t, mix_f), (all_t, all_f), (sems_t, sems_f))
    gather_finish((w_second,), sems_w, started)


def gelu_pair(values):
    share = 0.5 * (1.0 + lax.erf(values * (2.0**-0.5)))
    slope = share + values * (jnp.exp(-0.5 * values * values) * ((2.0 * math.pi) ** -0.5))
    return values * share, slope


def branches_back(grad_stream, mixed, weights, scales, grads, start, outgoing):
    for n, lanes in enumerate((slice(0, LANES), slice(LANES, None))):
        upstream = grad_stream[:, lanes]
        grad_out = mul(joined(mixed[n]), upstream.astype(BF), NT).astype(BF)
        grad_mix = mul(weights[n], (scales[n] * upstream).astype(BF), NN).astype(BF)
        group, width = outgoing[n].shape[:2]
        for g in range(group):
            part = slice(g * width, (g + 1) * width)
            grads[g, start + n * width : start + (n + 1) * width] = grad_out[part]
            outgoing[n][g] = grad_mix[part]


def third_kernel(
    live, in_t, in_f, time_x, spec_x, w_out, w_first, w_second, cols, time_dy, spec_dy,
    time_all, spec_all, backward, mix_t, mix_f, *rest,
):
    kept, totals = rest[:10], rest[10:12]
    result, grad_stream, turn_sum, grads_in, grad_norm = rest[12:17]
    (grads, out_t, out_f, back_t, back_f, rows_t, terms, held, held_two, ds_t, ds_f, query, upstream_ref,
     grad_k, grad_v, sems, sems_two, sems_t, sems_f) = rest[17:]
    me, mate, across, far = places()
    greet((mate, across, far))
    gain, shift, scale = cols[:, 12:13], cols[:, 13:14], cols[:, 18:19]
    weights = (whole_weight(w_out, 2), whole_weight(w_out, 3))
    scales = (cols[:, 16:17], cols[:, 17:18])
    stream = jnp.concatenate(
        [
            add_branch(joined(in_t), weights[0], scales[0], time_x[...]),
            add_branch(joined(in_f), weights[1], scales[1], spec_x[...]),
        ],
        axis=1,
    )
    rows_t[...] = jnp.zeros_like(rows_t)
    rows_t[:live, :] = time_dy[0].astype(F32)
    upstream = jnp.concatenate([rows_t[...].T, spec_dy[0].astype(F32).T], axis=1)
    unit, scale_inv = norm_parts(stream)
    normed = (unit * gain + shift).astype(BF)
    grad_branch = (scale * upstream).astype(BF)
    group, width, part = w_first.shape
    branch = grad_normed = None
    for g in range(group):
        hidden = mul(w_first[g], normed, TN)
        active, slope = gelu_pair(hidden)
        active = active.astype(BF)
        made = mul(w_second[g], active, TN)
        branch = made if branch is None else branch + made
        grad_hidden = (mul(w_second[g], grad_branch, NN) * slope).astype(BF)
        made = mul(w_first[g], grad_hidden, NN)
        grad_normed = made if grad_normed is None else grad_normed + made
        grads[g, :width] = mul(normed, grad_hidden, NT).astype(BF)
        grads[g, width : width + part] = mul(active, grad_branch, NT).astype(BF)
    result[...] = stream + scale * branch
    last = width + part + 2 * in_t.shape[1]
    sums = jnp.concatenate(
        [
            jnp.sum(value, axis=1, keepdims=True)
            for value in (grad_normed * unit, grad_normed, upstream * branch)
        ] + [jnp.zeros((width, LANES - 3), F32)],
        axis=1,
    ).T[:16].astype(BF)
    for g in range(group):
        grads[g, last : last + 16] = sums if g == 0 else jnp.zeros_like(sums)
    value = upstream + norm_back(unit, scale_inv, grad_normed * gain)
    grad_stream[...] = value
    branches_back(value, (in_t, in_f), weights, scales, grads, width + part, (out_t, out_f))
    exchange((out_t, out_f), (back_t, back_f), (sems_t, sems_f))
    scatter = Scatter(grads, held_two, sems_two)
    scatter.start()
    attend_back(
        True, kept, totals, (back_t, back_f), (mix_t, mix_f), (ds_t, ds_f, query, upstream_ref, grad_k, grad_v),
        scatter.middle,
    )
    stream_terms(time_all, spec_all, backward, ds_t, ds_f, terms, grads_in)
    scatter.middle()
    turn_sum[...] = scatter.finish().astype(BF)
    scatter = Scatter(terms, held, sems)
    scatter.start()
    scatter.middle()
    grad_norm[...] = scatter.finish()


def attend_back(cross, kept, totals, upstream_in, mixed, scratch, between):
    qt, kt, vt, qf, kf, vf, kt_rows, vt_rows, kf_rows, vf_rows = kept
    ds_t, ds_f, query, upstream, grad_k, grad_v = scratch
    group, _, block_t = mixed[0].shape
    block_f = mixed[1].shape[2]
    count = kt_rows.shape[0] // group

    def prepare(stream, q):
        size = q.shape[1]
        block = size // group
        for head in range(2):
            query[head, :, :size] = with_rows(q[...], head, split_three(-totals[stream][head : head + 1, :]))
            rows = slice(head * HD, (head + 1) * HD)
            for g in range(group):
                part = upstream_in[stream][g, rows, :]
                inner = jnp.sum(
                    part.astype(F32) * mixed[stream][g, rows, :].astype(F32), axis=0, keepdims=True
                )
                padded = jnp.concatenate(
                    [part, *split_three(-inner), jnp.zeros((HP - HD - 3, block), BF)], axis=0
                )
                other = jnp.zeros((HP, block), BF)
                both = [padded, other] if head == 0 else [other, padded]
                upstream[head, :, g * block : (g + 1) * block] = jnp.concatenate(both, axis=0)

    def spread(dst, base, source):
        turned = source.T
        for g in range(group):
            part = turned[g * count : (g + 1) * count]
            part = jnp.concatenate([part, jnp.zeros((block_t - count, LANES), F32)], axis=0)
            dst[base : base + LANES, g * block_t : (g + 1) * block_t] = part.T.astype(BF)

    def store_keys(time_keys):
        if time_keys:
            size = kt_rows.shape[0]
            spread(ds_t, LANES, grad_k[:, :size] * log_two)
            spread(ds_t, 2 * LANES, grad_v[:, :size])
        else:
            ds_f[LANES : 2 * LANES, :] = (grad_k[...] * log_two).astype(BF)
            ds_f[2 * LANES :, :] = grad_v[...].astype(BF)

    time_side, spec_side = (kt_rows, kt, vt_rows), (kf_rows, kf, vf_rows)
    if cross:
        time_side, spec_side = spec_side, time_side
    size_t = qt.shape[1]
    prepare(0, qt)
    back_blocks(
        size_t, *time_side, query.at[:, :, :size_t], upstream.at[:, :, :size_t], ds_t, grad_k, grad_v, None
    )
    store_keys(not cross)
    prepare(1, qf)
    back_blocks(block_f, *spec_side, query, upstream, ds_f, grad_k, grad_v, between)
    store_keys(cross)


def stream_terms(time_all, spec_all, backward, ds_t, ds_f, terms, grads):
    group = spec_all.shape[0]
    for n, (ds, whole) in enumerate(((ds_t, time_all), (ds_f, spec_all))):
        block = whole.shape[2]
        lanes_out = slice(0, LANES) if n == 0 else slice(LANES, None)
        total = None
        for g in range(group):
            part = ds[:, g * block : (g + 1) * block]
            terms[g, :, lanes_out] = mul(backward[n], part, NN).astype(BF)
            made = mul(part, whole[g], NT)
            total = made if total is None else total + made
        for piece in range(6):
            start = (n * 6 + piece) * HD
            grads[start : start + HD] = total[piece * HP : piece * HP + HD].astype(BF)
        row = lax.broadcasted_iota(jnp.int32, (16, group * block), 0)
        made = mul((row == n).astype(BF), ds[...], NT)
        sums = made if n == 0 else sums + made
    start = 12 * HD
    grads[start : start + 16] = sums.astype(BF)


def fourth_kernel(
    step_rows, grad_norm, grad_in, time_y, spec_y, time_x, spec_x, in_t, in_f, w_out, cols,
    time_all, spec_all, backward, mix_t, mix_f, *rest,
):
    kept, totals = rest[:10], rest[10:12]
    turn_sum, cross_in, attn_in, attn_out, small = rest[12:17]
    stream_grad, grad_a, grad_b, grad_c, grad_d, packed, scalars = rest[17:24]
    (early_in, late_in, stage_early, stage_late, early, late, grads, out_t, out_f, back_t, back_f, terms, held, held_two, ds_t, ds_f,
     query, upstream_ref, grad_k, grad_v, parts, sems, sems_two, sems_t, sems_f, sems_e, sems_l, sems_p) = rest[24:]
    me, mate, across, far = places()
    size = lax.axis_size("dp")
    early_sum = Sum(early_in, stage_early, early, sems_e, sum_parts(early.shape[0], size))
    late_sum = Sum(late_in, stage_late, late, sems_l, sum_parts(late.shape[0], size))
    greet((mate, across, far), [early_sum.bit(bit)[1] for bit in bit_orders(size)[0]])
    unit, scale_inv = norm_parts(jnp.concatenate([time_y[...], spec_y[...]], axis=1))
    value = grad_in[...] + norm_back(unit, scale_inv, grad_norm[...])
    weights = (whole_weight(w_out, 0), whole_weight(w_out, 1))
    branches_back(value, (in_t, in_f), weights, (cols[:, 14:15], cols[:, 15:16]), grads, 0, (out_t, out_f))
    scatter = Scatter(grads, held_two, sems_two)
    scatter.start()
    exchange((out_t, out_f), (back_t, back_f), (sems_t, sems_f))
    scatter.middle()
    rows_turn, rows_cross, rows_out = turn_sum.shape[0], cross_in.shape[0], grads.shape[1]
    rows_early = rows_turn + rows_cross + rows_out
    early_in[:rows_turn] = turn_sum[...]
    early_in[rows_turn : rows_turn + rows_cross] = cross_in[...]
    early_in[rows_early:] = jnp.zeros_like(early_in[rows_early:])
    early_in[rows_turn + rows_cross : rows_early] = scatter.finish().astype(BF)
    attend_back(
        False, kept, totals, (back_t, back_f), (mix_t, mix_f), (ds_t, ds_f, query, upstream_ref, grad_k, grad_v),
        early_sum.advance,
    )
    stream_terms(time_all, spec_all, backward, ds_t, ds_f, terms, late_in)
    late_in[rows_cross:] = jnp.zeros_like(late_in[rows_cross:])
    early_sum.advance()
    late_sum.advance()
    scatter = Scatter(terms, held, sems)
    scatter.start()
    early_sum.advance()
    late_sum.advance()
    scatter.middle()
    early_sum.advance()
    late_sum.advance()
    unit, scale_inv = norm_parts(jnp.concatenate([time_x[...], spec_x[...]], axis=1))
    stream_grad[...] = value + norm_back(unit, scale_inv, scatter.finish())
    early_sum.complete()
    late_sum.complete()
    local, width = attn_out.shape[1:]
    squares = jnp.zeros((1, width), F32)
    packed_rows = [jnp.zeros((1, width), F32) for _ in range(19)]

    def add_squares(total, gradient):
        return total + jnp.sum(gradient * gradient, axis=0, keepdims=True)

    for cross, buffer, base in ((False, late, 0), (True, early, rows_turn)):
        sums = buffer[base + 12 * HD : base + 12 * HD + 16].astype(F32)
        for stream, picks in enumerate(picks_of(cross)):
            turned = jnp.concatenate([sums, jnp.zeros((LANES - 16, width), F32)], axis=0).T
            for block, (index, group) in enumerate(picks):
                start = base + (stream * 6 + block * 2) * HD
                plain = buffer[start : start + local].astype(F32)
                column = jnp.concatenate(
                    [
                        turned[block * LANES + head * HP : block * LANES + head * HP + HD, stream : stream + 1]
                        for head in range(2)
                    ],
                    axis=0,
                )
                row = norm_rows[index][group]
                gradient = plain * small[row : row + 1, :] + column * small[row + 1 : row + 2, :]
                grad_a[index, group] = gradient
                squares = add_squares(squares, gradient)
                weight = attn_in[index, group]
                packed_rows[row] += jnp.sum(weight * plain, axis=0, keepdims=True)
                packed_rows[row + 1] += jnp.sum(weight * column, axis=0, keepdims=True)
    for index in range(4):
        start = rows_turn + rows_cross + index * local if index < 2 else 2 * width + (index - 2) * local
        plain = early[start : start + local].astype(F32)
        gradient = plain * small[14 + index : 15 + index, :]
        grad_b[index] = gradient
        squares = add_squares(squares, gradient)
        packed_rows[14 + index] += jnp.sum(attn_out[index] * plain, axis=0, keepdims=True)
    for target, start in ((grad_c, 0), (grad_d, width)):
        gradient = early[start : start + width].astype(F32)
        target[...] = gradient
        squares = add_squares(squares, gradient)
    smalls = early[2 * width + 2 * local : 2 * width + 2 * local + 16].astype(F32)
    for n, row in enumerate((12, 13, 18)):
        packed_rows[row] += smalls[n : n + 1]
    parts[me] = jnp.concatenate(packed_rows + [squares] + [jnp.zeros((4, width), F32)], axis=0)
    copies = [
        push(parts.at[me], parts.at[me], sems_p.at[0, n], sems_p.at[1, n], other)
        for n, other in enumerate((across, far, mate))
    ]
    for copy in copies:
        copy.wait()
    total = parts[0]
    for n in range(1, parts.shape[0]):
        total = total + parts[n]
    packed[...] = total
    row = lax.broadcasted_iota(jnp.int32, total.shape, 0)
    every = jnp.where(row < 19, total * total, jnp.where(row == 19, total, 0.0))
    norm = jnp.sqrt(jnp.sum(jnp.sum(every, axis=0, keepdims=True), axis=1, keepdims=True))
    factor = jnp.minimum(1.0, clip_level / norm)
    lane = lax.broadcasted_iota(jnp.int32, scalars.shape, 1)
    scalars[...] = jnp.where(lane == 0, norm, factor)


def adam_parts(weight, first_moment, second_moment, gradient, step_rate, decay_rate):
    first_new = beta_first * first_moment + (1.0 - beta_first) * gradient
    second_new = beta_second * second_moment + (1.0 - beta_second) * gradient * gradient
    first_fix = 1.0 - beta_first**STEP
    second_fix = 1.0 - beta_second**STEP
    direction = (first_new * (1.0 / first_fix)) / (jnp.sqrt(second_new * (1.0 / second_fix)) + adam_eps)
    return (weight - step_rate * (direction + decay_rate * weight), first_new, second_new)


def last_kernel(live, scalars, result, stream_grad, *refs):
    ins, outs = refs[:20], refs[20:]
    factor = scalars[:, 1:2]
    rates = (rate_matrix, rate_output, rate_matrix, rate_matrix, rate_small)
    for n, rate in enumerate(rates):
        gradient, weight, first_moment, second_moment = (ref[...] for ref in ins[4 * n : 4 * n + 4])
        if n == 4:
            gradient = gradient[: weight.shape[0]]
        made = adam_parts(
            weight, first_moment, second_moment, gradient * factor, rate, 0.0 if n == 4 else decay_matrix
        )
        for target, value in zip(outs[3 * n : 3 * n + 3], made):
            target[...] = value
    time_out, spec_out, time_grad, spec_grad, shift_gradient, norm = outs[15:]

    @pl.when(pl.program_id(0) == 0)
    def _():
        for source, one, two in ((result, time_out, spec_out), (stream_grad, time_grad, spec_grad)):
            one[0] = source[:, :LANES].T[:live]
            two[0] = source[:, LANES:].T
        shift_gradient[...] = ins[16][13:14] * factor
        norm[...] = scalars[:, 0:1]


def shards(
    time_in, spec_in, rate_flags, band_limits, time_cot, spec_cot, attn_in, attn_out, ffn_in, ffn_out, small,
    attn_in_m, attn_in_v, attn_out_m, attn_out_v, ffn_in_m, ffn_in_v, ffn_out_m, ffn_out_v, small_m, small_v,
):
    group, size = lax.axis_size("mp"), lax.axis_size("dp")
    live = time_in.shape[1]
    count = -(-live // 16) * 16
    block_t, block_f = LANES, spec_in.shape[1]
    width, local, part = time_in.shape[2], attn_in.shape[2], ffn_in.shape[1]
    lanes = block_t + block_f
    size_t, size_f, rows_t = group * block_t, group * block_f, group * count

    whole = (shape_of((group, width, block_t), BF), shape_of((group, width, block_f), BF))
    stream = (shape_of((width, block_t), F32), shape_of((width, block_f), F32))
    mix = (shape_of((group, local, block_t), BF), shape_of((group, local, block_f), BF))
    kept_shapes = tuple(
        shape_of(s, BF)
        for s in [(LANES, size_t)] + [(LANES, rows_t)] * 2 + [(LANES, size_f)] * 3 + [(rows_t, LANES)] * 2
        + [(size_f, LANES)] * 2
    ) + (shape_of((2, size_t), F32), shape_of((2, size_f), F32))
    packed_weights = (2, 3 * LANES, width)
    score = pltpu.VMEM((2, size_f, max(size_t, block_f)), F32)
    smem = pl.BlockSpec(memory_space=pltpu.SMEM)

    one = call(
        functools.partial(first_kernel, live), "first",
        stream + whole + mix + mix + kept_shapes + (
            shape_of(packed_weights, BF), shape_of((2, 3 * LANES, 1), F32), shape_of((2, 2, width, 3 * LANES), BF),
            shape_of((group,) + attn_out.shape, BF), shape_of((group, width, part), BF), shape_of((1, size_f), F32),
            shape_of((width, LANES), F32),
        ),
        (time_in, spec_in, rate_flags, band_limits, attn_in, attn_out, ffn_in, small),
        [
            pltpu.VMEM(packed_weights, BF), pltpu.VMEM((2, 3 * LANES, 1), F32), pltpu.VMEM((LANES, width), F32), score,
            dma(6, 2), dma(6, 2), dma(2, 3), dma(2, 3),
        ],
        0, specs={2: smem, 3: smem},
    )
    (time_x, spec_x, time_all, spec_all, mix_t, mix_f, all_t, all_f), kept = one[:8], one[8:20]
    forward_two, offsets_two, backward, w_out, w_first, bias, cols = one[20:]

    two = call(
        functools.partial(second_kernel, live), "second", stream + whole + mix + mix + kept_shapes + (
            shape_of((group, part, width), BF),
        ),
        (time_x, spec_x, all_t, all_f, w_out, cols, forward_two, offsets_two, bias, ffn_out),
        [score, dma(6, 2), dma(6, 1), dma(2, 3), dma(2, 3)], 1,
    )
    (time_y, spec_y, time_all_y, spec_all_y, mix_t_y, mix_f_y, all_t_y, all_f_y), kept_y = two[:8], two[8:20]
    w_second = two[20]

    rows_turn, rows_in = width + part + 2 * local + 16, 6 * local + 16
    back_scratch = [
        pltpu.VMEM((3 * LANES, size_t), BF), pltpu.VMEM((3 * LANES, size_f), BF),
        pltpu.VMEM((2, LANES, size_f), BF), pltpu.VMEM((2, LANES, size_f), BF),
        pltpu.VMEM((LANES, size_f), F32), pltpu.VMEM((LANES, size_f), F32),
    ]
    mixes = [pltpu.VMEM(m.shape, BF) for m in mix + mix]
    result, grad_stream, turn_sum, cross_in, grad_norm = call(
        functools.partial(third_kernel, live), "third",
        (
            shape_of((width, lanes), F32), shape_of((width, lanes), F32), shape_of((rows_turn, width), BF),
            shape_of((rows_in, width), BF), shape_of((width, lanes), F32),
        ),
        (
            all_t_y, all_f_y, time_y, spec_y, w_out, w_first, w_second, cols, time_cot, spec_cot,
            time_all_y, spec_all_y, backward[1], mix_t_y, mix_f_y,
        ) + tuple(kept_y),
        [pltpu.VMEM((group, rows_turn, width), BF)] + mixes + [
            pltpu.VMEM((LANES, width), F32), pltpu.VMEM((group, width, lanes), BF), pltpu.VMEM((4, width, lanes), BF),
            pltpu.VMEM((4, rows_turn, width), BF),
        ] + back_scratch + [dma(2, 3), dma(2, 3), dma(2, 3), dma(2, 3)], 2,
    )

    rows_early = sum_rows(rows_turn + rows_in + 2 * local, size)
    rows_late = sum_rows(rows_in, size)
    steps = 2 * (size.bit_length() - 1)
    stream_grad, grad_a, grad_b, grad_c, grad_d, packed, scalars = call(
        functools.partial(fourth_kernel, None), "fourth",
        (
            shape_of((width, lanes), F32), shape_of(attn_in.shape, F32), shape_of(attn_out.shape, F32),
            shape_of(ffn_in.shape, F32), shape_of(ffn_out.shape, F32), shape_of((24, width), F32), shape_of((1, LANES), F32),
        ),
        (
            grad_norm, grad_stream, time_y, spec_y, time_x, spec_x, all_t, all_f, w_out, cols,
            time_all, spec_all, backward[0], mix_t, mix_f,
        ) + tuple(kept) + (turn_sum, cross_in, attn_in, attn_out, small),
        [
            pltpu.VMEM((rows_early, width), BF), pltpu.VMEM((rows_late, width), BF),
            pltpu.VMEM((rows_early, width), BF), pltpu.VMEM((rows_late, width), BF),
            pltpu.VMEM((rows_early, width), BF), pltpu.VMEM((rows_late, width), BF), pltpu.VMEM((group, 2 * local, width), BF),
        ] + mixes + [
            pltpu.VMEM((group, width, lanes), BF), pltpu.VMEM((4, width, lanes), BF), pltpu.VMEM((4, 2 * local, width), BF),
        ] + back_scratch + [
            pltpu.VMEM((group, 24, width), F32), dma(2, 3), dma(2, 3), dma(2, 3), dma(2, 3), dma(2, 2, steps),
            dma(2, 2, steps), dma(2, 3),
        ], 3,
    )

    pieces = 4
    ins, in_specs, outs, out_specs = [], [], [], []
    for gradient, weight, first_moment, second_moment in (
        (grad_a, attn_in, attn_in_m, attn_in_v), (grad_b, attn_out, attn_out_m, attn_out_v),
        (grad_c, ffn_in, ffn_in_m, ffn_in_v), (grad_d, ffn_out, ffn_out_m, ffn_out_v),
    ):
        flat = (weight.size // width, width)
        spec = pl.BlockSpec((flat[0] // pieces, width), lambda i: (i, 0))
        ins += [value.reshape(flat) for value in (gradient, weight, first_moment, second_moment)]
        in_specs += [spec] * 4
        outs += [shape_of(flat, F32)] * 3
        out_specs += [spec] * 3

    def full(shape):
        return pl.BlockSpec(shape, lambda i: (0,) * len(shape))

    ins += [packed, small, small_m, small_v]
    in_specs += [full(packed.shape)] + [full(small.shape)] * 3
    outs += [shape_of(small.shape, F32)] * 3
    out_specs += [full(small.shape)] * 3
    for shape in ((1, live, width), (1, block_f, width)) * 2 + ((1, width), (1, 1)):
        outs.append(shape_of(shape, F32))
        out_specs.append(full(shape))
    made = pl.pallas_call(
        functools.partial(last_kernel, live), name="last", grid=(pieces,), out_shape=outs,
        in_specs=[full(scalars.shape), full(result.shape), full(stream_grad.shape)] + in_specs, out_specs=out_specs,
        compiler_params=pltpu.CompilerParams(vmem_limit_bytes=vmem_limit),
    )(scalars, result, stream_grad, *ins)
    updated = [
        value.reshape(weight.shape)
        for value, weight in zip(made[:15], [w for w in (attn_in, attn_out, ffn_in, ffn_out, small) for _ in range(3)])
    ]
    time_out, spec_out, time_grad, spec_grad, shift_gradient, norm = made[15:]
    return (time_out, spec_out, time_grad, spec_grad, norm[0, 0], *updated, shift_gradient[0])


def solution(mesh):
    tokens, copied = P("dp", "mp", None), P()
    a, b, c, d = P(None, None, "mp", None), P(None, "mp", None), P(None, "mp"), P("mp", None)
    return jax.shard_map(
        shards,
        mesh=mesh,
        in_specs=(
            tokens, tokens, P("dp"), P("dp"), tokens, tokens, a, b, c, d, copied,
            a, a, b, b, c, c, d, d, copied, copied,
        ),
        out_specs=(
            tokens, tokens, tokens, tokens, copied,
            a, a, a, b, b, b, c, c, c, d, d, d, copied, copied, copied, copied,
        ),
        check_vma=False,
    )
```

```python
import functools
import math

import jax
import jax.numpy as jnp
from jax import lax
from jax.experimental import pallas as pl
from jax.experimental.pallas import tpu as pltpu
from jax.sharding import PartitionSpec as P

HD = 48
HP = 64
LANES = 128
FRAMES = 256
STEP = 10
BF = jnp.bfloat16
F32 = jnp.float32
NN = ((1,), (0,))
NT = ((1,), (1,))
TN = ((0,), (0,))
MESH = pl.DeviceIdType.MESH

norm_eps = 1e-05
clip_level = 100.0
beta_first = 0.9
beta_second = 0.95
adam_eps = 1e-08
decay_matrix = 0.1
rate_matrix = 0.05
rate_output = 0.5
rate_small = 0.5
masked_score = -1000000000.0
score_scale = HD ** (-0.5)
log_two = math.log(2.0)
query_scale = score_scale / log_two
vmem_limit = 58 * 2**20
AUX = HD
MASK_ROW = HD + 3
norm_rows = ((0, 0, 0), (2, 2, 2), (4, 6, 6), (8, 10, 10))


def mul(left, right, dims):
    return lax.dot_general(left, right, (dims, ((), ())), preferred_element_type=F32)


def dma(*shape):
    return pltpu.SemaphoreType.DMA(shape)


def vmem():
    return pl.BlockSpec(memory_space=pltpu.VMEM)


def shape_of(shape, kind):
    return jax.ShapeDtypeStruct(shape, kind)


def call(kernel, name, outs, args, scratch, collective, specs=None):
    return pl.pallas_call(
        kernel,
        name=name,
        out_shape=outs,
        in_specs=[(specs or {}).get(n, vmem()) for n in range(len(args))],
        out_specs=tuple(vmem() for _ in outs),
        scratch_shapes=list(scratch),
        compiler_params=pltpu.CompilerParams(
            vmem_limit_bytes=vmem_limit, collective_id=collective, has_side_effects=True
        ),
    )(*args)


def places():
    me = lax.axis_index("mp")
    mate = me + 1 - 2 * lax.rem(me, 2)
    across = lax.rem(me + 2, 4)
    far = lax.rem(mate + 2, 4)
    return me, mate, across, far


def greet(others, partners=()):
    barrier = pltpu.get_barrier_semaphore()
    for other in others:
        pl.semaphore_signal(barrier, inc=1, device_id={"mp": other}, device_id_type=MESH)
    for partner in partners:
        pl.semaphore_signal(barrier, inc=1, device_id={"dp": partner}, device_id_type=MESH)
    pl.semaphore_wait(barrier, len(others) + len(partners))


def push_to(source, target, send, recv, device):
    copy = pltpu.make_async_remote_copy(
        source, target, send, recv, device_id=device, device_id_type=MESH
    )
    copy.start()
    return copy


def push(source, target, send, recv, device):
    return push_to(source, target, send, recv, {"mp": device})


def gather_start(refs, sems):
    me, mate, across, far = places()
    first = [push(ref.at[me], ref.at[me], sems.at[0, n], sems.at[1, n], across) for n, ref in enumerate(refs)]
    second = [push(ref.at[me], ref.at[me], sems.at[2, n], sems.at[3, n], mate) for n, ref in enumerate(refs)]
    return first, second


def gather_finish(refs, sems, started):
    me, mate, across, far = places()
    first, second = started
    third = []
    for n, ref in enumerate(refs):
        first[n].wait_recv()
        third.append(push(ref.at[across], ref.at[across], sems.at[4, n], sems.at[5, n], mate))
    for copy in first:
        copy.wait_send()
    for copy in second + third:
        copy.wait()


def send_block(source, target, sems, n, other):
    me, mate, across, far = places()
    return push(source.at[other], target.at[me], sems.at[0, n], sems.at[1, n], other)


def send_blocks(source, target, sems):
    me, mate, across, far = places()
    copies = [send_block(source, target, sems, n, other) for n, other in enumerate((across, far, mate))]
    target[me] = source[me]
    return copies


class Scatter:
    def __init__(self, source, held, sems):
        self.source, self.held, self.sems = source, held, sems

    def start_far(self):
        me, mate, across, far = places()
        self.one = push(self.source.at[far], self.held.at[0], self.sems.at[0, 0], self.sems.at[1, 0], mate)

    def start_mate(self):
        me, mate, across, far = places()
        self.two = push(self.source.at[mate], self.held.at[1], self.sems.at[0, 1], self.sems.at[1, 1], mate)

    def start(self):
        self.start_far()
        self.start_mate()

    def middle(self):
        me, mate, across, far = places()
        self.one.wait()
        self.held[2] = (self.source[across].astype(F32) + self.held[0].astype(F32)).astype(BF)
        self.cross = push(self.held.at[2], self.held.at[3], self.sems.at[0, 2], self.sems.at[1, 2], across)

    def finish(self):
        me, mate, across, far = places()
        self.two.wait()
        total = self.source[me].astype(F32) + self.held[1].astype(F32)
        self.cross.wait()
        return total + self.held[3].astype(F32)


def norm_parts(stream):
    center = stream - jnp.mean(stream, axis=0, keepdims=True)
    scale_inv = lax.rsqrt(jnp.mean(center * center, axis=0, keepdims=True) + norm_eps)
    return center * scale_inv, scale_inv


def norm_back(unit, scale_inv, scaled):
    return scale_inv * (
        scaled
        - jnp.mean(scaled, axis=0, keepdims=True)
        - unit * jnp.mean(scaled * unit, axis=0, keepdims=True)
    )


def attend_blocks(places_in, block, keys, queries, values, score, write, after):
    rows_k = keys.shape[0]
    row = lax.broadcasted_iota(jnp.int32, (LANES, block), 0)

    def make(n, head):
        query = queries[:, lanes_of(n, block)]
        own = (row < HP) if head == 0 else (row >= HP)
        score[head, :rows_k, :] = mul(keys[...], jnp.where(own, query, jnp.zeros_like(query)), NN)

    def finish(n, head):
        held = score[head, :rows_k, :]
        peak = jnp.max(held, axis=0, keepdims=True)
        shares = jnp.exp2(held - peak).astype(BF)
        mixed = mul(values[head * HP : (head + 1) * HP, :], shares, NN)
        total = mixed[AUX : AUX + 1, :]
        write(n, head, (mixed[:HD] * (1.0 / total)).astype(BF), peak + jnp.log2(total))

    make(places_in[0], 0)
    for step, n in enumerate(places_in):
        make(n, 1)
        finish(n, 0)
        if step + 1 < len(places_in):
            make(places_in[step + 1], 0)
        finish(n, 1)
        after(step, n)


def lanes_of(n, block):
    return pl.ds(n * block if isinstance(n, int) else pl.multiple_of(n * block, LANES), block)


def split_three(value):
    high = value.astype(BF)
    rest = value - high.astype(F32)
    middle = rest.astype(BF)
    return high, middle, (rest - middle.astype(F32)).astype(BF)


def with_rows(body, head, parts):
    row = lax.broadcasted_iota(jnp.int32, body.shape, 0) - head * HP
    out = jnp.where((row >= 0) & (row < HP), body.astype(F32), 0.0)
    for n, part in enumerate(parts):
        out = jnp.where(row == AUX + n, part.astype(F32), out)
    return out.astype(BF)


def back_unit(head, lanes, fresh, side, queries, upstream, grad_q, grad_k, grad_v):
    keys_rows, keys, values_rows = side
    rows_k = keys_rows.shape[0]
    own = slice(head * HP, (head + 1) * HP)
    shares = jnp.exp2(mul(keys_rows[...], queries[head, :, lanes], NN))
    inner = mul(values_rows[...], upstream[head, :, lanes], NN)
    grad_score = (shares * inner).astype(BF)
    shares = shares.astype(BF)
    grad_q[own, lanes] = (mul(keys[own, :], grad_score, NN) * score_scale).astype(BF)
    made_k = mul(queries[head, own, lanes], grad_score, NT)
    made_v = mul(upstream[head, own, lanes], shares, NT)
    grad_k[own, :rows_k] = made_k if fresh else grad_k[own, :rows_k] + made_k
    grad_v[own, :rows_k] = made_v if fresh else grad_v[own, :rows_k] + made_v


def prepare_queries(q, total, query):
    size = q.shape[1]
    for head in range(2):
        query[head, :, :size] = with_rows(q[...], head, split_three(-total[head : head + 1, :]))


def prepare_upstream(part, mixed, upstream, lanes):
    block = part.shape[1]
    for head in range(2):
        rows = slice(head * HD, (head + 1) * HD)
        inner = jnp.sum(part[rows].astype(F32) * mixed[rows].astype(F32), axis=0, keepdims=True)
        padded = jnp.concatenate(
            [part[rows], *split_three(-inner), jnp.zeros((HP - HD - 3, block), BF)], axis=0
        )
        other = jnp.zeros((HP, block), BF)
        both = [padded, other] if head == 0 else [other, padded]
        upstream[head, :, lanes] = jnp.concatenate(both, axis=0)


def back_time(side, kept, totals, back_t, mix_t, ds_t, query, upstream, grad_k, grad_v):
    group, _, block = mix_t.shape
    prepare_queries(kept[0], totals[0], query)
    for g in range(group):
        prepare_upstream(back_t[g], mix_t[g], upstream, lanes_of(g, block))
    for head in range(2):
        back_unit(head, slice(0, group * block), True, side, query, upstream, ds_t, grad_k, grad_v)


def spread_keys(ds, base, source, group, block):
    turned = source.T
    count, width = turned.shape[0] // group, turned.shape[1]
    for g in range(group):
        part = turned[g * count : (g + 1) * count]
        part = jnp.concatenate([part, jnp.zeros((block - count, width), F32)], axis=0)
        ds[base : base + width, g * block : (g + 1) * block] = part.T.astype(BF)


def keep_keys(time_keys, ds, grad_k, grad_v, rows, size, group, block):
    start, stop = rows
    key, value = grad_k[start:stop, :size] * log_two, grad_v[start:stop, :size]
    for base, made in ((LANES, key), (2 * LANES, value)):
        if time_keys:
            spread_keys(ds, base + start, made, group, block)
        else:
            ds[base + start : base + stop, :] = made.astype(BF)


def row_gradients(ds, whole, rows):
    group, _, block = whole.shape
    total = None
    for g in range(group):
        made = mul(ds[rows, g * block : (g + 1) * block], whole[g], NT)
        total = made if total is None else total + made
    return total


def bit_orders(size):
    bits = [1 << n for n in range(size.bit_length() - 1)]
    return bits, bits[1:2] + bits[:1] + bits[2:]


def cut_parts(count, size, parts):
    tile = 16 * size
    parts = min(parts, -(-count // tile))
    rows = -(-count // (tile * parts)) * tile
    return rows * parts, [(n * rows, rows, bit_orders(size)[n % 2]) for n in range(parts)]


def partner_of(bit):
    index = lax.axis_index("dp")
    mine = lax.rem(index // bit, 2)
    return mine, index + bit * (1 - 2 * mine)


def segment_of(part):
    first, rows, bits = part
    for bit in bits:
        rows = rows // 2
        first = first + partner_of(bit)[0] * rows
    return first, rows


def rows_of(first, rows):
    return pl.ds(first if isinstance(first, int) else pl.multiple_of(first, 16), rows)


class Halving:
    def __init__(self, source, stage, target, sems, parts):
        self.source, self.stage, self.target, self.sems = source, stage, target, sems
        self.state = [list(part[:2]) for part in parts]
        self.orders = [part[2] for part in parts]
        self.full = [part[1] for part in parts]
        self.steps, self.at, self.copies = len(self.orders[0]), 0, []

    def start(self):
        self.copies = []
        for n, (first, rows) in enumerate(self.state):
            mine, partner = partner_of(self.orders[n][self.at])
            half = rows // 2
            place = self.held(n)
            self.copies.append(
                push_to(
                    self.source.at[rows_of(first + (1 - mine) * half, half)], self.stage.at[rows_of(place, half)],
                    self.sems.at[0, n, self.at], self.sems.at[1, n, self.at], {"dp": partner},
                )
            )

    def held(self, n):
        total = self.full[n]
        return sum(self.full[:n]) + total - (total >> self.at)

    def finish(self):
        into = self.target if self.at == self.steps - 1 else self.source
        for n, copy in enumerate(self.copies):
            first, rows = self.state[n]
            mine, partner = partner_of(self.orders[n][self.at])
            half = rows // 2
            here, there = rows_of(first + mine * half, half), rows_of(self.held(n), half)
            copy.wait()
            into[here, :] = (self.source[here, :].astype(F32) + self.stage[there, :].astype(F32)).astype(BF)
            self.state[n] = [first + mine * half, half]
        self.at += 1


class Doubling:
    def __init__(self, target, sems, parts):
        self.target, self.sems = target, sems
        self.state = [list(segment_of(part)) for part in parts]
        self.orders = [part[2][::-1] for part in parts]
        self.steps, self.at, self.copies = len(self.orders[0]), 0, []

    def start(self):
        self.copies = []
        for n, (first, rows) in enumerate(self.state):
            mine, partner = partner_of(self.orders[n][self.at])
            here = self.target.at[rows_of(first, rows)]
            self.copies.append(
                push_to(here, here, self.sems.at[0, n, self.at], self.sems.at[1, n, self.at], {"dp": partner})
            )

    def finish(self):
        for n, copy in enumerate(self.copies):
            first, rows = self.state[n]
            mine, partner = partner_of(self.orders[n][self.at])
            copy.wait()
            self.state[n] = [first - mine * rows, 2 * rows]
        self.at += 1


class Direct:
    steps = 2

    def __init__(self, source, stage, target, sems):
        self.source, self.stage, self.target, self.sems, self.at = source, stage, target, sems, 0
        self.size = lax.axis_size("dp")
        self.rows = source.shape[0] // self.size

    def piece(self, index):
        return rows_of(index * self.rows, self.rows)

    def start(self):
        index = lax.axis_index("dp")
        self.copies = []
        for n in range(1, self.size):
            other = lax.rem(index + n, self.size)
            if self.at == 0:
                source, target = self.source.at[self.piece(other)], self.stage.at[n - 1]
            else:
                source = target = self.target.at[self.piece(index)]
            self.copies.append(
                push_to(
                    source, target, self.sems.at[self.at, 0, n - 1], self.sems.at[self.at, 1, n - 1], {"dp": other}
                )
            )

    def finish(self):
        for copy in self.copies:
            copy.wait()
        if self.at == 0:
            here = self.piece(lax.axis_index("dp"))
            total = self.source[here, :].astype(F32)
            for n in range(self.size - 1):
                total = total + self.stage[n].astype(F32)
            self.target[here, :] = total.astype(BF)
        self.at += 1


class Across:
    steps = 1

    def __init__(self, whole, sems, parts):
        self.whole, self.sems, self.parts, self.at = whole, sems, parts, 0

    def start(self):
        me, mate, across, far = places()
        self.copies = []
        for n, part in enumerate(self.parts):
            here = self.whole.at[me, rows_of(*segment_of(part))]
            self.copies.append(push(here, here, self.sems.at[0, n], self.sems.at[1, n], across))

    def finish(self):
        for copy in self.copies:
            copy.wait()
        self.at += 1


def segment_after(part):
    first, rows, bits = part
    for bit in bits[:-1]:
        rows = rows // 2
        first = first + partner_of(bit)[0] * rows
    return first, rows, bits[-1:]


class Chips:
    steps = 1

    def __init__(self, source, held, target, sems, parts):
        self.source, self.held, self.target, self.sems, self.at = source, held, target, sems, 0
        self.parts = parts[: len(parts) // 2]
        self.half = sum(part[1] for part in self.parts)

    def start(self):
        me, mate, across, far = places()
        chip = me // 2
        self.copies = []
        for n, part in enumerate(self.parts):
            first, rows = segment_of(part)
            self.copies.append(
                push(
                    self.source.at[rows_of(first + (1 - chip) * self.half, rows)],
                    self.held.at[n * rows : (n + 1) * rows], self.sems.at[0, n], self.sems.at[1, n], across,
                )
            )

    def finish(self):
        chip = places()[0] // 2
        for n, copy in enumerate(self.copies):
            copy.wait()
            first, rows = segment_of(self.parts[n])
            own = self.source[rows_of(first + chip * self.half, rows), :].astype(F32)
            total = own + self.held[n * rows : (n + 1) * rows].astype(F32)
            self.target[rows_of(first, rows), :] = total.astype(BF)
        self.at += 1


class Relay:
    steps = 1

    def __init__(self, whole, sems, blocks):
        self.whole, self.sems, self.blocks, self.at = whole, sems, blocks, 0

    def start(self):
        me, mate, across, far = places()
        self.copies = [
            push(self.whole.at[block], self.whole.at[block], self.sems.at[0, n], self.sems.at[1, n], mate)
            for n, block in enumerate(self.blocks)
        ]

    def finish(self):
        for copy in self.copies:
            copy.wait()
        self.at += 1


class Chain:
    def __init__(self, *stages):
        self.stages, self.now, self.flying = list(stages), 0, False

    def advance(self):
        if self.now == len(self.stages):
            return
        stage = self.stages[self.now]
        if self.flying:
            stage.finish()
            if stage.at == stage.steps:
                self.now += 1
                self.flying = False
                if self.now == len(self.stages):
                    return
                stage = self.stages[self.now]
        stage.start()
        self.flying = True

    def complete(self):
        while self.now < len(self.stages):
            self.advance()


def picks_of(cross):
    if cross:
        return ((2, 0), (3, 1), (3, 2)), ((3, 0), (2, 1), (2, 2))
    return ((0, 0), (0, 1), (0, 2)), ((1, 0), (1, 1), (1, 2))


def fold_weights(cross, attn_in, small, forward, offsets, backward):
    width = attn_in.shape[3]
    for stream, picks in enumerate(picks_of(cross)):
        blocks = []
        for block, (index, group) in enumerate(picks):
            row = norm_rows[index][group]
            weight = attn_in[index, group]
            folded = weight * small[row : row + 1, :]
            offset = jnp.sum(weight * small[row + 1 : row + 2, :], axis=1, keepdims=True)
            factor = query_scale if group == 0 else 1.0
            ones = (MASK_ROW,) if group == 0 else (AUX, AUX + 1, AUX + 2)
            spare = lax.broadcasted_iota(jnp.int32, (HP - HD, 1), 0) + HD
            marks = jnp.zeros((HP - HD, 1), F32)
            for one in ones:
                marks = jnp.where(spare == one, 1.0, marks)
            for head in range(2):
                rows = slice(head * HD, (head + 1) * HD)
                start = block * LANES + head * HP
                forward[stream, start : start + HD, :] = (folded[rows] * factor).astype(BF)
                forward[stream, start + HD : start + HP, :] = jnp.zeros((HP - HD, width), BF)
                offsets[stream, start : start + HD, :] = offset[rows] * factor
                offsets[stream, start + HD : start + HP, :] = marks
                blocks += [folded[rows], jnp.zeros((HP - HD, width), F32)]
        backward[stream] = jnp.concatenate(blocks, axis=0).T.astype(BF)


def project_time(live, time_all, forward, offsets, kept):
    qt, kt, vt, qf, kf, vf, kt_rows, vt_rows, kf_rows, vf_rows = kept
    group, _, block = time_all.shape
    row = lax.broadcasted_iota(jnp.int32, (LANES, block), 0)
    lane = lax.broadcasted_iota(jnp.int32, (LANES, block), 1)
    dead = jnp.where(lane < live, 0.0, masked_score)
    mask = jnp.where((row == MASK_ROW) | (row == MASK_ROW + HP), dead, 0.0)
    count = kt_rows.shape[0] // group
    for n in range(group):
        made = mul(forward[0], time_all[n], NN) + offsets[0]
        qt[:, n * block : (n + 1) * block] = made[:LANES].astype(BF)
        key, value = (made[LANES : 2 * LANES] + mask).astype(BF), made[2 * LANES :].astype(BF)
        lanes = slice(n * count, (n + 1) * count)
        kt_rows[lanes, :], vt_rows[lanes, :] = key.T[:count], value.T[:count]
    kt[...] = kt_rows[...].T
    vt[...] = vt_rows[...].T


def project_spec(n, spec_all, forward, offsets, bias, kept):
    qt, kt, vt, qf, kf, vf, kt_rows, vt_rows, kf_rows, vf_rows = kept
    block = spec_all.shape[2]
    lanes = lanes_of(n, block)
    row = lax.broadcasted_iota(jnp.int32, (LANES, block), 0)
    made = mul(forward[1], spec_all[n], NN) + offsets[1]
    qf[:, lanes] = made[:LANES].astype(BF)
    mask = jnp.where((row == MASK_ROW) | (row == MASK_ROW + HP), bias[:, lanes], 0.0)
    key, value = (made[LANES : 2 * LANES] + mask).astype(BF), made[2 * LANES :].astype(BF)
    kf[:, lanes], vf[:, lanes] = key, value
    kf_rows[lanes, :], vf_rows[lanes, :] = key.T, value.T


def time_attention(side, kept, totals, mix_t, all_t, sems, score):
    group, _, block = mix_t.shape
    copies = []

    def write(n, head, value, total):
        for g in range(group):
            mix_t[g, head * HD : (head + 1) * HD, :] = value[:, g * block : (g + 1) * block]
        totals[0][head : head + 1, :] = total

    def after(step, n):
        copies.extend(send_blocks(mix_t, all_t, sems))

    attend_blocks((0,), group * block, side[0], kept[0], side[1], score, write, after)
    return copies


def spec_attention(blocks, side, kept, totals, mix_f, all_f, sems, score, first, between):
    block = mix_f.shape[2]
    copies = []

    def write(n, head, value, total):
        mix_f[n, head * HD : (head + 1) * HD, :] = value
        totals[1][head : head + 1, lanes_of(n, block)] = total

    def after(step, n):
        step += first
        if step < 3:
            copies.append(send_block(mix_f, all_f, sems, step, n))
        else:
            all_f[n] = mix_f[n]
        between(step)

    attend_blocks(blocks, block, side[0], kept[3], side[1], score, write, after)
    return copies


def first_kernel(
    live, parts, time_in, spec_in, flags, limits, attn_in, attn_out, ffn_in, ffn_out, small,
    time_x, spec_x, time_all, spec_all, mix_t, mix_f, all_t, all_f, *rest,
):
    kept, totals = rest[:10], rest[10:12]
    forward_two, offsets_two, backward, weights, bias, cols = rest[12:18]
    forward, offsets, rows_t, score, sems_p, sems_q, sems_t, sems_f, sems_a, sems_d, sems_r, sems_s = rest[18:]
    me, mate, across, far = places()
    greet((mate, across, far), [partner_of(bit)[1] for bit in parts[0][2]])
    width = ffn_in.shape[0]
    for n, weight in enumerate((attn_out[...].reshape(width, width), ffn_in[...], ffn_out[...])):
        first = parts[n][0]
        weights[me, first : first + width] = weight.astype(BF)
        if parts[n][1] > width:
            weights[me, first + width : first + parts[n][1]] = jnp.zeros((parts[n][1] - width, width), BF)
    chain = Chain(
        Across(weights, sems_a, parts), Doubling(weights.at[across], sems_d, parts), Relay(weights, sems_r, (across,)),
    )
    chain.advance()
    rows_t[...] = jnp.zeros_like(rows_t)
    rows_t[:live, :] = time_in[0].astype(F32)
    time_x[...] = rows_t[...].T
    time_all[me] = norm_parts(time_x[...])[0].astype(BF)
    started_t = gather_start((time_all,), sems_p)
    spec_x[...] = spec_in[0].astype(F32).T
    spec_all[me] = norm_parts(spec_x[...])[0].astype(BF)
    started_f = gather_start((spec_all,), sems_q)
    own = Relay(weights, sems_s, (me,))
    own.start()
    fold_weights(False, attn_in, small, forward, offsets, backward.at[0])
    bins = lax.broadcasted_iota(jnp.int32, bias.shape, 1) // FRAMES
    bias[...] = jnp.where((bins < limits[0]) | (flags[0] == 0), 0.0, masked_score)
    gather_finish((time_all,), sems_p, started_t)
    chain.advance()
    project_time(live, time_all, forward, offsets, kept)
    time_side, spec_side = (kept[6], kept[2]), (kept[8], kept[5])
    copies = time_attention(time_side, kept, totals, mix_t, all_t, sems_t, score)
    project_spec(me, spec_all, forward, offsets, bias, kept)
    fold_weights(True, attn_in, small, forward_two, offsets_two, backward.at[1])
    cols[...] = jnp.concatenate(
        [small[...], jnp.zeros((LANES - small.shape[0], small.shape[1]), F32)], axis=0
    ).T
    own.finish()
    chain.advance()
    gather_finish((spec_all,), sems_q, started_f)
    for n in (mate, across, far):
        project_spec(n, spec_all, forward, offsets, bias, kept)

    def between(step):
        if step < 3:
            chain.advance()

    copies += spec_attention(
        (across, far, mate, me), spec_side, kept, totals, mix_f, all_f, sems_f, score, 0, between
    )
    for copy in copies:
        copy.wait()
    chain.complete()


def whole_weight(weights, index, rows):
    part = weights[:, index * rows : (index + 1) * rows]
    return part.reshape(-1, part.shape[2])


def joined(mixed):
    part = mixed[...]
    return part.reshape(-1, part.shape[2])


def add_branch(mixed, w_out, scale, stream):
    return stream + scale * mul(w_out, mixed, TN)


def second_kernel(
    live, time_x, spec_x, in_t, in_f, weights, cols, forward, offsets, bias,
    time_y, spec_y, time_all, spec_all, mix_t, mix_f, all_t, all_f, *rest,
):
    kept, totals = rest[:10], rest[10:12]
    score, sems_p, sems_q, sems_t, sems_f = rest[12:]
    local = in_t.shape[1]
    me, mate, across, far = places()
    greet((mate, across, far))
    time_y[...] = add_branch(joined(in_t), whole_weight(weights, 0, local), cols[:, 14:15], time_x[...])
    time_all[me] = norm_parts(time_y[...])[0].astype(BF)
    started_t = gather_start((time_all,), sems_p)
    spec_y[...] = add_branch(joined(in_f), whole_weight(weights, 1, local), cols[:, 15:16], spec_x[...])
    spec_all[me] = norm_parts(spec_y[...])[0].astype(BF)
    started_f = gather_start((spec_all,), sems_q)
    gather_finish((time_all,), sems_p, started_t)
    project_time(live, time_all, forward, offsets, kept)
    project_spec(me, spec_all, forward, offsets, bias, kept)
    gather_finish((spec_all,), sems_q, started_f)
    time_side, spec_side = (kept[6], kept[2]), (kept[8], kept[5])
    copies = []
    for step, n in enumerate((across, far, mate, me)):
        if step < 3:
            project_spec(n, spec_all, forward, offsets, bias, kept)
        copies += spec_attention((n,), time_side, kept, totals, mix_f, all_f, sems_f, score, step, lambda step: None)
    copies += time_attention(spec_side, kept, totals, mix_t, all_t, sems_t, score)
    for copy in copies:
        copy.wait()


def gelu_pair(values):
    share = 0.5 * (1.0 + lax.erf(values * (2.0**-0.5)))
    slope = share + values * (jnp.exp(-0.5 * values * values) * ((2.0 * math.pi) ** -0.5))
    return values * share, slope


def mixed_gradients(grad_stream, weights, scales, outgoing):
    for n, lanes in enumerate((slice(0, LANES), slice(LANES, None))):
        grad_mix = mul(weights[n], (scales[n] * grad_stream[:, lanes]).astype(BF), NN).astype(BF)
        group, width = outgoing[n].shape[:2]
        for g in range(group):
            outgoing[n][g] = grad_mix[g * width : (g + 1) * width]


def output_gradients(grad_stream, mixed, grads, start):
    for n, lanes in enumerate((slice(0, LANES), slice(LANES, None))):
        grad_out = mul(joined(mixed[n]), grad_stream[:, lanes].astype(BF), NT).astype(BF)
        group, width = mixed[n].shape[:2]
        for g in range(group):
            grads[g, start + n * width : start + (n + 1) * width] = grad_out[g * width : (g + 1) * width]


def third_kernel(
    live, parts, parts_turn, in_t, in_f, time_x, spec_x, w_all, cols, time_dy, spec_dy,
    time_all, spec_all, backward, mix_t, mix_f, *rest,
):
    kept, totals = rest[:10], rest[10:12]
    result, grad_stream, turn_part, grads_in, grad_norm = rest[12:17]
    (grads, out_t, out_f, back_t, back_f, rows_t, terms_t, terms_f, held_t, held_f, held_core, turn_in, turn_stage, actives,
     grad_hiddens, ds_t, ds_f, query, upstream_ref, grad_k, grad_v, sems_p, sems_q, sems_t, sems_f, sems_c, sems_h) = rest[17:]
    me, mate, across, far = places()
    greet((mate, across, far), [partner_of(bit)[1] for bit in parts[0][2]])
    group, local, block_t = mix_t.shape
    block_f, width = mix_f.shape[2], w_all.shape[2]
    w_first = w_all.at[:, parts[1][0] : parts[1][0] + width]
    w_second = w_all.at[:, parts[2][0] : parts[2][0] + width]
    gain, shift, scale = cols[:, 12:13], cols[:, 13:14], cols[:, 18:19]
    weights = (whole_weight(w_all, 2, local), whole_weight(w_all, 3, local))
    scales = (cols[:, 16:17], cols[:, 17:18])
    stream = jnp.concatenate(
        [
            add_branch(joined(in_t), weights[0], scales[0], time_x[...]),
            add_branch(joined(in_f), weights[1], scales[1], spec_x[...]),
        ],
        axis=1,
    )
    rows_t[...] = jnp.zeros_like(rows_t)
    rows_t[:live, :] = time_dy[0].astype(F32)
    upstream = jnp.concatenate([rows_t[...].T, spec_dy[0].astype(F32).T], axis=1)
    unit, scale_inv = norm_parts(stream)
    normed = (unit * gain + shift).astype(BF)
    grad_branch = (scale * upstream).astype(BF)
    branch = grad_normed = None
    for g in range(group):
        hidden = mul(w_first[g], normed, TN)
        active, slope = gelu_pair(hidden)
        actives[g] = active.astype(BF)
        made = mul(w_second[g], actives[g], TN)
        branch = made if branch is None else branch + made
        grad_hiddens[g] = (mul(w_second[g], grad_branch, NN) * slope).astype(BF)
        made = mul(w_first[g], grad_hiddens[g], NN)
        grad_normed = made if grad_normed is None else grad_normed + made
    value = upstream + norm_back(unit, scale_inv, grad_normed * gain)
    mixed_gradients(value, weights, scales, (out_t, out_f))
    copies_t = send_blocks(out_t, back_t, sems_t)
    copies_f = send_blocks(out_f, back_f, sems_f)
    last = 2 * width + 2 * local
    for g in range(group):
        grads[g, :width] = mul(normed, grad_hiddens[g], NT).astype(BF)
        grads[g, width : 2 * width] = mul(actives[g], grad_branch, NT).astype(BF)
    output_gradients(value, (in_t, in_f), grads, 2 * width)
    sums = jnp.concatenate(
        [
            jnp.sum(item, axis=1, keepdims=True)
            for item in (grad_normed * unit, grad_normed, upstream * branch)
        ] + [jnp.zeros((width, LANES - 3), F32)],
        axis=1,
    ).T[:16].astype(BF)
    for g in range(group):
        grads[g, last : last + 16] = sums if g == 0 else jnp.zeros_like(sums)
    core = lax.rem(me, 2)
    rows_turn, rows_half = grads.shape[1], turn_in.shape[0] // 2
    copies = [
        push(grads.at[2 * n + 1 - core], held_core.at[n], sems_c.at[0, n], sems_c.at[1, n], mate) for n in range(2)
    ]
    result[...] = stream + scale * branch
    grad_stream[...] = value
    for copy in copies_t:
        copy.wait()
    time_side, spec_side = (kept[6], kept[1], kept[7]), (kept[8], kept[4], kept[9])
    back_time(spec_side, kept, totals, back_t, mix_t, ds_t, query, upstream_ref, grad_k, grad_v)
    keep_keys(False, ds_f, grad_k, grad_v, (0, LANES), grad_k.shape[1], group, block_f)
    for n, copy in enumerate(copies):
        copy.wait()
        made = grads[2 * n + core].astype(F32) + held_core[n].astype(F32)
        first = n * rows_half
        turn_in[first : first + rows_turn] = made.astype(BF)
        if rows_half > rows_turn:
            turn_in[first + rows_turn : first + rows_half] = jnp.zeros((rows_half - rows_turn, width), BF)
    halving = Halving(turn_in, turn_stage, turn_in, sems_h, parts_turn)
    halving.start()
    prepare_queries(kept[3], totals[1], query)
    scatter = Scatter(terms_f, held_f, sems_q)
    size_t = kept[6].shape[0]
    for step, n in enumerate((across, far, mate, me)):
        lanes = lanes_of(n, block_f)
        if step < 3:
            copies_f[step].wait()
        prepare_upstream(back_f[n], mix_f[n], upstream_ref, lanes)
        for head in range(2):
            back_unit(head, lanes, step == 0, time_side, query, upstream_ref, ds_f, grad_k, grad_v)
        terms_f[n] = mul(backward[1, 1], ds_f[:, lanes], NN).astype(BF)
        if step == 1:
            scatter.start_far()
        if step == 2:
            scatter.middle()
            scatter.start_mate()
    keep_keys(True, ds_t, grad_k, grad_v, (0, LANES), size_t, group, block_t)
    for g in range(group):
        terms_t[g] = mul(backward[1, 0], ds_t[:, g * block_t : (g + 1) * block_t], NN).astype(BF)
    scatter_t = Scatter(terms_t, held_t, sems_p)
    scatter_t.start()
    halving.finish()
    halving.start()
    scatter_t.middle()
    store_rows(grads_in, ((ds_t, time_all), (ds_f, spec_all)))
    grad_norm[:, :LANES] = scatter_t.finish()
    grad_norm[:, LANES:] = scatter.finish()
    halving.finish()
    while halving.at < halving.steps - 1:
        halving.start()
        halving.finish()
    for n, (first, rows) in enumerate(halving.state):
        turn_part[n * rows : (n + 1) * rows] = turn_in[rows_of(first, rows), :]


def store_rows(target, streams):
    start = 0
    for n, (ds, whole) in enumerate(streams):
        for block in range(3):
            total = row_gradients(ds, whole, slice(block * LANES, (block + 1) * LANES))
            for head in range(2):
                target[start : start + HD] = total[head * HP : head * HP + HD].astype(BF)
                start += HD
        made = row_sums(ds, n)
        sums = made if n == 0 else sums + made
    target[start : start + 16] = sums.astype(BF)


def row_sums(ds, n):
    row = lax.broadcasted_iota(jnp.int32, (16, ds.shape[1]), 0)
    return mul((row == n).astype(BF), ds[...], NT)


def store_head(target, head, ds, whole):
    tiles = whole.shape[1] // LANES
    count = 3 * HD + 16
    for block in range(3):
        base = block * LANES + head * HP
        total = row_gradients(ds, whole, slice(base, base + HP))[:HD].astype(BF)
        for n in range(tiles):
            start = n * count + block * HD
            target[start : start + HD] = total[:, n * LANES : (n + 1) * LANES]
    sums = row_sums(ds, 0).astype(BF)
    for n in range(tiles):
        target[n * count + 3 * HD : (n + 1) * count] = sums[:, n * LANES : (n + 1) * LANES]
    if target.shape[0] > tiles * count:
        target[tiles * count :] = jnp.zeros_like(target[tiles * count :])


def load_head(target, tiles):
    count = 3 * HD + 16
    return jnp.concatenate([target[n * count : (n + 1) * count] for n in range(tiles)], axis=1)


def fourth_kernel(
    parts_turn, parts_in, parts_out, grad_norm, grad_in, time_y, spec_y, time_x, spec_x, in_t, in_f,
    w_all, cols, time_all, spec_all, backward, mix_t, mix_f, *rest,
):
    kept, totals = rest[:10], rest[10:12]
    turn_part, cross_in, attn_in, attn_out, small = rest[12:17]
    stream_grad, grad_a, grad_b, grad_c, grad_d, packed, scalars = rest[17:24]
    (turn_in, turn_stage, turn_out, turn_far, turn, cross, late_a, late_b, out, cross_one, late_a_one, late_b_one, out_one,
     cross_two, out_two, late_a_two, late_b_two, grads, out_t, out_f, back_t, back_f, terms_t, terms_f, held_t, held_f, held_two,
     ds_t, ds_f, query, upstream_ref, grad_k, grad_v, pieces, sems_q, sems_two, sems_three, sems_t, sems_f, sems_p, sems_y, sems_s,
     sems_turn, sems_cross, sems_a, sems_b, sems_out) = rest[24:]
    me, mate, across, far = places()
    size = lax.axis_size("dp")
    greet((mate, across, far), [lax.rem(lax.axis_index("dp") + n, size) for n in range(1, size)])
    group, local, block_t = mix_t.shape
    block_f, width = mix_f.shape[2], w_all.shape[2]

    def both(first, stage, last, sems, cut):
        return Chain(Halving(first, stage, last, sems.at[0], cut), Doubling(last, sems.at[1], cut))

    rest_parts = [segment_after(part) for part in parts_turn]
    rows = turn_part.shape[0] // len(parts_turn)
    for n, (first, count, _) in enumerate(rest_parts):
        turn_in[rows_of(first, rows), :] = turn_part[n * rows : (n + 1) * rows]
    rows_cross, rows_out = cross_in.shape[0], grads.shape[1]
    cross_one[:rows_cross] = cross_in[...]
    if cross_one.shape[0] > rows_cross:
        cross_one[rows_cross:] = jnp.zeros_like(cross_one[rows_cross:])
    chain_turn = Chain(
        Halving(turn_in, turn_stage, turn_out, sems_s, rest_parts),
        Chips(turn_out, turn_far, turn, sems_y, parts_turn), Doubling(turn, sems_turn, parts_turn[: len(parts_turn) // 2]),
    )
    chain_cross = both(cross_one, cross_two, cross, sems_cross, parts_in)
    chain_out = both(out_one, out_two, out, sems_out, parts_out)
    chain_a = Chain(Direct(late_a_one, late_a_two, late_a, sems_a))
    chain_b = Chain(Direct(late_b_one, late_b_two, late_b, sems_b))
    chain_turn.advance()
    chain_cross.advance()
    unit, scale_inv = norm_parts(jnp.concatenate([time_y[...], spec_y[...]], axis=1))
    value = grad_in[...] + norm_back(unit, scale_inv, grad_norm[...])
    weights = (whole_weight(w_all, 0, local), whole_weight(w_all, 1, local))
    mixed_gradients(value, weights, (cols[:, 14:15], cols[:, 15:16]), (out_t, out_f))
    copies_t = send_blocks(out_t, back_t, sems_t)
    copies_f = send_blocks(out_f, back_f, sems_f)
    output_gradients(value, (in_t, in_f), grads, 0)
    scatter = Scatter(grads, held_two, sems_two)
    scatter.start()
    stream_grad[...] = value
    for copy in copies_t:
        copy.wait()
    scatter.middle()
    time_side, spec_side = (kept[6], kept[1], kept[7]), (kept[8], kept[4], kept[9])
    size_t, size_f = kept[6].shape[0], kept[8].shape[0]
    back_time(time_side, kept, totals, back_t, mix_t, ds_t, query, upstream_ref, grad_k, grad_v)
    keep_keys(True, ds_t, grad_k, grad_v, (0, LANES), size_t, group, block_t)
    for g in range(group):
        terms_t[g] = mul(backward[0, 0], ds_t[:, g * block_t : (g + 1) * block_t], NN).astype(BF)
    chain_cross.advance()
    out_one[:rows_out] = scatter.finish().astype(BF)
    store_rows(out_one.at[rows_out:], ((ds_t, time_all),))
    rows_used = rows_out + 6 * HD + 16
    if out_one.shape[0] > rows_used:
        out_one[rows_used:] = jnp.zeros_like(out_one[rows_used:])
    chain_out.advance()
    prepare_queries(kept[3], totals[1], query)
    order = ((me, None), (mate, 2), (across, 0), (far, 1))
    moves = (
        (chain_turn, (0, 2, 4, 6, 7)), (chain_cross, (1, 3, 5, 6, 7)), (chain_out, (1, 2, 4, 5, 6, 7)), (chain_a, (5, 7)),
    )
    for head in range(2):
        for step, (n, arrival) in enumerate(order):
            lanes = lanes_of(n, block_f)
            if head == 0:
                if arrival is not None:
                    copies_f[arrival].wait()
                prepare_upstream(back_f[n], mix_f[n], upstream_ref, lanes)
            back_unit(head, lanes, step == 0, spec_side, query, upstream_ref, ds_f, grad_k, grad_v)
            for chain, when in moves:
                if head * 4 + step in when:
                    chain.advance()
        keep_keys(False, ds_f, grad_k, grad_v, (head * HP, (head + 1) * HP), size_f, group, block_f)
        if head == 0:
            store_head(late_a_one, 0, ds_f, spec_all)
            chain_a.advance()
    for n in (far, mate, across, me):
        terms_f[n] = mul(backward[0, 1], ds_f[:, lanes_of(n, block_f)], NN).astype(BF)
    scatter_t = Scatter(terms_t, held_t, sems_three)
    scatter = Scatter(terms_f, held_f, sems_q)
    scatter.start()
    scatter_t.start()
    store_head(late_b_one, 1, ds_f, spec_all)
    chain_b.advance()
    scatter.middle()
    scatter_t.middle()
    chains = (chain_turn, chain_cross, chain_out, chain_a, chain_b)
    for chain in chains:
        chain.advance()
    unit, scale_inv = norm_parts(jnp.concatenate([time_x[...], spec_x[...]], axis=1))
    for chain in chains:
        chain.complete()
    scaled = jnp.concatenate([scatter_t.finish(), scatter.finish()], axis=1)
    stream_grad[...] = stream_grad[...] + norm_back(unit, scale_inv, scaled)
    width = attn_out.shape[2]
    squares = jnp.zeros((1, width), F32)
    packed_rows = [jnp.zeros((1, width), F32) for _ in range(19)]

    def add_squares(total, gradient):
        return total + jnp.sum(gradient * gradient, axis=0, keepdims=True)

    tiles = width // LANES
    halves = [load_head(late, tiles).astype(F32) for late in (late_a, late_b)]
    time_rows = out[rows_out : rows_out + 6 * HD + 16].astype(F32)
    cross_rows = cross[: 12 * HD + 16].astype(F32)

    def turned(sums):
        return jnp.concatenate([sums, jnp.zeros((LANES - 16, width), F32)], axis=0).T

    sums_time, sums_cross = turned(time_rows[6 * HD :]), turned(cross_rows[12 * HD :])
    sums_late = [turned(half[3 * HD :]) for half in halves]
    for crossing in (False, True):
        for stream, picks in enumerate(picks_of(crossing)):
            for block, (index, group) in enumerate(picks):
                if crossing:
                    start, rows = (stream * 6 + block * 2) * HD, cross_rows
                else:
                    start, rows = block * 2 * HD, time_rows
                if crossing or stream == 0:
                    plain = rows[start : start + local]
                    sums = sums_cross if crossing else sums_time
                    sums, lane = (sums, sums), stream
                else:
                    plain = jnp.concatenate([half[block * HD : (block + 1) * HD] for half in halves], axis=0)
                    sums, lane = sums_late, 0
                column = jnp.concatenate(
                    [
                        sums[head][block * LANES + head * HP : block * LANES + head * HP + HD, lane : lane + 1]
                        for head in range(2)
                    ],
                    axis=0,
                )
                row = norm_rows[index][group]
                gradient = plain * small[row : row + 1, :] + column * small[row + 1 : row + 2, :]
                grad_a[index, group] = gradient.astype(BF)
                squares = add_squares(squares, gradient)
                weight = attn_in[index, group]
                packed_rows[row] += jnp.sum(weight * plain, axis=0, keepdims=True)
                packed_rows[row + 1] += jnp.sum(weight * column, axis=0, keepdims=True)
    for index in range(4):
        if index < 2:
            plain = out[index * local : (index + 1) * local].astype(F32)
        else:
            start = 2 * width + (index - 2) * local
            plain = turn[start : start + local].astype(F32)
        gradient = plain * small[14 + index : 15 + index, :]
        grad_b[index] = gradient.astype(BF)
        squares = add_squares(squares, gradient)
        packed_rows[14 + index] += jnp.sum(attn_out[index] * plain, axis=0, keepdims=True)
    for target, start in ((grad_c, 0), (grad_d, width)):
        target[...] = turn[start : start + width]
        squares = add_squares(squares, turn[start : start + width].astype(F32))
    smalls = turn[2 * width + 2 * local : 2 * width + 2 * local + 16].astype(F32)
    for n, row in enumerate((12, 13, 18)):
        packed_rows[row] += smalls[n : n + 1]
    pieces[me] = jnp.concatenate(packed_rows + [squares] + [jnp.zeros((4, width), F32)], axis=0)
    copies = [
        push(pieces.at[me], pieces.at[me], sems_p.at[0, n], sems_p.at[1, n], other)
        for n, other in enumerate((across, far, mate))
    ]
    for copy in copies:
        copy.wait()
    total = pieces[0]
    for n in range(1, pieces.shape[0]):
        total = total + pieces[n]
    packed[...] = total
    row = lax.broadcasted_iota(jnp.int32, total.shape, 0)
    every = jnp.where(row < 19, total * total, jnp.where(row == 19, total, 0.0))
    norm = jnp.sqrt(jnp.sum(jnp.sum(every, axis=0, keepdims=True), axis=1, keepdims=True))
    factor = jnp.minimum(1.0, clip_level / norm)
    lane = lax.broadcasted_iota(jnp.int32, scalars.shape, 1)
    scalars[...] = jnp.where(lane == 0, norm, factor)


def adam_parts(weight, first_moment, second_moment, gradient, step_rate, decay_rate):
    first_new = beta_first * first_moment + (1.0 - beta_first) * gradient
    second_new = beta_second * second_moment + (1.0 - beta_second) * gradient * gradient
    first_fix = 1.0 - beta_first**STEP
    second_fix = 1.0 - beta_second**STEP
    direction = (first_new * (1.0 / first_fix)) / (jnp.sqrt(second_new * (1.0 / second_fix)) + adam_eps)
    return (weight - step_rate * (direction + decay_rate * weight), first_new, second_new)


def last_kernel(live, scalars, packed, small, small_m, small_v, result, stream_grad, *refs):
    ins, outs = refs[:16], refs[16:28]
    small_outs, (time_out, spec_out, time_grad, spec_grad, shift_gradient, norm) = refs[28:31], refs[31:37]
    held, (sems_in, sems_out) = refs[37:53], refs[53:]
    rates = (rate_matrix, rate_output, rate_matrix, rate_matrix)
    copies = [pltpu.make_async_copy(ins[n], held[n], sems_in.at[n]) for n in range(16)]
    for copy in copies:
        copy.start()
    factor = scalars[:, 1:2]
    gradient = packed[: small.shape[0]] * factor
    made = adam_parts(small[...], small_m[...], small_v[...], gradient, rate_small, 0.0)
    for target, value in zip(small_outs, made):
        target[...] = value
    shift_gradient[...] = gradient[13:14].reshape(-1)
    norm[...] = scalars[:, 0:1]
    leaving = []
    for n, rate in enumerate(rates):
        for copy in copies[4 * n : 4 * n + 4]:
            copy.wait()
        gradient, weight, first_moment, second_moment = held[4 * n : 4 * n + 4]
        rows = weight.shape[0] // 3
        for piece in range(3):
            part = slice(piece * rows, (piece + 1) * rows)
            made = adam_parts(
                weight[part], first_moment[part], second_moment[part], gradient[part].astype(F32) * factor, rate, decay_matrix
            )
            for m, (target, value) in enumerate(zip((weight, first_moment, second_moment), made)):
                target[part] = value
                copy = pltpu.make_async_copy(
                    target.at[part], outs[3 * n + m].at[part], sems_out.at[9 * n + 3 * piece + m]
                )
                copy.start()
                leaving.append(copy)
        if n < 2:
            source, one, two = ((result, time_out, spec_out), (stream_grad, time_grad, spec_grad))[n]
            one[...] = source[:, :LANES].T[:live].reshape(live, 1, -1)
            two[0] = source[:, LANES:].T
    for copy in leaving:
        copy.wait()


def shards(
    time_in, spec_in, rate_flags, band_limits, time_cot, spec_cot, attn_in, attn_out, ffn_in, ffn_out, small,
    attn_in_m, attn_in_v, attn_out_m, attn_out_v, ffn_in_m, ffn_in_v, ffn_out_m, ffn_out_v, small_m, small_v,
):
    group, size = lax.axis_size("mp"), lax.axis_size("dp")
    live = time_in.shape[1]
    count = -(-live // 16) * 16
    block_t, block_f = LANES, spec_in.shape[1]
    width, local, part = time_in.shape[2], attn_in.shape[2], ffn_in.shape[1]
    lanes = block_t + block_f
    size_t, size_f, rows_t = group * block_t, group * block_f, group * count

    whole = (shape_of((group, width, block_t), BF), shape_of((group, width, block_f), BF))
    stream = (shape_of((width, block_t), F32), shape_of((width, block_f), F32))
    mix = (shape_of((group, local, block_t), BF), shape_of((group, local, block_f), BF))
    kept_shapes = tuple(
        shape_of(s, BF)
        for s in [(LANES, size_t)] + [(LANES, rows_t)] * 2 + [(LANES, size_f)] * 3 + [(rows_t, LANES)] * 2
        + [(size_f, LANES)] * 2
    ) + (shape_of((2, size_t), F32), shape_of((2, size_f), F32))
    packed_weights = (2, 3 * LANES, width)
    score = pltpu.VMEM((2, size_f, max(size_t, block_f)), F32)
    smem = pl.BlockSpec(memory_space=pltpu.SMEM)

    rows_one, _ = cut_parts(width, size, 1)
    rows_w = 3 * rows_one
    parts_w = [(n * rows_one, rows_one, bit_orders(size)[n % 2]) for n in range(3)]
    bits = len(parts_w[0][2])
    one = call(
        functools.partial(first_kernel, live, parts_w), "first",
        stream + whole + mix + mix + kept_shapes + (
            shape_of(packed_weights, BF), shape_of((2, 3 * LANES, 1), F32), shape_of((2, 2, width, 3 * LANES), BF),
            shape_of((group, rows_w, width), BF), shape_of((1, size_f), F32), shape_of((width, LANES), F32),
        ),
        (time_in, spec_in, rate_flags, band_limits, attn_in, attn_out, ffn_in, ffn_out, small),
        [
            pltpu.VMEM(packed_weights, BF), pltpu.VMEM((2, 3 * LANES, 1), F32), pltpu.VMEM((LANES, width), F32), score,
            dma(6, 1), dma(6, 1), dma(2, 3), dma(2, 3), dma(2, 3), dma(2, 3, bits), dma(2, 1), dma(2, 1),
        ],
        0, specs={2: smem, 3: smem},
    )
    (time_x, spec_x, time_all, spec_all, mix_t, mix_f, all_t, all_f), kept = one[:8], one[8:20]
    forward_two, offsets_two, backward, w_all, bias, cols = one[20:]

    two = call(
        functools.partial(second_kernel, live), "second", stream + whole + mix + mix + kept_shapes,
        (time_x, spec_x, all_t, all_f, w_all, cols, forward_two, offsets_two, bias),
        [score, dma(6, 1), dma(6, 1), dma(2, 3), dma(2, 3)], 1,
    )
    (time_y, spec_y, time_all_y, spec_all_y, mix_t_y, mix_f_y, all_t_y, all_f_y), kept_y = two[:8], two[8:20]

    rows_turn, rows_in = width + part + 2 * local + 16, 6 * local + 16
    back_scratch = [
        pltpu.VMEM((3 * LANES, size_t), BF), pltpu.VMEM((3 * LANES, size_f), BF),
        pltpu.VMEM((2, LANES, size_f), BF), pltpu.VMEM((2, LANES, size_f), BF),
        pltpu.VMEM((LANES, size_f), F32), pltpu.VMEM((LANES, size_f), F32),
    ]
    mixes = [pltpu.VMEM(m.shape, BF) for m in mix + mix]
    rows_pair, parts_turn = cut_parts(rows_turn, size, 2)
    parts_turn = parts_turn + [(first + rows_pair, rows, order) for first, rows, order in parts_turn]
    pair = pltpu.VMEM((2 * rows_pair, width), BF)
    terms = [pltpu.VMEM((group, width, block_t), BF), pltpu.VMEM((group, width, block_f), BF)]
    result, grad_stream, turn_part, cross_in, grad_norm = call(
        functools.partial(third_kernel, live, parts_w, parts_turn), "third",
        (
            shape_of((width, lanes), F32), shape_of((width, lanes), F32), shape_of((4 * rows_pair // size, width), BF),
            shape_of((rows_in, width), BF), shape_of((width, lanes), F32),
        ),
        (
            all_t_y, all_f_y, time_y, spec_y, w_all, cols, time_cot, spec_cot,
            time_all_y, spec_all_y, backward, mix_t_y, mix_f_y,
        ) + tuple(kept_y),
        [pltpu.VMEM((group, rows_turn, width), BF)] + mixes + [pltpu.VMEM((LANES, width), F32)] + terms + terms + [
            pltpu.VMEM((2, rows_turn, width), BF), pair, pair,
            pltpu.VMEM((group, part, lanes), BF), pltpu.VMEM((group, part, lanes), BF),
        ] + back_scratch + [dma(2, 3), dma(2, 3), dma(2, 3), dma(2, 3), dma(2, 2), dma(2, 4, bits)], 2,
    )

    rows_sum, parts_in = cut_parts(rows_in, size, 5)
    rows_out, parts_out = cut_parts(5 * local + 16, size, 4)
    rows_late, _ = cut_parts((width // LANES) * (3 * HD + 16), size, 1)
    sums, late, outs = (
        pltpu.VMEM(shape, BF) for shape in ((rows_sum, width), (rows_late, LANES), (rows_out, width))
    )
    pieces = pltpu.VMEM((size - 1, rows_late // size, LANES), BF)
    stream_grad, grad_a, grad_b, grad_c, grad_d, packed, scalars = call(
        functools.partial(fourth_kernel, parts_turn, parts_in, parts_out), "fourth",
        (
            shape_of((width, lanes), F32), shape_of(attn_in.shape, BF), shape_of(attn_out.shape, BF),
            shape_of(ffn_in.shape, BF), shape_of(ffn_out.shape, BF), shape_of((24, width), F32), shape_of((1, LANES), F32),
        ),
        (
            grad_norm, grad_stream, time_y, spec_y, time_x, spec_x, all_t, all_f, w_all, cols,
            time_all, spec_all, backward, mix_t, mix_f,
        ) + tuple(kept) + (turn_part, cross_in, attn_in, attn_out, small),
        [pair, pair, pair, pltpu.VMEM((rows_pair // size, width), BF), pltpu.VMEM((rows_pair, width), BF)] + [sums, late, late, outs] * 2 + [
            sums, outs, pieces, pieces, pltpu.VMEM((group, 2 * local, width), BF)] + mixes + terms + terms + [pltpu.VMEM((4, 2 * local, width), BF)]
        + back_scratch + [
            pltpu.VMEM((group, 24, width), F32), dma(2, 3), dma(2, 3), dma(2, 3), dma(2, 3), dma(2, 3), dma(2, 3), dma(2, 2), dma(2, 4, 1),
            dma(2, 2, bits), dma(2, 2, 5, bits), dma(2, 2, size - 1), dma(2, 2, size - 1), dma(2, 2, 4, bits),
        ], 3,
    )

    ins, outs = [], []
    for gradient, weight, first_moment, second_moment in (
        (grad_a, attn_in, attn_in_m, attn_in_v), (grad_b, attn_out, attn_out_m, attn_out_v),
        (grad_c, ffn_in, ffn_in_m, ffn_in_v), (grad_d, ffn_out, ffn_out_m, ffn_out_v),
    ):
        flat = (weight.size // width, width)
        ins += [value.reshape(flat) for value in (gradient, weight, first_moment, second_moment)]
        outs += [shape_of(flat, F32)] * 3
    outs += [shape_of(small.shape, F32)] * 3
    outs += [shape_of((live, 1, width), F32), shape_of((1, block_f, width), F32)] * 2
    outs += [shape_of((width,), F32), shape_of((1, 1), F32)]
    anywhere = pl.BlockSpec(memory_space=pl.ANY)
    made = pl.pallas_call(
        functools.partial(last_kernel, live), name="last", out_shape=outs,
        in_specs=[vmem()] * 7 + [anywhere] * 16, out_specs=[anywhere] * 12 + [vmem()] * 9,
        scratch_shapes=[pltpu.VMEM(value.shape, value.dtype) for value in ins] + [dma(16), dma(36)],
        compiler_params=pltpu.CompilerParams(vmem_limit_bytes=vmem_limit),
    )(scalars, packed, small, small_m, small_v, result, stream_grad, *ins)
    updated = [
        value.reshape(weight.shape)
        for value, weight in zip(made[:15], [w for w in (attn_in, attn_out, ffn_in, ffn_out, small) for _ in range(3)])
    ]
    time_out, spec_out, time_grad, spec_grad, shift_gradient, norm = made[15:]
    time_out, time_grad = (jnp.swapaxes(value, 0, 1) for value in (time_out, time_grad))
    return (time_out, spec_out, time_grad, spec_grad, norm[0, 0], *updated, shift_gradient)


def solution(mesh):
    tokens, copied = P("dp", "mp", None), P()
    a, b, c, d = P(None, None, "mp", None), P(None, "mp", None), P(None, "mp"), P("mp", None)
    return jax.shard_map(
        shards,
        mesh=mesh,
        in_specs=(
            tokens, tokens, P("dp"), P("dp"), tokens, tokens, a, b, c, d, copied,
            a, a, b, b, c, c, d, d, copied, copied,
        ),
        out_specs=(
            tokens, tokens, tokens, tokens, copied,
            a, a, a, b, b, b, c, c, c, d, d, d, copied, copied, copied, copied,
        ),
        check_vma=False,
    )
```

```python
import functools
import math

import jax
import jax.numpy as jnp
from jax import lax
from jax.experimental import pallas as pl
from jax.experimental.pallas import tpu as pltpu
from jax.sharding import PartitionSpec as P

HD = 48
HP = 64
LANES = 128
FRAMES = 256
STEP = 10
BF = jnp.bfloat16
F32 = jnp.float32
NN = ((1,), (0,))
NT = ((1,), (1,))
TN = ((0,), (0,))
MESH = pl.DeviceIdType.MESH

norm_eps = 1e-05
clip_level = 100.0
beta_first = 0.9
beta_second = 0.95
adam_eps = 1e-08
decay_matrix = 0.1
rate_matrix = 0.05
rate_output = 0.5
rate_small = 0.5
masked_score = -1000000000.0
score_scale = HD ** (-0.5)
log_two = math.log(2.0)
query_scale = score_scale / log_two
vmem_limit = 58 * 2**20
AUX = HD
MASK_ROW = HD + 3
norm_rows = ((0, 0, 0), (2, 2, 2), (4, 6, 6), (8, 10, 10))


def mul(left, right, dims):
    return lax.dot_general(left, right, (dims, ((), ())), preferred_element_type=F32)


def dma(*shape):
    return pltpu.SemaphoreType.DMA(shape)


def vmem():
    return pl.BlockSpec(memory_space=pltpu.VMEM)


def shape_of(shape, kind):
    return jax.ShapeDtypeStruct(shape, kind)


class Traffic:
    def __init__(self):
        self.loads, self.stores, self.leaving = [], {}, []

    def ready(self, group):
        for copy in self.loads[group]:
            copy.wait()

    def done(self, *refs):
        for ref in refs:
            copy = self.stores.pop(id(ref))
            copy.start()
            self.leaving.append(copy)

    def finish(self):
        for copy in list(self.stores.values()):
            copy.start()
            self.leaving.append(copy)
        for copy in self.leaving:
            copy.wait()


def call(kernel, name, outs, args, scratch, collective, specs=None, late=(), early=(), direct=()):
    ins, count = len(args), len(args) + len(outs) + len(scratch)
    flat = [n for group in late for n in group]
    extra = [pltpu.VMEM(args[n].shape, args[n].dtype) for n in flat]
    extra += [pltpu.VMEM(outs[n].shape, outs[n].dtype) for n in early]
    extra += [dma(max(len(flat), 1)), dma(max(len(early), 1))]

    def body(*refs):
        refs, held = list(refs[:count]), refs[count:]
        traffic = Traffic()
        place = 0
        for group in late:
            copies = []
            for n in group:
                copies.append(pltpu.make_async_copy(refs[n], held[place], held[-2].at[place]))
                copies[-1].start()
                refs[n] = held[place]
                place += 1
            traffic.loads.append(copies)
        for m, n in enumerate(early):
            ref = held[place + m]
            traffic.stores[id(ref)] = pltpu.make_async_copy(ref, refs[ins + n], held[-1].at[m])
            refs[ins + n] = ref
        kernel(traffic, *refs)
        traffic.finish()

    anywhere = pl.BlockSpec(memory_space=pl.ANY)
    remote = {} if collective is None else {"collective_id": collective, "has_side_effects": True}
    return pl.pallas_call(
        body,
        name=name,
        out_shape=outs,
        in_specs=[anywhere if n in flat else (specs or {}).get(n, vmem()) for n in range(ins)],
        out_specs=tuple(anywhere if n in early or n in direct else vmem() for n in range(len(outs))),
        scratch_shapes=list(scratch) + extra,
        compiler_params=pltpu.CompilerParams(vmem_limit_bytes=vmem_limit, **remote),
    )(*args)


def places():
    me = lax.axis_index("mp")
    mate = me + 1 - 2 * lax.rem(me, 2)
    across = lax.rem(me + 2, 4)
    far = lax.rem(mate + 2, 4)
    return me, mate, across, far


def greet(others, partners=()):
    barrier = pltpu.get_barrier_semaphore()
    for other in others:
        pl.semaphore_signal(barrier, inc=1, device_id={"mp": other}, device_id_type=MESH)
    for partner in partners:
        pl.semaphore_signal(barrier, inc=1, device_id={"dp": partner}, device_id_type=MESH)
    pl.semaphore_wait(barrier, len(others) + len(partners))


def push_to(source, target, send, recv, device):
    copy = pltpu.make_async_remote_copy(
        source, target, send, recv, device_id=device, device_id_type=MESH
    )
    copy.start()
    return copy


def push(source, target, send, recv, device):
    return push_to(source, target, send, recv, {"mp": device})


def gather_start(refs, sems):
    me, mate, across, far = places()
    first = [push(ref.at[me], ref.at[me], sems.at[0, n], sems.at[1, n], across) for n, ref in enumerate(refs)]
    second = [push(ref.at[me], ref.at[me], sems.at[2, n], sems.at[3, n], mate) for n, ref in enumerate(refs)]
    return first, second


def gather_finish(refs, sems, started):
    me, mate, across, far = places()
    first, second = started
    third = []
    for n, ref in enumerate(refs):
        first[n].wait_recv()
        third.append(push(ref.at[across], ref.at[across], sems.at[4, n], sems.at[5, n], mate))
    for copy in first:
        copy.wait_send()
    for copy in second + third:
        copy.wait()


def send_block(source, target, sems, n, other):
    me, mate, across, far = places()
    return push(source.at[other], target.at[me], sems.at[0, n], sems.at[1, n], other)


def send_blocks(source, target, sems):
    me, mate, across, far = places()
    copies = [send_block(source, target, sems, n, other) for n, other in enumerate((across, far, mate))]
    target[me] = source[me]
    return copies


class Scatter:
    def __init__(self, source, held, sems):
        self.source, self.held, self.sems = source, held, sems

    def start_far(self):
        me, mate, across, far = places()
        self.one = push(self.source.at[far], self.held.at[0], self.sems.at[0, 0], self.sems.at[1, 0], mate)

    def start_mate(self):
        me, mate, across, far = places()
        self.two = push(self.source.at[mate], self.held.at[1], self.sems.at[0, 1], self.sems.at[1, 1], mate)

    def start(self):
        self.start_far()
        self.start_mate()

    def middle(self):
        me, mate, across, far = places()
        self.one.wait()
        self.held[2] = (self.source[across].astype(F32) + self.held[0].astype(F32)).astype(BF)
        self.cross = push(self.held.at[2], self.held.at[3], self.sems.at[0, 2], self.sems.at[1, 2], across)

    def finish(self):
        me, mate, across, far = places()
        self.two.wait()
        total = self.source[me].astype(F32) + self.held[1].astype(F32)
        self.cross.wait()
        return total + self.held[3].astype(F32)


def norm_parts(stream):
    center = stream - jnp.mean(stream, axis=0, keepdims=True)
    scale_inv = lax.rsqrt(jnp.mean(center * center, axis=0, keepdims=True) + norm_eps)
    return center * scale_inv, scale_inv


def norm_back(unit, scale_inv, scaled):
    return scale_inv * (
        scaled
        - jnp.mean(scaled, axis=0, keepdims=True)
        - unit * jnp.mean(scaled * unit, axis=0, keepdims=True)
    )


def attend_blocks(places_in, block, keys, queries, values, score, write, after):
    rows_k = keys.shape[0]
    row = lax.broadcasted_iota(jnp.int32, (LANES, block), 0)

    def make(n, head):
        query = queries[:, lanes_of(n, block)]
        own = (row < HP) if head == 0 else (row >= HP)
        score[head, :rows_k, :] = mul(keys[...], jnp.where(own, query, jnp.zeros_like(query)), NN)

    def finish(n, head):
        held = score[head, :rows_k, :]
        peak = jnp.max(held, axis=0, keepdims=True)
        shares = jnp.exp2(held - peak).astype(BF)
        mixed = mul(values[head * HP : (head + 1) * HP, :], shares, NN)
        total = mixed[AUX : AUX + 1, :]
        write(n, head, (mixed[:HD] * (1.0 / total)).astype(BF), peak + jnp.log2(total))

    make(places_in[0], 0)
    for step, n in enumerate(places_in):
        make(n, 1)
        finish(n, 0)
        if step + 1 < len(places_in):
            make(places_in[step + 1], 0)
        finish(n, 1)
        after(step, n)


def lanes_of(n, block):
    return pl.ds(n * block if isinstance(n, int) else pl.multiple_of(n * block, LANES), block)


def split_three(value):
    high = value.astype(BF)
    rest = value - high.astype(F32)
    middle = rest.astype(BF)
    return high, middle, (rest - middle.astype(F32)).astype(BF)


def with_rows(body, head, parts):
    row = lax.broadcasted_iota(jnp.int32, body.shape, 0) - head * HP
    out = jnp.where((row >= 0) & (row < HP), body.astype(F32), 0.0)
    for n, part in enumerate(parts):
        out = jnp.where(row == AUX + n, part.astype(F32), out)
    return out.astype(BF)


def back_unit(head, lanes, fresh, side, queries, upstream, grad_q, grad_k, grad_v):
    keys_rows, keys, values_rows = side
    rows_k = keys_rows.shape[0]
    own = slice(head * HP, (head + 1) * HP)
    shares = jnp.exp2(mul(keys_rows[...], queries[head, :, lanes], NN))
    inner = mul(values_rows[...], upstream[head, :, lanes], NN)
    grad_score = (shares * inner).astype(BF)
    shares = shares.astype(BF)
    grad_q[own, lanes] = (mul(keys[own, :], grad_score, NN) * score_scale).astype(BF)
    made_k = mul(queries[head, own, lanes], grad_score, NT)
    made_v = mul(upstream[head, own, lanes], shares, NT)
    grad_k[own, :rows_k] = made_k if fresh else grad_k[own, :rows_k] + made_k
    grad_v[own, :rows_k] = made_v if fresh else grad_v[own, :rows_k] + made_v


def prepare_queries(q, total, query):
    size = q.shape[1]
    for head in range(2):
        query[head, :, :size] = with_rows(q[...], head, split_three(-total[head : head + 1, :]))


def prepare_upstream(part, mixed, upstream, lanes):
    block = part.shape[1]
    for head in range(2):
        rows = slice(head * HD, (head + 1) * HD)
        inner = jnp.sum(part[rows].astype(F32) * mixed[rows].astype(F32), axis=0, keepdims=True)
        padded = jnp.concatenate(
            [part[rows], *split_three(-inner), jnp.zeros((HP - HD - 3, block), BF)], axis=0
        )
        other = jnp.zeros((HP, block), BF)
        both = [padded, other] if head == 0 else [other, padded]
        upstream[head, :, lanes] = jnp.concatenate(both, axis=0)


def back_time(side, kept, totals, back_t, mix_t, ds_t, query, upstream, grad_k, grad_v):
    group, _, block = mix_t.shape
    prepare_queries(kept[0], totals[0], query)
    for g in range(group):
        prepare_upstream(back_t[g], mix_t[g], upstream, lanes_of(g, block))
    for head in range(2):
        back_unit(head, slice(0, group * block), True, side, query, upstream, ds_t, grad_k, grad_v)


def spread_keys(ds, base, source, group, block):
    turned = source.T
    count, width = turned.shape[0] // group, turned.shape[1]
    for g in range(group):
        part = turned[g * count : (g + 1) * count]
        part = jnp.concatenate([part, jnp.zeros((block - count, width), F32)], axis=0)
        ds[base : base + width, g * block : (g + 1) * block] = part.T.astype(BF)


def keep_keys(time_keys, ds, grad_k, grad_v, rows, size, group, block):
    start, stop = rows
    key, value = grad_k[start:stop, :size] * log_two, grad_v[start:stop, :size]
    for base, made in ((LANES, key), (2 * LANES, value)):
        if time_keys:
            spread_keys(ds, base + start, made, group, block)
        else:
            ds[base + start : base + stop, :] = made.astype(BF)


def row_gradients(ds, whole, rows):
    group, _, block = whole.shape
    total = None
    for g in range(group):
        made = mul(ds[rows, g * block : (g + 1) * block], whole[g], NT)
        total = made if total is None else total + made
    return total


def bit_orders(size):
    bits = [1 << n for n in range(size.bit_length() - 1)]
    return bits, bits[1:2] + bits[:1] + bits[2:]


def cut_parts(count, size, parts):
    tile = 16 * size
    parts = min(parts, -(-count // tile))
    rows = -(-count // (tile * parts)) * tile
    return rows * parts, [(n * rows, rows, bit_orders(size)[n % 2]) for n in range(parts)]


def partner_of(bit):
    index = lax.axis_index("dp")
    mine = lax.rem(index // bit, 2)
    return mine, index + bit * (1 - 2 * mine)


def segment_of(part):
    first, rows, bits = part
    for bit in bits:
        rows = rows // 2
        first = first + partner_of(bit)[0] * rows
    return first, rows


def rows_of(first, rows):
    return pl.ds(first if isinstance(first, int) else pl.multiple_of(first, 16), rows)


class Halving:
    def __init__(self, source, stage, target, sems, parts):
        self.source, self.stage, self.target, self.sems = source, stage, target, sems
        self.state = [list(part[:2]) for part in parts]
        self.orders = [part[2] for part in parts]
        self.full = [part[1] for part in parts]
        self.steps, self.at, self.copies = len(self.orders[0]), 0, []

    def start(self):
        self.copies = []
        for n, (first, rows) in enumerate(self.state):
            mine, partner = partner_of(self.orders[n][self.at])
            half = rows // 2
            place = self.held(n)
            self.copies.append(
                push_to(
                    self.source.at[rows_of(first + (1 - mine) * half, half)], self.stage.at[rows_of(place, half)],
                    self.sems.at[0, n, self.at], self.sems.at[1, n, self.at], {"dp": partner},
                )
            )

    def held(self, n):
        total = self.full[n]
        return sum(self.full[:n]) + total - (total >> self.at)

    def finish(self):
        into = self.target if self.at == self.steps - 1 else self.source
        for n, copy in enumerate(self.copies):
            first, rows = self.state[n]
            mine, partner = partner_of(self.orders[n][self.at])
            half = rows // 2
            here, there = rows_of(first + mine * half, half), rows_of(self.held(n), half)
            copy.wait()
            into[here, :] = (self.source[here, :].astype(F32) + self.stage[there, :].astype(F32)).astype(BF)
            self.state[n] = [first + mine * half, half]
        self.at += 1


class Doubling:
    def __init__(self, target, sems, parts):
        self.target, self.sems = target, sems
        self.state = [list(segment_of(part)) for part in parts]
        self.orders = [part[2][::-1] for part in parts]
        self.steps, self.at, self.copies = len(self.orders[0]), 0, []

    def start(self):
        self.copies = []
        for n, (first, rows) in enumerate(self.state):
            mine, partner = partner_of(self.orders[n][self.at])
            here = self.target.at[rows_of(first, rows)]
            self.copies.append(
                push_to(here, here, self.sems.at[0, n, self.at], self.sems.at[1, n, self.at], {"dp": partner})
            )

    def finish(self):
        for n, copy in enumerate(self.copies):
            first, rows = self.state[n]
            mine, partner = partner_of(self.orders[n][self.at])
            copy.wait()
            self.state[n] = [first - mine * rows, 2 * rows]
        self.at += 1


class Direct:
    steps = 2

    def __init__(self, source, stage, target, sems):
        self.source, self.stage, self.target, self.sems, self.at = source, stage, target, sems, 0
        self.size = lax.axis_size("dp")
        self.rows = source.shape[0] // self.size

    def piece(self, index):
        return rows_of(index * self.rows, self.rows)

    def start(self):
        index = lax.axis_index("dp")
        self.copies = []
        for n in range(1, self.size):
            other = lax.rem(index + n, self.size)
            if self.at == 0:
                source, target = self.source.at[self.piece(other)], self.stage.at[n - 1]
            else:
                source = target = self.target.at[self.piece(index)]
            self.copies.append(
                push_to(
                    source, target, self.sems.at[self.at, 0, n - 1], self.sems.at[self.at, 1, n - 1], {"dp": other}
                )
            )

    def finish(self):
        for copy in self.copies:
            copy.wait()
        if self.at == 0:
            here = self.piece(lax.axis_index("dp"))
            total = self.source[here, :].astype(F32)
            for n in range(self.size - 1):
                total = total + self.stage[n].astype(F32)
            self.target[here, :] = total.astype(BF)
        self.at += 1


class Across:
    steps = 1

    def __init__(self, source, target, sems, parts):
        self.source, self.target, self.sems, self.parts, self.at = source, target, sems, parts, 0

    def start(self):
        me, mate, across, far = places()
        self.copies = []
        for n, part in enumerate(self.parts):
            rows = rows_of(*segment_of(part))
            self.copies.append(
                push(self.source.at[rows], self.target.at[rows], self.sems.at[0, n], self.sems.at[1, n], across)
            )

    def finish(self):
        for copy in self.copies:
            copy.wait()
        self.at += 1


def segment_after(part):
    first, rows, bits = part
    for bit in bits[:-1]:
        rows = rows // 2
        first = first + partner_of(bit)[0] * rows
    return first, rows, bits[-1:]


class Chips:
    steps = 1

    def __init__(self, source, held, target, sems, parts):
        self.source, self.held, self.target, self.sems, self.at = source, held, target, sems, 0
        self.parts = parts[: len(parts) // 2]
        self.half = sum(part[1] for part in self.parts)

    def start(self):
        me, mate, across, far = places()
        chip = me // 2
        self.copies = []
        for n, part in enumerate(self.parts):
            first, rows = segment_of(part)
            self.copies.append(
                push(
                    self.source.at[rows_of(first + (1 - chip) * self.half, rows)],
                    self.held.at[n * rows : (n + 1) * rows], self.sems.at[0, n], self.sems.at[1, n], across,
                )
            )

    def finish(self):
        chip = places()[0] // 2
        for n, copy in enumerate(self.copies):
            copy.wait()
            first, rows = segment_of(self.parts[n])
            own = self.source[rows_of(first + chip * self.half, rows), :].astype(F32)
            total = own + self.held[n * rows : (n + 1) * rows].astype(F32)
            self.target[rows_of(first, rows), :] = total.astype(BF)
        self.at += 1


class Relay:
    steps = 1

    def __init__(self, whole, sems, blocks):
        self.whole, self.sems, self.blocks, self.at = whole, sems, blocks, 0

    def start(self):
        me, mate, across, far = places()
        self.copies = [
            push(self.whole.at[block], self.whole.at[block], self.sems.at[0, n], self.sems.at[1, n], mate)
            for n, block in enumerate(self.blocks)
        ]

    def finish(self):
        for copy in self.copies:
            copy.wait()
        self.at += 1


class Chain:
    def __init__(self, *stages):
        self.stages, self.now, self.flying = list(stages), 0, False

    def advance(self):
        if self.now == len(self.stages):
            return
        stage = self.stages[self.now]
        if self.flying:
            stage.finish()
            if stage.at == stage.steps:
                self.now += 1
                self.flying = False
                if self.now == len(self.stages):
                    return
                stage = self.stages[self.now]
        stage.start()
        self.flying = True

    def complete(self):
        while self.now < len(self.stages):
            self.advance()


def picks_of(cross):
    if cross:
        return ((2, 0), (3, 1), (3, 2)), ((3, 0), (2, 1), (2, 2))
    return ((0, 0), (0, 1), (0, 2)), ((1, 0), (1, 1), (1, 2))


def fold_weights(cross, attn_in, small, forward, offsets, backward):
    width = attn_in.shape[3]
    for stream, picks in enumerate(picks_of(cross)):
        blocks = []
        for block, (index, group) in enumerate(picks):
            row = norm_rows[index][group]
            weight = attn_in[index, group]
            folded = weight * small[row : row + 1, :]
            offset = jnp.sum(weight * small[row + 1 : row + 2, :], axis=1, keepdims=True)
            factor = query_scale if group == 0 else 1.0
            ones = (MASK_ROW,) if group == 0 else (AUX, AUX + 1, AUX + 2)
            spare = lax.broadcasted_iota(jnp.int32, (HP - HD, 1), 0) + HD
            marks = jnp.zeros((HP - HD, 1), F32)
            for one in ones:
                marks = jnp.where(spare == one, 1.0, marks)
            for head in range(2):
                rows = slice(head * HD, (head + 1) * HD)
                start = block * LANES + head * HP
                forward[stream, start : start + HD, :] = (folded[rows] * factor).astype(BF)
                forward[stream, start + HD : start + HP, :] = jnp.zeros((HP - HD, width), BF)
                offsets[stream, start : start + HD, :] = offset[rows] * factor
                offsets[stream, start + HD : start + HP, :] = marks
                blocks += [folded[rows], jnp.zeros((HP - HD, width), F32)]
        backward[stream] = jnp.concatenate(blocks, axis=0).T.astype(BF)


def project_time(live, time_all, forward, offsets, kept):
    qt, kt, vt, qf, kf, vf, kt_rows, vt_rows, kf_rows, vf_rows = kept
    group, _, block = time_all.shape
    row = lax.broadcasted_iota(jnp.int32, (LANES, block), 0)
    lane = lax.broadcasted_iota(jnp.int32, (LANES, block), 1)
    dead = jnp.where(lane < live, 0.0, masked_score)
    mask = jnp.where((row == MASK_ROW) | (row == MASK_ROW + HP), dead, 0.0)
    count = kt_rows.shape[0] // group
    for n in range(group):
        made = mul(forward[0], time_all[n], NN) + offsets[0]
        qt[:, n * block : (n + 1) * block] = made[:LANES].astype(BF)
        key, value = (made[LANES : 2 * LANES] + mask).astype(BF), made[2 * LANES :].astype(BF)
        lanes = slice(n * count, (n + 1) * count)
        kt_rows[lanes, :], vt_rows[lanes, :] = key.T[:count], value.T[:count]
    kt[...] = kt_rows[...].T
    vt[...] = vt_rows[...].T


def project_spec(n, spec_all, forward, offsets, bias, kept):
    qt, kt, vt, qf, kf, vf, kt_rows, vt_rows, kf_rows, vf_rows = kept
    block = spec_all.shape[2]
    lanes = lanes_of(n, block)
    row = lax.broadcasted_iota(jnp.int32, (LANES, block), 0)
    made = mul(forward[1], spec_all[n], NN) + offsets[1]
    qf[:, lanes] = made[:LANES].astype(BF)
    mask = jnp.where((row == MASK_ROW) | (row == MASK_ROW + HP), bias[:, lanes], 0.0)
    key, value = (made[LANES : 2 * LANES] + mask).astype(BF), made[2 * LANES :].astype(BF)
    kf[:, lanes], vf[:, lanes] = key, value
    kf_rows[lanes, :], vf_rows[lanes, :] = key.T, value.T


def time_attention(side, kept, totals, mix_t, all_t, sems, score):
    group, _, block = mix_t.shape
    copies = []

    def write(n, head, value, total):
        for g in range(group):
            mix_t[g, head * HD : (head + 1) * HD, :] = value[:, g * block : (g + 1) * block]
        totals[0][head : head + 1, :] = total

    def after(step, n):
        copies.extend(send_blocks(mix_t, all_t, sems))

    attend_blocks((0,), group * block, side[0], kept[0], side[1], score, write, after)
    return copies


def spec_attention(blocks, side, kept, totals, mix_f, all_f, sems, score, first, between):
    block = mix_f.shape[2]
    copies = []

    def write(n, head, value, total):
        mix_f[n, head * HD : (head + 1) * HD, :] = value
        totals[1][head : head + 1, lanes_of(n, block)] = total

    def after(step, n):
        step += first
        if step < 3:
            copies.append(send_block(mix_f, all_f, sems, step, n))
        else:
            all_f[n] = mix_f[n]
        between(step)

    attend_blocks(blocks, block, side[0], kept[3], side[1], score, write, after)
    return copies


def first_kernel(
    live, parts, parts_ffn, traffic, time_in, spec_in, flags, limits, attn_in, attn_out, ffn_in, ffn_out, small,
    time_x, spec_x, time_all, spec_all, mix_t, mix_f, all_t, all_f, *rest,
):
    kept, totals = rest[:10], rest[10:12]
    forward_two, offsets_two, backward, weights, ffn, bias, cols = rest[12:19]
    forward, offsets, rows_t, score, sems_p, sems_q, sems_t, sems_f, sems_a, sems_d, sems_r, sems_s, sems_n = rest[19:]
    me, mate, across, far = places()
    greet((mate, across, far), [partner_of(bit)[1] for bit in parts[0][2]])
    width = ffn_in.shape[0]
    weights[me, :width] = attn_out[...].reshape(width, width).astype(BF)
    if weights.shape[1] > width:
        weights[me, width:] = jnp.zeros_like(weights[me, width:])
    ffn[0, :width] = ffn_in[...].astype(BF)
    ffn[0, width : 2 * width] = ffn_out[...].astype(BF)
    if ffn.shape[1] > 2 * width:
        ffn[0, 2 * width :] = jnp.zeros_like(ffn[0, 2 * width :])
    chain = Chain(
        Across(weights.at[me], weights.at[me], sems_a, parts), Doubling(weights.at[across], sems_d, parts),
        Relay(weights, sems_r, (across,)),
    )
    chain.advance()
    other = Across(ffn.at[0], ffn.at[1], sems_n, parts_ffn)
    other.start()
    rows_t[...] = jnp.zeros_like(rows_t)
    rows_t[:live, :] = time_in[0].astype(F32)
    time_x[...] = rows_t[...].T
    time_all[me] = norm_parts(time_x[...])[0].astype(BF)
    started_t = gather_start((time_all,), sems_p)
    spec_x[...] = spec_in[0].astype(F32).T
    spec_all[me] = norm_parts(spec_x[...])[0].astype(BF)
    started_f = gather_start((spec_all,), sems_q)
    own = Relay(weights, sems_s, (me,))
    own.start()
    traffic.done(time_x, spec_x)
    traffic.ready(0)
    fold_weights(False, attn_in, small, forward, offsets, backward.at[0])
    bins = lax.broadcasted_iota(jnp.int32, bias.shape, 1) // FRAMES
    bias[...] = jnp.where((bins < limits[0]) | (flags[0] == 0), 0.0, masked_score)
    gather_finish((time_all,), sems_p, started_t)
    chain.advance()
    project_time(live, time_all, forward, offsets, kept)
    time_side, spec_side = (kept[6], kept[2]), (kept[8], kept[5])
    copies = time_attention(time_side, kept, totals, mix_t, all_t, sems_t, score)
    project_spec(me, spec_all, forward, offsets, bias, kept)
    chain.advance()
    fold_weights(True, attn_in, small, forward_two, offsets_two, backward.at[1])
    cols[...] = jnp.concatenate(
        [small[...], jnp.zeros((LANES - small.shape[0], small.shape[1]), F32)], axis=0
    ).T
    own.finish()
    other.finish()
    traffic.done(time_all, forward_two, offsets_two, backward, bias, cols)
    gather_finish((spec_all,), sems_q, started_f)
    chain.advance()
    for n in (mate, across, far):
        project_spec(n, spec_all, forward, offsets, bias, kept)
    traffic.done(spec_all, *kept)

    def between(step):
        if step in (0, 1, 2):
            chain.advance()
        if step == 2:
            traffic.done(ffn)

    copies += spec_attention(
        (across, far, mate, me), spec_side, kept, totals, mix_f, all_f, sems_f, score, 0, between
    )
    chain.complete()
    for copy in copies:
        copy.wait()


def whole_weight(weights, index, rows):
    part = weights[:, index * rows : (index + 1) * rows]
    return part.reshape(-1, part.shape[2])


def joined(mixed):
    part = mixed[...]
    return part.reshape(-1, part.shape[2])


def add_branch(mixed, w_out, scale, stream):
    return stream + scale * mul(w_out, mixed, TN)


def second_kernel(
    live, parts_ffn, traffic, time_x, spec_x, in_t, in_f, weights, cols, forward, offsets, bias, ffn,
    time_y, spec_y, time_all, spec_all, mix_t, mix_f, all_t, all_f, *rest,
):
    kept, totals, w_ffn = rest[:10], rest[10:12], rest[12]
    score, sems_p, sems_q, sems_t, sems_f, sems_d, sems_r, sems_s = rest[13:]
    local = in_t.shape[1]
    me, mate, across, far = places()
    greet((mate, across, far), [partner_of(bit)[1] for bit in parts_ffn[0][2]])
    time_y[...] = add_branch(joined(in_t), whole_weight(weights, 0, local), cols[:, 14:15], time_x[...])
    time_all[me] = norm_parts(time_y[...])[0].astype(BF)
    started_t = gather_start((time_all,), sems_p)
    traffic.ready(0)
    for part in parts_ffn:
        rows = rows_of(*segment_of(part))
        w_ffn[across, rows, :] = ffn[1, rows, :]
    chain = Chain(Doubling(w_ffn.at[across], sems_d, parts_ffn), Relay(w_ffn, sems_r, (across,)))
    chain.advance()
    spec_y[...] = add_branch(joined(in_f), whole_weight(weights, 1, local), cols[:, 15:16], spec_x[...])
    spec_all[me] = norm_parts(spec_y[...])[0].astype(BF)
    started_f = gather_start((spec_all,), sems_q)
    traffic.done(time_y, spec_y)
    w_ffn[me] = ffn[0]
    own = Relay(w_ffn, sems_s, (me,))
    own.start()
    traffic.ready(1)
    gather_finish((time_all,), sems_p, started_t)
    project_time(live, time_all, forward, offsets, kept)
    project_spec(me, spec_all, forward, offsets, bias, kept)
    chain.advance()
    own.finish()
    gather_finish((spec_all,), sems_q, started_f)
    chain.advance()
    time_side, spec_side = (kept[6], kept[2]), (kept[8], kept[5])
    copies = []
    for step, n in enumerate((across, far, mate, me)):
        if step < 3:
            project_spec(n, spec_all, forward, offsets, bias, kept)
        copies += spec_attention((n,), time_side, kept, totals, mix_f, all_f, sems_f, score, step, lambda step: None)
    traffic.done(time_all, spec_all, *kept)
    chain.advance()
    copies += time_attention(spec_side, kept, totals, mix_t, all_t, sems_t, score)
    chain.complete()
    for copy in copies:
        copy.wait()


def gelu_pair(values):
    share = 0.5 * (1.0 + lax.erf(values * (2.0**-0.5)))
    slope = share + values * (jnp.exp(-0.5 * values * values) * ((2.0 * math.pi) ** -0.5))
    return values * share, slope


def mixed_gradients(grad_stream, weights, scales, outgoing):
    for n, lanes in enumerate((slice(0, LANES), slice(LANES, None))):
        grad_mix = mul(weights[n], (scales[n] * grad_stream[:, lanes]).astype(BF), NN).astype(BF)
        group, width = outgoing[n].shape[:2]
        for g in range(group):
            outgoing[n][g] = grad_mix[g * width : (g + 1) * width]


def output_gradients(grad_stream, mixed, grads, start):
    for n, lanes in enumerate((slice(0, LANES), slice(LANES, None))):
        grad_out = mul(joined(mixed[n]), grad_stream[:, lanes].astype(BF), NT).astype(BF)
        group, width = mixed[n].shape[:2]
        for g in range(group):
            grads[g, start + n * width : start + (n + 1) * width] = grad_out[g * width : (g + 1) * width]


def third_kernel(
    live, parts_turn, traffic, in_t, in_f, time_x, spec_x, w_out, w_ffn, cols, time_dy, spec_dy,
    time_all, spec_all, backward, mix_t, mix_f, *rest,
):
    kept, totals = rest[:10], rest[10:12]
    result, grad_stream, turn_part, grads_in, grad_norm = rest[12:17]
    (grads, out_t, out_f, back_t, back_f, rows_t, terms_t, terms_f, held_t, held_f, held_core, turn_in, turn_stage, actives,
     grad_hiddens, ds_t, ds_f, query, upstream_ref, grad_k, grad_v, sems_p, sems_q, sems_t, sems_f, sems_c, sems_h) = rest[17:]
    me, mate, across, far = places()
    greet((mate, across, far), [partner_of(bit)[1] for bit in parts_turn[0][2]])
    group, local, block_t = mix_t.shape
    block_f, width = mix_f.shape[2], w_out.shape[2]
    w_first, w_second = w_ffn.at[:, :width], w_ffn.at[:, width : 2 * width]
    gain, shift, scale = cols[:, 12:13], cols[:, 13:14], cols[:, 18:19]
    weights = (whole_weight(w_out, 2, local), whole_weight(w_out, 3, local))
    scales = (cols[:, 16:17], cols[:, 17:18])
    stream = jnp.concatenate(
        [
            add_branch(joined(in_t), weights[0], scales[0], time_x[...]),
            add_branch(joined(in_f), weights[1], scales[1], spec_x[...]),
        ],
        axis=1,
    )
    traffic.ready(0)
    rows_t[...] = jnp.zeros_like(rows_t)
    rows_t[:live, :] = time_dy[0].astype(F32)
    upstream = jnp.concatenate([rows_t[...].T, spec_dy[0].astype(F32).T], axis=1)
    unit, scale_inv = norm_parts(stream)
    normed = (unit * gain + shift).astype(BF)
    grad_branch = (scale * upstream).astype(BF)
    branch = grad_normed = None
    for g in range(group):
        hidden = mul(w_first[g], normed, TN)
        active, slope = gelu_pair(hidden)
        actives[g] = active.astype(BF)
        made = mul(w_second[g], actives[g], TN)
        branch = made if branch is None else branch + made
        grad_hiddens[g] = (mul(w_second[g], grad_branch, NN) * slope).astype(BF)
        made = mul(w_first[g], grad_hiddens[g], NN)
        grad_normed = made if grad_normed is None else grad_normed + made
    value = upstream + norm_back(unit, scale_inv, grad_normed * gain)
    mixed_gradients(value, weights, scales, (out_t, out_f))
    copies_t = send_blocks(out_t, back_t, sems_t)
    copies_f = send_blocks(out_f, back_f, sems_f)
    last = 2 * width + 2 * local
    for g in range(group):
        grads[g, :width] = mul(normed, grad_hiddens[g], NT).astype(BF)
        grads[g, width : 2 * width] = mul(actives[g], grad_branch, NT).astype(BF)
    output_gradients(value, (in_t, in_f), grads, 2 * width)
    sums = jnp.concatenate(
        [
            jnp.sum(item, axis=1, keepdims=True)
            for item in (grad_normed * unit, grad_normed, upstream * branch)
        ] + [jnp.zeros((width, LANES - 3), F32)],
        axis=1,
    ).T[:16].astype(BF)
    for g in range(group):
        grads[g, last : last + 16] = sums if g == 0 else jnp.zeros_like(sums)
    core = lax.rem(me, 2)
    rows_turn, rows_half = grads.shape[1], turn_in.shape[0] // 2
    copies = [
        push(grads.at[2 * n + 1 - core], held_core.at[n], sems_c.at[0, n], sems_c.at[1, n], mate) for n in range(2)
    ]
    result[...] = stream + scale * branch
    grad_stream[...] = value
    traffic.done(result, grad_stream)
    traffic.ready(1)
    for copy in copies_t:
        copy.wait()
    time_side, spec_side = (kept[6], kept[1], kept[7]), (kept[8], kept[4], kept[9])
    back_time(spec_side, kept, totals, back_t, mix_t, ds_t, query, upstream_ref, grad_k, grad_v)
    keep_keys(False, ds_f, grad_k, grad_v, (0, LANES), grad_k.shape[1], group, block_f)
    for n, copy in enumerate(copies):
        copy.wait()
        made = grads[2 * n + core].astype(F32) + held_core[n].astype(F32)
        first = n * rows_half
        turn_in[first : first + rows_turn] = made.astype(BF)
        if rows_half > rows_turn:
            turn_in[first + rows_turn : first + rows_half] = jnp.zeros((rows_half - rows_turn, width), BF)
    halving = Halving(turn_in, turn_stage, turn_in, sems_h, parts_turn)
    halving.start()
    prepare_queries(kept[3], totals[1], query)
    scatter = Scatter(terms_f, held_f, sems_q)
    size_t = kept[6].shape[0]
    for step, n in enumerate((across, far, mate, me)):
        lanes = lanes_of(n, block_f)
        if step < 3:
            copies_f[step].wait()
        prepare_upstream(back_f[n], mix_f[n], upstream_ref, lanes)
        for head in range(2):
            back_unit(head, lanes, step == 0, time_side, query, upstream_ref, ds_f, grad_k, grad_v)
        terms_f[n] = mul(backward[1, 1], ds_f[:, lanes], NN).astype(BF)
        if step == 1:
            scatter.start_far()
        if step == 2:
            scatter.middle()
            scatter.start_mate()
    keep_keys(True, ds_t, grad_k, grad_v, (0, LANES), size_t, group, block_t)
    for g in range(group):
        terms_t[g] = mul(backward[1, 0], ds_t[:, g * block_t : (g + 1) * block_t], NN).astype(BF)
    scatter_t = Scatter(terms_t, held_t, sems_p)
    scatter_t.start()
    halving.finish()
    halving.start()
    scatter_t.middle()
    store_rows(grads_in, ((ds_t, time_all), (ds_f, spec_all)))
    grad_norm[:, :LANES] = scatter_t.finish()
    grad_norm[:, LANES:] = scatter.finish()
    halving.finish()
    while halving.at < halving.steps - 1:
        halving.start()
        halving.finish()
    for n, (first, rows) in enumerate(halving.state):
        turn_part[n * rows : (n + 1) * rows] = turn_in[rows_of(first, rows), :]


def store_rows(target, streams):
    start = 0
    for n, (ds, whole) in enumerate(streams):
        for block in range(3):
            total = row_gradients(ds, whole, slice(block * LANES, (block + 1) * LANES))
            for head in range(2):
                target[start : start + HD] = total[head * HP : head * HP + HD].astype(BF)
                start += HD
        made = row_sums(ds, n)
        sums = made if n == 0 else sums + made
    target[start : start + 16] = sums.astype(BF)


def row_sums(ds, n):
    row = lax.broadcasted_iota(jnp.int32, (16, ds.shape[1]), 0)
    return mul((row == n).astype(BF), ds[...], NT)


def store_head(target, head, ds, whole):
    tiles = whole.shape[1] // LANES
    count = 3 * HD + 16
    for block in range(3):
        base = block * LANES + head * HP
        total = row_gradients(ds, whole, slice(base, base + HP))[:HD].astype(BF)
        for n in range(tiles):
            start = n * count + block * HD
            target[start : start + HD] = total[:, n * LANES : (n + 1) * LANES]
    sums = row_sums(ds, 0).astype(BF)
    for n in range(tiles):
        target[n * count + 3 * HD : (n + 1) * count] = sums[:, n * LANES : (n + 1) * LANES]
    if target.shape[0] > tiles * count:
        target[tiles * count :] = jnp.zeros_like(target[tiles * count :])


def load_head(target, tiles):
    count = 3 * HD + 16
    return jnp.concatenate([target[n * count : (n + 1) * count] for n in range(tiles)], axis=1)


def fourth_kernel(
    parts_turn, parts_in, parts_out, traffic, grad_norm, grad_in, time_y, spec_y, time_x, spec_x, in_t, in_f,
    w_out, cols, time_all, spec_all, backward, mix_t, mix_f, *rest,
):
    kept, totals = rest[:10], rest[10:12]
    turn_part, cross_in, attn_in, attn_out, small = rest[12:17]
    stream_grad, grad_a, grad_b, grad_c, grad_d, packed, scalars = rest[17:24]
    (turn_in, turn_stage, turn_out, turn_far, turn, cross, late_a, late_b, out, cross_one, late_a_one, late_b_one, out_one,
     cross_two, out_two, late_a_two, late_b_two, grads, out_t, out_f, back_t, back_f, terms_t, terms_f, held_t, held_f, held_two,
     ds_t, ds_f, query, upstream_ref, grad_k, grad_v, pieces, sems_q, sems_two, sems_three, sems_t, sems_f, sems_p, sems_y, sems_s,
     sems_turn, sems_cross, sems_a, sems_b, sems_out) = rest[24:]
    me, mate, across, far = places()
    size = lax.axis_size("dp")
    greet((mate, across, far), [lax.rem(lax.axis_index("dp") + n, size) for n in range(1, size)])
    group, local, block_t = mix_t.shape
    block_f, width = mix_f.shape[2], w_out.shape[2]

    def both(first, stage, last, sems, cut):
        return Chain(Halving(first, stage, last, sems.at[0], cut), Doubling(last, sems.at[1], cut))

    rest_parts = [segment_after(part) for part in parts_turn]
    rows = turn_part.shape[0] // len(parts_turn)
    for n, (first, count, _) in enumerate(rest_parts):
        turn_in[rows_of(first, rows), :] = turn_part[n * rows : (n + 1) * rows]
    rows_cross, rows_out = cross_in.shape[0], grads.shape[1]
    cross_one[:rows_cross] = cross_in[...]
    if cross_one.shape[0] > rows_cross:
        cross_one[rows_cross:] = jnp.zeros_like(cross_one[rows_cross:])
    chain_turn = Chain(
        Halving(turn_in, turn_stage, turn_out, sems_s, rest_parts),
        Chips(turn_out, turn_far, turn, sems_y, parts_turn), Doubling(turn, sems_turn, parts_turn[: len(parts_turn) // 2]),
    )
    chain_cross = both(cross_one, cross_two, cross, sems_cross, parts_in)
    chain_out = both(out_one, out_two, out, sems_out, parts_out)
    chain_a = Chain(Direct(late_a_one, late_a_two, late_a, sems_a))
    chain_b = Chain(Direct(late_b_one, late_b_two, late_b, sems_b))
    chain_turn.advance()
    chain_cross.advance()
    unit, scale_inv = norm_parts(jnp.concatenate([time_y[...], spec_y[...]], axis=1))
    value = grad_in[...] + norm_back(unit, scale_inv, grad_norm[...])
    weights = (whole_weight(w_out, 0, local), whole_weight(w_out, 1, local))
    mixed_gradients(value, weights, (cols[:, 14:15], cols[:, 15:16]), (out_t, out_f))
    copies_t = send_blocks(out_t, back_t, sems_t)
    copies_f = send_blocks(out_f, back_f, sems_f)
    output_gradients(value, (in_t, in_f), grads, 0)
    scatter = Scatter(grads, held_two, sems_two)
    scatter.start()
    stream_grad[...] = value
    traffic.ready(0)
    for copy in copies_t:
        copy.wait()
    scatter.middle()
    time_side, spec_side = (kept[6], kept[1], kept[7]), (kept[8], kept[4], kept[9])
    size_t, size_f = kept[6].shape[0], kept[8].shape[0]
    back_time(time_side, kept, totals, back_t, mix_t, ds_t, query, upstream_ref, grad_k, grad_v)
    keep_keys(True, ds_t, grad_k, grad_v, (0, LANES), size_t, group, block_t)
    for g in range(group):
        terms_t[g] = mul(backward[0, 0], ds_t[:, g * block_t : (g + 1) * block_t], NN).astype(BF)
    chain_cross.advance()
    out_one[:rows_out] = scatter.finish().astype(BF)
    store_rows(out_one.at[rows_out:], ((ds_t, time_all),))
    rows_used = rows_out + 6 * HD + 16
    if out_one.shape[0] > rows_used:
        out_one[rows_used:] = jnp.zeros_like(out_one[rows_used:])
    chain_out.advance()
    prepare_queries(kept[3], totals[1], query)
    order = ((me, None), (mate, 2), (across, 0), (far, 1))
    moves = (
        (chain_turn, (0, 2, 4, 6)), (chain_cross, (1, 3, 5, 7)), (chain_out, (1, 3, 5, 7)), (chain_a, (6,)),
    )
    for head in range(2):
        for step, (n, arrival) in enumerate(order):
            lanes = lanes_of(n, block_f)
            if head == 0:
                if arrival is not None:
                    copies_f[arrival].wait()
                prepare_upstream(back_f[n], mix_f[n], upstream_ref, lanes)
            back_unit(head, lanes, step == 0, spec_side, query, upstream_ref, ds_f, grad_k, grad_v)
            for chain, when in moves:
                if head * 4 + step in when:
                    chain.advance()
        keep_keys(False, ds_f, grad_k, grad_v, (head * HP, (head + 1) * HP), size_f, group, block_f)
        if head == 0:
            store_head(late_a_one, 0, ds_f, spec_all)
            chain_a.advance()
    for n in (far, mate, across, me):
        terms_f[n] = mul(backward[0, 1], ds_f[:, lanes_of(n, block_f)], NN).astype(BF)
    scatter_t = Scatter(terms_t, held_t, sems_three)
    scatter = Scatter(terms_f, held_f, sems_q)
    scatter.start()
    scatter_t.start()
    store_head(late_b_one, 1, ds_f, spec_all)
    chain_b.advance()
    scatter.middle()
    scatter_t.middle()
    chains = (chain_turn, chain_cross, chain_out, chain_a)
    for chain in chains:
        chain.advance()
    traffic.ready(1)
    unit, scale_inv = norm_parts(jnp.concatenate([time_x[...], spec_x[...]], axis=1))
    chain_b.advance()
    for chain in chains:
        chain.complete()
    squares = jnp.zeros((1, width), F32)
    packed_rows = [jnp.zeros((1, width), F32) for _ in range(19)]
    tiles = width // LANES

    def add_squares(total, gradient):
        return total + jnp.sum(gradient * gradient, axis=0, keepdims=True)

    def turned(sums):
        return jnp.concatenate([sums, jnp.zeros((LANES - 16, width), F32)], axis=0).T

    def rows_done(squares, pick, plain, sums, lane, block):
        index, group = pick
        column = jnp.concatenate(
            [
                sums[head][block * LANES + head * HP : block * LANES + head * HP + HD, lane : lane + 1]
                for head in range(2)
            ],
            axis=0,
        )
        row = norm_rows[index][group]
        gradient = plain * small[row : row + 1, :] + column * small[row + 1 : row + 2, :]
        grad_a[index, group] = gradient.astype(BF)
        weight = attn_in[index, group]
        packed_rows[row] += jnp.sum(weight * plain, axis=0, keepdims=True)
        packed_rows[row + 1] += jnp.sum(weight * column, axis=0, keepdims=True)
        return add_squares(squares, gradient)

    rows = cross[: 12 * HD + 16].astype(F32)
    sums = (turned(rows[12 * HD :]),) * 2
    for stream, picks in enumerate(picks_of(True)):
        for block, pick in enumerate(picks):
            start = (stream * 6 + block * 2) * HD
            squares = rows_done(squares, pick, rows[start : start + local], sums, stream, block)
    rows = out[rows_out : rows_out + 6 * HD + 16].astype(F32)
    sums = (turned(rows[6 * HD :]),) * 2
    for block, pick in enumerate(picks_of(False)[0]):
        squares = rows_done(squares, pick, rows[block * local : (block + 1) * local], sums, 0, block)
    for index in range(4):
        if index < 2:
            plain = out[index * local : (index + 1) * local].astype(F32)
        else:
            start = 2 * width + (index - 2) * local
            plain = turn[start : start + local].astype(F32)
        gradient = plain * small[14 + index : 15 + index, :]
        grad_b[index] = gradient.astype(BF)
        squares = add_squares(squares, gradient)
        packed_rows[14 + index] += jnp.sum(attn_out[index] * plain, axis=0, keepdims=True)
    for target, start in ((grad_c, 0), (grad_d, width)):
        target[...] = turn[start : start + width]
        squares = add_squares(squares, turn[start : start + width].astype(F32))
    smalls = turn[2 * width + 2 * local : 2 * width + 2 * local + 16].astype(F32)
    for n, row in enumerate((12, 13, 18)):
        packed_rows[row] += smalls[n : n + 1]
    traffic.done(grad_b, grad_c, grad_d)
    chain_b.advance()
    halves = [load_head(late, tiles).astype(F32) for late in (late_a, late_b)]
    sums = [turned(half[3 * HD :]) for half in halves]
    for block, pick in enumerate(picks_of(False)[1]):
        plain = jnp.concatenate([half[block * HD : (block + 1) * HD] for half in halves], axis=0)
        squares = rows_done(squares, pick, plain, sums, 0, block)
    pieces[me] = jnp.concatenate(packed_rows + [squares] + [jnp.zeros((4, width), F32)], axis=0)
    copies = [
        push(pieces.at[me], pieces.at[me], sems_p.at[0, n], sems_p.at[1, n], other)
        for n, other in enumerate((across, far, mate))
    ]
    traffic.done(grad_a)
    scaled = jnp.concatenate([scatter_t.finish(), scatter.finish()], axis=1)
    stream_grad[...] = stream_grad[...] + norm_back(unit, scale_inv, scaled)
    traffic.done(stream_grad)
    for copy in copies:
        copy.wait()
    total = pieces[0]
    for n in range(1, pieces.shape[0]):
        total = total + pieces[n]
    packed[...] = total
    row = lax.broadcasted_iota(jnp.int32, total.shape, 0)
    every = jnp.where(row < 19, total * total, jnp.where(row == 19, total, 0.0))
    norm = jnp.sqrt(jnp.sum(jnp.sum(every, axis=0, keepdims=True), axis=1, keepdims=True))
    factor = jnp.minimum(1.0, clip_level / norm)
    lane = lax.broadcasted_iota(jnp.int32, scalars.shape, 1)
    scalars[...] = jnp.where(lane == 0, norm, factor)


def adam_parts(weight, first_moment, second_moment, gradient, step_rate, decay_rate):
    first_new = beta_first * first_moment + (1.0 - beta_first) * gradient
    second_new = beta_second * second_moment + (1.0 - beta_second) * gradient * gradient
    first_fix = 1.0 - beta_first**STEP
    second_fix = 1.0 - beta_second**STEP
    direction = (first_new * (1.0 / first_fix)) / (jnp.sqrt(second_new * (1.0 / second_fix)) + adam_eps)
    return (weight - step_rate * (direction + decay_rate * weight), first_new, second_new)


def last_kernel(live, traffic, scalars, packed, small, small_m, small_v, result, stream_grad, *refs):
    held, outs = refs[:16], refs[16:28]
    small_outs, (time_out, spec_out, time_grad, spec_grad, shift_gradient, norm) = refs[28:31], refs[31:37]
    sems_out = refs[37]
    rates = (rate_matrix, rate_output, rate_matrix, rate_matrix)
    factor = scalars[:, 1:2]
    gradient = packed[: small.shape[0]] * factor
    made = adam_parts(small[...], small_m[...], small_v[...], gradient, rate_small, 0.0)
    for target, value in zip(small_outs, made):
        target[...] = value
    shift_gradient[...] = gradient[13:14].reshape(-1)
    norm[...] = scalars[:, 0:1]
    leaving = []
    for n, rate in enumerate(rates):
        traffic.ready(n)
        gradient, weight, first_moment, second_moment = held[4 * n : 4 * n + 4]
        rows = weight.shape[0] // 3
        for piece in range(3):
            part = slice(piece * rows, (piece + 1) * rows)
            made = adam_parts(
                weight[part], first_moment[part], second_moment[part], gradient[part].astype(F32) * factor, rate, decay_matrix
            )
            for m, (target, value) in enumerate(zip((weight, first_moment, second_moment), made)):
                target[part] = value
                copy = pltpu.make_async_copy(
                    target.at[part], outs[3 * n + m].at[part], sems_out.at[9 * n + 3 * piece + m]
                )
                copy.start()
                leaving.append(copy)
        if n == 1:
            traffic.ready(4)
            for source, one, two in ((result, time_out, spec_out), (stream_grad, time_grad, spec_grad)):
                one[...] = source[:, :LANES].T[:live].reshape(live, 1, -1)
                two[0] = source[:, LANES:].T
                traffic.done(one, two)
    for copy in leaving:
        copy.wait()


def shards(
    time_in, spec_in, rate_flags, band_limits, time_cot, spec_cot, attn_in, attn_out, ffn_in, ffn_out, small,
    attn_in_m, attn_in_v, attn_out_m, attn_out_v, ffn_in_m, ffn_in_v, ffn_out_m, ffn_out_v, small_m, small_v,
):
    group, size = lax.axis_size("mp"), lax.axis_size("dp")
    live = time_in.shape[1]
    count = -(-live // 16) * 16
    block_t, block_f = LANES, spec_in.shape[1]
    width, local, part = time_in.shape[2], attn_in.shape[2], ffn_in.shape[1]
    lanes = block_t + block_f
    size_t, size_f, rows_t = group * block_t, group * block_f, group * count

    whole = (shape_of((group, width, block_t), BF), shape_of((group, width, block_f), BF))
    stream = (shape_of((width, block_t), F32), shape_of((width, block_f), F32))
    mix = (shape_of((group, local, block_t), BF), shape_of((group, local, block_f), BF))
    kept_shapes = tuple(
        shape_of(s, BF)
        for s in [(LANES, size_t)] + [(LANES, rows_t)] * 2 + [(LANES, size_f)] * 3 + [(rows_t, LANES)] * 2
        + [(size_f, LANES)] * 2
    ) + (shape_of((2, size_t), F32), shape_of((2, size_f), F32))
    packed_weights = (2, 3 * LANES, width)
    score = pltpu.VMEM((2, size_f, max(size_t, block_f)), F32)
    smem = pl.BlockSpec(memory_space=pltpu.SMEM)

    rows_w, parts_w = cut_parts(width, size, 3)
    rows_ffn, parts_ffn = cut_parts(2 * width, size, 6)
    bits = len(parts_w[0][2])
    count_w, count_ffn = len(parts_w), len(parts_ffn)
    one = call(
        functools.partial(first_kernel, live, parts_w, parts_ffn), "first",
        stream + whole + mix + mix + kept_shapes + (
            shape_of(packed_weights, BF), shape_of((2, 3 * LANES, 1), F32), shape_of((2, 2, width, 3 * LANES), BF),
            shape_of((group, rows_w, width), BF), shape_of((2, rows_ffn, width), BF), shape_of((1, size_f), F32),
            shape_of((width, LANES), F32),
        ),
        (time_in, spec_in, rate_flags, band_limits, attn_in, attn_out, ffn_in, ffn_out, small),
        [
            pltpu.VMEM(packed_weights, BF), pltpu.VMEM((2, 3 * LANES, 1), F32), pltpu.VMEM((LANES, width), F32), score,
            dma(6, 1), dma(6, 1), dma(2, 3), dma(2, 3), dma(2, count_w), dma(2, count_w, bits), dma(2, 1), dma(2, 1),
            dma(2, count_ffn),
        ],
        0, specs={2: smem, 3: smem}, late=((4,),),
        early=(0, 1, 2, 3) + tuple(range(8, 18)) + (20, 21, 22, 24, 25, 26),
    )
    (time_x, spec_x, time_all, spec_all, mix_t, mix_f, all_t, all_f), kept = one[:8], one[8:20]
    forward_two, offsets_two, backward, w_out, ffn, bias, cols = one[20:]

    two = call(
        functools.partial(second_kernel, live, parts_ffn), "second",
        stream + whole + mix + mix + kept_shapes + (shape_of((group, rows_ffn, width), BF),),
        (time_x, spec_x, all_t, all_f, w_out, cols, forward_two, offsets_two, bias, ffn),
        [
            score, dma(6, 1), dma(6, 1), dma(2, 3), dma(2, 3), dma(2, count_ffn, bits), dma(2, 1), dma(2, 1),
        ],
        1, late=((9,), (6, 7, 8)), early=(0, 1, 2, 3) + tuple(range(8, 18)),
    )
    (time_y, spec_y, time_all_y, spec_all_y, mix_t_y, mix_f_y, all_t_y, all_f_y), kept_y = two[:8], two[8:20]
    w_ffn = two[20]

    rows_turn, rows_in = width + part + 2 * local + 16, 6 * local + 16
    back_scratch = [
        pltpu.VMEM((3 * LANES, size_t), BF), pltpu.VMEM((3 * LANES, size_f), BF),
        pltpu.VMEM((2, LANES, size_f), BF), pltpu.VMEM((2, LANES, size_f), BF),
        pltpu.VMEM((LANES, size_f), F32), pltpu.VMEM((LANES, size_f), F32),
    ]
    mixes = [pltpu.VMEM(m.shape, BF) for m in mix + mix]
    rows_pair, parts_turn = cut_parts(rows_turn, size, 2)
    parts_turn = parts_turn + [(first + rows_pair, rows, order) for first, rows, order in parts_turn]
    pair = pltpu.VMEM((2 * rows_pair, width), BF)
    terms = [pltpu.VMEM((group, width, block_t), BF), pltpu.VMEM((group, width, block_f), BF)]
    result, grad_stream, turn_part, cross_in, grad_norm = call(
        functools.partial(third_kernel, live, parts_turn), "third",
        (
            shape_of((width, lanes), F32), shape_of((width, lanes), F32), shape_of((4 * rows_pair // size, width), BF),
            shape_of((rows_in, width), BF), shape_of((width, lanes), F32),
        ),
        (
            all_t_y, all_f_y, time_y, spec_y, w_out, w_ffn, cols, time_cot, spec_cot,
            time_all_y, spec_all_y, backward, mix_t_y, mix_f_y,
        ) + tuple(kept_y),
        [pltpu.VMEM((group, rows_turn, width), BF)] + mixes + [pltpu.VMEM((LANES, width), F32)] + terms + terms + [
            pltpu.VMEM((2, rows_turn, width), BF), pair, pair,
            pltpu.VMEM((group, part, lanes), BF), pltpu.VMEM((group, part, lanes), BF),
        ] + back_scratch + [dma(2, 3), dma(2, 3), dma(2, 3), dma(2, 3), dma(2, 2), dma(2, 4, bits)], 2,
        late=((5, 7, 8), tuple(range(9, 26))), early=(0, 1),
    )

    rows_sum, parts_in = cut_parts(rows_in, size, 5)
    rows_out, parts_out = cut_parts(5 * local + 16, size, 4)
    rows_late, _ = cut_parts((width // LANES) * (3 * HD + 16), size, 1)
    sums, late, outs = (
        pltpu.VMEM(shape, BF) for shape in ((rows_sum, width), (rows_late, LANES), (rows_out, width))
    )
    pieces = pltpu.VMEM((size - 1, rows_late // size, LANES), BF)
    stream_grad, grad_a, grad_b, grad_c, grad_d, packed, scalars = call(
        functools.partial(fourth_kernel, parts_turn, parts_in, parts_out), "fourth",
        (
            shape_of((width, lanes), F32), shape_of(attn_in.shape, BF), shape_of(attn_out.shape, BF),
            shape_of(ffn_in.shape, BF), shape_of(ffn_out.shape, BF), shape_of((24, width), F32), shape_of((1, LANES), F32),
        ),
        (
            grad_norm, grad_stream, time_y, spec_y, time_x, spec_x, all_t, all_f, w_out, cols,
            time_all, spec_all, backward, mix_t, mix_f,
        ) + tuple(kept) + (turn_part, cross_in, attn_in, attn_out, small),
        [pair, pair, pair, pltpu.VMEM((rows_pair // size, width), BF), pltpu.VMEM((rows_pair, width), BF)] + [sums, late, late, outs] * 2 + [
            sums, outs, pieces, pieces, pltpu.VMEM((group, 2 * local, width), BF)] + mixes + terms + terms + [pltpu.VMEM((4, 2 * local, width), BF)]
        + back_scratch + [
            pltpu.VMEM((group, 24, width), F32), dma(2, 3), dma(2, 3), dma(2, 3), dma(2, 3), dma(2, 3), dma(2, 3), dma(2, 2), dma(2, 4, 1),
            dma(2, 2, bits), dma(2, 2, 5, bits), dma(2, 2, size - 1), dma(2, 2, size - 1), dma(2, 2, 4, bits),
        ], 3,
        late=(tuple(range(10, 27)), (4, 5, 29, 30, 31)), early=(0, 1, 2, 3, 4),
    )

    ins, outs = [], []
    for gradient, weight, first_moment, second_moment in (
        (grad_a, attn_in, attn_in_m, attn_in_v), (grad_b, attn_out, attn_out_m, attn_out_v),
        (grad_c, ffn_in, ffn_in_m, ffn_in_v), (grad_d, ffn_out, ffn_out_m, ffn_out_v),
    ):
        flat = (weight.size // width, width)
        ins += [value.reshape(flat) for value in (gradient, weight, first_moment, second_moment)]
        outs += [shape_of(flat, F32)] * 3
    outs += [shape_of(small.shape, F32)] * 3
    outs += [shape_of((live, 1, width), F32), shape_of((1, block_f, width), F32)] * 2
    outs += [shape_of((width,), F32), shape_of((1, 1), F32)]
    made = call(
        functools.partial(last_kernel, live), "last", outs, (scalars, packed, small, small_m, small_v, result, stream_grad, *ins),
        [dma(36)], None, late=tuple(tuple(range(7 + 4 * n, 11 + 4 * n)) for n in range(4)) + ((5, 6),),
        early=tuple(range(15, 19)), direct=tuple(range(12)),
    )
    updated = [
        value.reshape(weight.shape)
        for value, weight in zip(made[:15], [w for w in (attn_in, attn_out, ffn_in, ffn_out, small) for _ in range(3)])
    ]
    time_out, spec_out, time_grad, spec_grad, shift_gradient, norm = made[15:]
    time_out, time_grad = (jnp.swapaxes(value, 0, 1) for value in (time_out, time_grad))
    return (time_out, spec_out, time_grad, spec_grad, norm[0, 0], *updated, shift_gradient)


def solution(mesh):
    tokens, copied = P("dp", "mp", None), P()
    a, b, c, d = P(None, None, "mp", None), P(None, "mp", None), P(None, "mp"), P("mp", None)
    return jax.shard_map(
        shards,
        mesh=mesh,
        in_specs=(
            tokens, tokens, P("dp"), P("dp"), tokens, tokens, a, b, c, d, copied,
            a, a, b, b, c, c, d, d, copied, copied,
        ),
        out_specs=(
            tokens, tokens, tokens, tokens, copied,
            a, a, a, b, b, b, c, c, c, d, d, d, copied, copied, copied, copied,
        ),
        check_vma=False,
    )
```

```python
import functools
import math

import jax
import jax.numpy as jnp
from jax import lax
from jax.experimental import pallas as pl
from jax.experimental.pallas import tpu as pltpu
from jax.sharding import PartitionSpec as P

HD = 48
HP = 64
LANES = 128
FRAMES = 256
STEP = 10
BF = jnp.bfloat16
F32 = jnp.float32
NN = ((1,), (0,))
NT = ((1,), (1,))
TN = ((0,), (0,))
MESH = pl.DeviceIdType.MESH

norm_eps = 1e-05
clip_level = 100.0
beta_first = 0.9
beta_second = 0.95
adam_eps = 1e-08
decay_matrix = 0.1
rate_matrix = 0.05
rate_output = 0.5
rate_small = 0.5
masked_score = -1000000000.0
score_scale = HD ** (-0.5)
log_two = math.log(2.0)
query_scale = score_scale / log_two
vmem_limit = 58 * 2**20
AUX = HD
MASK_ROW = HD + 3
norm_rows = ((0, 0, 0), (2, 2, 2), (4, 6, 6), (8, 10, 10))


def mul(left, right, dims):
    return lax.dot_general(left, right, (dims, ((), ())), preferred_element_type=F32)


def dma(*shape):
    return pltpu.SemaphoreType.DMA(shape)


def vmem():
    return pl.BlockSpec(memory_space=pltpu.VMEM)


def shape_of(shape, kind):
    return jax.ShapeDtypeStruct(shape, kind)


class Traffic:
    def __init__(self):
        self.loads, self.stores, self.leaving = [], {}, []

    def ready(self, group):
        for copy in self.loads[group]:
            copy.wait()

    def done(self, *refs):
        for ref in refs:
            copy = self.stores.pop(id(ref))
            copy.start()
            self.leaving.append(copy)

    def finish(self):
        for copy in list(self.stores.values()):
            copy.start()
            self.leaving.append(copy)
        for copy in self.leaving:
            copy.wait()


def call(kernel, name, outs, args, scratch, collective, specs=None, late=(), early=(), direct=()):
    ins, count = len(args), len(args) + len(outs) + len(scratch)
    flat = [n for group in late for n in group]
    extra = [pltpu.VMEM(args[n].shape, args[n].dtype) for n in flat]
    extra += [pltpu.VMEM(outs[n].shape, outs[n].dtype) for n in early]
    extra += [dma(max(len(flat), 1)), dma(max(len(early), 1))]

    def body(*refs):
        refs, held = list(refs[:count]), refs[count:]
        traffic = Traffic()
        place = 0
        for group in late:
            copies = []
            for n in group:
                copies.append(pltpu.make_async_copy(refs[n], held[place], held[-2].at[place]))
                copies[-1].start()
                refs[n] = held[place]
                place += 1
            traffic.loads.append(copies)
        for m, n in enumerate(early):
            ref = held[place + m]
            traffic.stores[id(ref)] = pltpu.make_async_copy(ref, refs[ins + n], held[-1].at[m])
            refs[ins + n] = ref
        kernel(traffic, *refs)
        traffic.finish()

    anywhere = pl.BlockSpec(memory_space=pl.ANY)
    remote = {} if collective is None else {"collective_id": collective, "has_side_effects": True}
    return pl.pallas_call(
        body,
        name=name,
        out_shape=outs,
        in_specs=[anywhere if n in flat else (specs or {}).get(n, vmem()) for n in range(ins)],
        out_specs=tuple(anywhere if n in early or n in direct else vmem() for n in range(len(outs))),
        scratch_shapes=list(scratch) + extra,
        compiler_params=pltpu.CompilerParams(vmem_limit_bytes=vmem_limit, **remote),
    )(*args)


def places():
    me = lax.axis_index("mp")
    mate = me + 1 - 2 * lax.rem(me, 2)
    across = lax.rem(me + 2, 4)
    far = lax.rem(mate + 2, 4)
    return me, mate, across, far


def greet(others, partners=()):
    barrier = pltpu.get_barrier_semaphore()
    for other in others:
        pl.semaphore_signal(barrier, inc=1, device_id={"mp": other}, device_id_type=MESH)
    for partner in partners:
        pl.semaphore_signal(barrier, inc=1, device_id={"dp": partner}, device_id_type=MESH)
    pl.semaphore_wait(barrier, len(others) + len(partners))


def push_to(source, target, send, recv, device):
    copy = pltpu.make_async_remote_copy(
        source, target, send, recv, device_id=device, device_id_type=MESH
    )
    copy.start()
    return copy


def push(source, target, send, recv, device):
    return push_to(source, target, send, recv, {"mp": device})


def gather_start(refs, sems):
    me, mate, across, far = places()
    first = [push(ref.at[me], ref.at[me], sems.at[0, n], sems.at[1, n], across) for n, ref in enumerate(refs)]
    second = [push(ref.at[me], ref.at[me], sems.at[2, n], sems.at[3, n], mate) for n, ref in enumerate(refs)]
    return first, second


def gather_near(started):
    for copy in started[1]:
        copy.wait_recv()


def gather_finish(refs, sems, started, near=False):
    me, mate, across, far = places()
    first, second = started
    third = []
    for n, ref in enumerate(refs):
        first[n].wait_recv()
        third.append(push(ref.at[across], ref.at[across], sems.at[4, n], sems.at[5, n], mate))
    for copy in first:
        copy.wait_send()
    for copy in second:
        copy.wait_send() if near else copy.wait()
    for copy in third:
        copy.wait()


def send_block(source, target, sems, n, other):
    me, mate, across, far = places()
    return push(source.at[other], target.at[me], sems.at[0, n], sems.at[1, n], other)


def send_blocks(source, target, sems):
    me, mate, across, far = places()
    copies = [send_block(source, target, sems, n, other) for n, other in enumerate((across, far, mate))]
    target[me] = source[me]
    return copies


class Scatter:
    def __init__(self, source, held, sems):
        self.source, self.held, self.sems = source, held, sems

    def start_far(self):
        me, mate, across, far = places()
        self.one = push(self.source.at[far], self.held.at[0], self.sems.at[0, 0], self.sems.at[1, 0], mate)

    def start_mate(self):
        me, mate, across, far = places()
        self.two = push(self.source.at[mate], self.held.at[1], self.sems.at[0, 1], self.sems.at[1, 1], mate)

    def start(self):
        self.start_far()
        self.start_mate()

    def middle(self):
        me, mate, across, far = places()
        self.one.wait()
        self.held[2] = (self.source[across].astype(F32) + self.held[0].astype(F32)).astype(BF)
        self.cross = push(self.held.at[2], self.held.at[3], self.sems.at[0, 2], self.sems.at[1, 2], across)

    def finish(self):
        me, mate, across, far = places()
        self.two.wait()
        total = self.source[me].astype(F32) + self.held[1].astype(F32)
        self.cross.wait()
        return total + self.held[3].astype(F32)


def norm_parts(stream):
    center = stream - jnp.mean(stream, axis=0, keepdims=True)
    scale_inv = lax.rsqrt(jnp.mean(center * center, axis=0, keepdims=True) + norm_eps)
    return center * scale_inv, scale_inv


def norm_back(unit, scale_inv, scaled):
    return scale_inv * (
        scaled
        - jnp.mean(scaled, axis=0, keepdims=True)
        - unit * jnp.mean(scaled * unit, axis=0, keepdims=True)
    )


def attend_blocks(
    places_in, block, keys, queries, values, score, write, after, span=None, keep=None, prior=None
):
    first, rows_k = span or (0, keys.shape[0])
    here, there = rows_of(first, rows_k), lanes_from(first, rows_k)
    row = lax.broadcasted_iota(jnp.int32, (LANES, block), 0)

    def make(n, head):
        query = queries[:, lanes_of(n, block)]
        own = (row < HP) if head == 0 else (row >= HP)
        score[head, :rows_k, :] = mul(keys[here, :], jnp.where(own, query, jnp.zeros_like(query)), NN)

    def finish(step, n, head):
        held = score[head, :rows_k, :]
        peak = jnp.max(held, axis=0, keepdims=True)
        shares = jnp.exp2(held - peak).astype(BF)
        mixed = mul(values[head * HP : (head + 1) * HP, there], shares, NN)
        if keep is not None:
            keep(step, head, mixed, peak)
            return
        if prior is not None:
            other, other_peak = prior(step, head)
            new_peak = jnp.maximum(peak, other_peak)
            mixed = mixed * jnp.exp2(peak - new_peak) + other * jnp.exp2(other_peak - new_peak)
            peak = new_peak
        total = mixed[AUX : AUX + 1, :]
        write(n, head, (mixed[:HD] * (1.0 / total)).astype(BF), peak + jnp.log2(total))

    make(places_in[0], 0)
    for step, n in enumerate(places_in):
        make(n, 1)
        finish(step, n, 0)
        if step + 1 < len(places_in):
            make(places_in[step + 1], 0)
        finish(step, n, 1)
        after(step, n)


def lanes_from(first, count):
    return pl.ds(first if isinstance(first, int) else pl.multiple_of(first, LANES), count)


def lanes_of(n, block):
    return pl.ds(n * block if isinstance(n, int) else pl.multiple_of(n * block, LANES), block)


def split_three(value):
    high = value.astype(BF)
    rest = value - high.astype(F32)
    middle = rest.astype(BF)
    return high, middle, (rest - middle.astype(F32)).astype(BF)


def with_rows(body, head, parts):
    row = lax.broadcasted_iota(jnp.int32, body.shape, 0) - head * HP
    out = jnp.where((row >= 0) & (row < HP), body.astype(F32), 0.0)
    for n, part in enumerate(parts):
        out = jnp.where(row == AUX + n, part.astype(F32), out)
    return out.astype(BF)


def back_unit(head, lanes, fresh, side, queries, upstream, grad_q, grad_k, grad_v):
    keys_rows, keys, values_rows = side
    rows_k = keys_rows.shape[0]
    own = slice(head * HP, (head + 1) * HP)
    shares = jnp.exp2(mul(keys_rows[...], queries[head, :, lanes], NN))
    inner = mul(values_rows[...], upstream[head, :, lanes], NN)
    grad_score = (shares * inner).astype(BF)
    shares = shares.astype(BF)
    grad_q[own, lanes] = (mul(keys[own, :], grad_score, NN) * score_scale).astype(BF)
    made_k = mul(queries[head, own, lanes], grad_score, NT)
    made_v = mul(upstream[head, own, lanes], shares, NT)
    grad_k[own, :rows_k] = made_k if fresh else grad_k[own, :rows_k] + made_k
    grad_v[own, :rows_k] = made_v if fresh else grad_v[own, :rows_k] + made_v


def prepare_queries(q, total, query):
    size = q.shape[1]
    for head in range(2):
        query[head, :, :size] = with_rows(q[...], head, split_three(-total[head : head + 1, :]))


def prepare_upstream(part, mixed, upstream, lanes):
    block = part.shape[1]
    for head in range(2):
        rows = slice(head * HD, (head + 1) * HD)
        inner = jnp.sum(part[rows].astype(F32) * mixed[rows].astype(F32), axis=0, keepdims=True)
        padded = jnp.concatenate(
            [part[rows], *split_three(-inner), jnp.zeros((HP - HD - 3, block), BF)], axis=0
        )
        other = jnp.zeros((HP, block), BF)
        both = [padded, other] if head == 0 else [other, padded]
        upstream[head, :, lanes] = jnp.concatenate(both, axis=0)


def back_time(side, kept, totals, back_t, mix_t, ds_t, query, upstream, grad_k, grad_v):
    group, _, block = mix_t.shape
    prepare_queries(kept[0], totals[0], query)
    for g in range(group):
        prepare_upstream(back_t[g], mix_t[g], upstream, lanes_of(g, block))
    for head in range(2):
        back_unit(head, slice(0, group * block), True, side, query, upstream, ds_t, grad_k, grad_v)


def spread_keys(ds, base, source, group, block):
    turned = source.T
    count, width = turned.shape[0] // group, turned.shape[1]
    for g in range(group):
        part = turned[g * count : (g + 1) * count]
        part = jnp.concatenate([part, jnp.zeros((block - count, width), F32)], axis=0)
        ds[base : base + width, g * block : (g + 1) * block] = part.T.astype(BF)


def keep_keys(time_keys, ds, grad_k, grad_v, rows, size, group, block):
    start, stop = rows
    key, value = grad_k[start:stop, :size] * log_two, grad_v[start:stop, :size]
    for base, made in ((LANES, key), (2 * LANES, value)):
        if time_keys:
            spread_keys(ds, base + start, made, group, block)
        else:
            ds[base + start : base + stop, :] = made.astype(BF)


def row_gradients(ds, whole, rows):
    group, _, block = whole.shape
    total = None
    for g in range(group):
        made = mul(ds[rows, g * block : (g + 1) * block], whole[g], NT)
        total = made if total is None else total + made
    return total


def bit_orders(size):
    bits = [1 << n for n in range(size.bit_length() - 1)]
    return bits, bits[1:2] + bits[:1] + bits[2:]


def cut_parts(count, size, parts):
    tile = 16 * size
    parts = min(parts, -(-count // tile))
    rows = -(-count // (tile * parts)) * tile
    return rows * parts, [(n * rows, rows, bit_orders(size)[n % 2]) for n in range(parts)]


def partner_of(bit):
    index = lax.axis_index("dp")
    mine = lax.rem(index // bit, 2)
    return mine, index + bit * (1 - 2 * mine)


def segment_of(part):
    first, rows, bits = part
    for bit in bits:
        rows = rows // 2
        first = first + partner_of(bit)[0] * rows
    return first, rows


def rows_of(first, rows):
    return pl.ds(first if isinstance(first, int) else pl.multiple_of(first, 16), rows)


class Halving:
    def __init__(self, source, stage, target, sems, parts):
        self.source, self.stage, self.target, self.sems = source, stage, target, sems
        self.state = [list(part[:2]) for part in parts]
        self.orders = [part[2] for part in parts]
        self.full = [part[1] for part in parts]
        self.steps, self.at, self.copies = len(self.orders[0]), 0, []

    def start(self):
        self.copies = []
        for n, (first, rows) in enumerate(self.state):
            mine, partner = partner_of(self.orders[n][self.at])
            half = rows // 2
            place = self.held(n)
            self.copies.append(
                push_to(
                    self.source.at[rows_of(first + (1 - mine) * half, half)], self.stage.at[rows_of(place, half)],
                    self.sems.at[0, n, self.at], self.sems.at[1, n, self.at], {"dp": partner},
                )
            )

    def held(self, n):
        total = self.full[n]
        return sum(self.full[:n]) + total - (total >> self.at)

    def finish(self):
        into = self.target if self.at == self.steps - 1 else self.source
        for n, copy in enumerate(self.copies):
            first, rows = self.state[n]
            mine, partner = partner_of(self.orders[n][self.at])
            half = rows // 2
            here, there = rows_of(first + mine * half, half), rows_of(self.held(n), half)
            copy.wait()
            into[here, :] = (self.source[here, :].astype(F32) + self.stage[there, :].astype(F32)).astype(BF)
            self.state[n] = [first + mine * half, half]
        self.at += 1


class Doubling:
    def __init__(self, target, sems, parts):
        self.target, self.sems = target, sems
        self.state = [list(segment_of(part)) for part in parts]
        self.orders = [part[2][::-1] for part in parts]
        self.steps, self.at, self.copies = len(self.orders[0]), 0, []

    def start(self):
        self.copies = []
        for n, (first, rows) in enumerate(self.state):
            mine, partner = partner_of(self.orders[n][self.at])
            here = self.target.at[rows_of(first, rows)]
            self.copies.append(
                push_to(here, here, self.sems.at[0, n, self.at], self.sems.at[1, n, self.at], {"dp": partner})
            )

    def finish(self):
        for n, copy in enumerate(self.copies):
            first, rows = self.state[n]
            mine, partner = partner_of(self.orders[n][self.at])
            copy.wait()
            self.state[n] = [first - mine * rows, 2 * rows]
        self.at += 1


class Direct:
    steps = 2

    def __init__(self, source, stage, target, sems):
        self.source, self.stage, self.target, self.sems, self.at = source, stage, target, sems, 0
        self.size = lax.axis_size("dp")
        self.rows = source.shape[0] // self.size

    def piece(self, index):
        return rows_of(index * self.rows, self.rows)

    def start(self):
        index = lax.axis_index("dp")
        self.copies = []
        for n in range(1, self.size):
            other = lax.rem(index + n, self.size)
            if self.at == 0:
                source, target = self.source.at[self.piece(other)], self.stage.at[n - 1]
            else:
                source = target = self.target.at[self.piece(index)]
            self.copies.append(
                push_to(
                    source, target, self.sems.at[self.at, 0, n - 1], self.sems.at[self.at, 1, n - 1], {"dp": other}
                )
            )

    def finish(self):
        for copy in self.copies:
            copy.wait()
        if self.at == 0:
            here = self.piece(lax.axis_index("dp"))
            total = self.source[here, :].astype(F32)
            for n in range(self.size - 1):
                total = total + self.stage[n].astype(F32)
            self.target[here, :] = total.astype(BF)
        self.at += 1


class Across:
    steps = 1

    def __init__(self, source, target, sems, parts):
        self.source, self.target, self.sems, self.parts, self.at = source, target, sems, parts, 0

    def start(self):
        me, mate, across, far = places()
        self.copies = []
        for n, part in enumerate(self.parts):
            rows = rows_of(*segment_of(part))
            self.copies.append(
                push(self.source.at[rows], self.target.at[rows], self.sems.at[0, n], self.sems.at[1, n], across)
            )

    def finish(self):
        for copy in self.copies:
            copy.wait()
        self.at += 1


def segment_after(part):
    first, rows, bits = part
    for bit in bits[:-1]:
        rows = rows // 2
        first = first + partner_of(bit)[0] * rows
    return first, rows, bits[-1:]


class Chips:
    steps = 1

    def __init__(self, source, held, target, sems, parts):
        self.source, self.held, self.target, self.sems, self.at = source, held, target, sems, 0
        self.parts = parts[: len(parts) // 2]
        self.half = sum(part[1] for part in self.parts)

    def start(self):
        me, mate, across, far = places()
        chip = me // 2
        self.copies = []
        for n, part in enumerate(self.parts):
            first, rows = segment_of(part)
            self.copies.append(
                push(
                    self.source.at[rows_of(first + (1 - chip) * self.half, rows)],
                    self.held.at[n * rows : (n + 1) * rows], self.sems.at[0, n], self.sems.at[1, n], across,
                )
            )

    def finish(self):
        chip = places()[0] // 2
        for n, copy in enumerate(self.copies):
            copy.wait()
            first, rows = segment_of(self.parts[n])
            own = self.source[rows_of(first + chip * self.half, rows), :].astype(F32)
            total = own + self.held[n * rows : (n + 1) * rows].astype(F32)
            self.target[rows_of(first, rows), :] = total.astype(BF)
        self.at += 1


class Relay:
    steps = 1

    def __init__(self, whole, sems, blocks):
        self.whole, self.sems, self.blocks, self.at = whole, sems, blocks, 0

    def start(self):
        me, mate, across, far = places()
        self.copies = [
            push(self.whole.at[block], self.whole.at[block], self.sems.at[0, n], self.sems.at[1, n], mate)
            for n, block in enumerate(self.blocks)
        ]

    def finish(self):
        for copy in self.copies:
            copy.wait()
        self.at += 1


class Chain:
    def __init__(self, *stages):
        self.stages, self.now, self.flying = list(stages), 0, False

    def advance(self):
        if self.now == len(self.stages):
            return
        stage = self.stages[self.now]
        if self.flying:
            stage.finish()
            if stage.at == stage.steps:
                self.now += 1
                self.flying = False
                if self.now == len(self.stages):
                    return
                stage = self.stages[self.now]
        stage.start()
        self.flying = True

    def complete(self):
        while self.now < len(self.stages):
            self.advance()


def picks_of(cross):
    if cross:
        return ((2, 0), (3, 1), (3, 2)), ((3, 0), (2, 1), (2, 2))
    return ((0, 0), (0, 1), (0, 2)), ((1, 0), (1, 1), (1, 2))


def fold_weights(cross, attn_in, small, forward, offsets, backward):
    width = attn_in.shape[3]
    for stream, picks in enumerate(picks_of(cross)):
        blocks = []
        for block, (index, group) in enumerate(picks):
            row = norm_rows[index][group]
            weight = attn_in[index, group]
            folded = weight * small[row : row + 1, :]
            offset = jnp.sum(weight * small[row + 1 : row + 2, :], axis=1, keepdims=True)
            factor = query_scale if group == 0 else 1.0
            ones = (MASK_ROW,) if group == 0 else (AUX, AUX + 1, AUX + 2)
            spare = lax.broadcasted_iota(jnp.int32, (HP - HD, 1), 0) + HD
            marks = jnp.zeros((HP - HD, 1), F32)
            for one in ones:
                marks = jnp.where(spare == one, 1.0, marks)
            for head in range(2):
                rows = slice(head * HD, (head + 1) * HD)
                start = block * LANES + head * HP
                forward[stream, start : start + HD, :] = (folded[rows] * factor).astype(BF)
                forward[stream, start + HD : start + HP, :] = jnp.zeros((HP - HD, width), BF)
                offsets[stream, start : start + HD, :] = offset[rows] * factor
                offsets[stream, start + HD : start + HP, :] = marks
                blocks += [folded[rows], jnp.zeros((HP - HD, width), F32)]
        backward[stream] = jnp.concatenate(blocks, axis=0).T.astype(BF)


def project_time(live, time_all, forward, offsets, kept):
    qt, kt, vt, qf, kf, vf, kt_rows, vt_rows, kf_rows, vf_rows = kept
    group, _, block = time_all.shape
    row = lax.broadcasted_iota(jnp.int32, (LANES, block), 0)
    lane = lax.broadcasted_iota(jnp.int32, (LANES, block), 1)
    dead = jnp.where(lane < live, 0.0, masked_score)
    mask = jnp.where((row == MASK_ROW) | (row == MASK_ROW + HP), dead, 0.0)
    count = kt_rows.shape[0] // group
    for n in range(group):
        made = mul(forward[0], time_all[n], NN) + offsets[0]
        qt[:, n * block : (n + 1) * block] = made[:LANES].astype(BF)
        key, value = (made[LANES : 2 * LANES] + mask).astype(BF), made[2 * LANES :].astype(BF)
        lanes = slice(n * count, (n + 1) * count)
        kt_rows[lanes, :], vt_rows[lanes, :] = key.T[:count], value.T[:count]
    kt[...] = kt_rows[...].T
    vt[...] = vt_rows[...].T


def project_spec(n, spec_all, forward, offsets, bias, kept):
    qt, kt, vt, qf, kf, vf, kt_rows, vt_rows, kf_rows, vf_rows = kept
    block = spec_all.shape[2]
    lanes = lanes_of(n, block)
    row = lax.broadcasted_iota(jnp.int32, (LANES, block), 0)
    made = mul(forward[1], spec_all[n], NN) + offsets[1]
    qf[:, lanes] = made[:LANES].astype(BF)
    mask = jnp.where((row == MASK_ROW) | (row == MASK_ROW + HP), bias[:, lanes], 0.0)
    key, value = (made[LANES : 2 * LANES] + mask).astype(BF), made[2 * LANES :].astype(BF)
    kf[:, lanes], vf[:, lanes] = key, value
    kf_rows[lanes, :], vf_rows[lanes, :] = key.T, value.T


def time_attention(side, kept, totals, mix_t, all_t, sems, score):
    group, _, block = mix_t.shape
    copies = []

    def write(n, head, value, total):
        for g in range(group):
            mix_t[g, head * HD : (head + 1) * HD, :] = value[:, g * block : (g + 1) * block]
        totals[0][head : head + 1, :] = total

    def after(step, n):
        copies.extend(send_blocks(mix_t, all_t, sems))

    attend_blocks((0,), group * block, side[0], kept[0], side[1], score, write, after)
    return copies


def spec_attention(blocks, side, kept, totals, mix_f, all_f, sems, score, first, between, **part):
    block = mix_f.shape[2]
    copies = []

    def write(n, head, value, total):
        mix_f[n, head * HD : (head + 1) * HD, :] = value
        totals[1][head : head + 1, lanes_of(n, block)] = total

    def after(step, n):
        step += first
        if step < 3:
            copies.append(send_block(mix_f, all_f, sems, step, n))
        else:
            all_f[n] = mix_f[n]
        between(step)

    attend_blocks(blocks, block, side[0], kept[3], side[1], score, write, after, **part)
    return copies


def forward_kernel(
    live, parts, parts_ffn, traffic, time_in, spec_in, flags, limits, attn_in, attn_out, ffn_in, ffn_out, small,
    time_x, spec_x, time_all, spec_all, mix_t, mix_f, all_t, all_f, *rest,
):
    kept, totals = rest[:10], rest[10:12]
    time_y, spec_y, time_all_y, spec_all_y, mix_t_y, mix_f_y, all_t_y, all_f_y = rest[12:20]
    kept_y, totals_y = rest[20:30], rest[30:32]
    backward, weights, w_ffn, cols = rest[32:36]
    (forward, offsets, forward_two, offsets_two, bias, rows_t, score, part_mix, part_peak, sems_p, sems_q, sems_t, sems_f, sems_a, sems_d,
     sems_r, sems_s, sems_n, sems_p_two, sems_q_two, sems_t_two, sems_f_two, sems_m, sems_u, sems_v) = rest[36:]
    me, mate, across, far = places()
    greet((mate, across, far), [partner_of(bit)[1] for bit in parts[0][2]])
    width, local = ffn_in.shape[0], mix_t.shape[1]
    weights[me, :width] = attn_out[...].reshape(width, width).astype(BF)
    if weights.shape[1] > width:
        weights[me, width:] = jnp.zeros_like(weights[me, width:])
    w_ffn[me, :width] = ffn_in[...].astype(BF)
    w_ffn[me, width : 2 * width] = ffn_out[...].astype(BF)
    if w_ffn.shape[1] > 2 * width:
        w_ffn[me, 2 * width :] = jnp.zeros_like(w_ffn[me, 2 * width :])
    chain = Chain(
        Across(weights.at[me], weights.at[me], sems_a, parts), Doubling(weights.at[across], sems_d, parts),
        Relay(weights, sems_r, (across,)),
    )
    chain.advance()
    chain_ffn = Chain(
        Across(w_ffn.at[me], w_ffn.at[me], sems_n, parts_ffn), Doubling(w_ffn.at[across], sems_m, parts_ffn),
        Relay(w_ffn, sems_u, (across,)),
    )
    chain_ffn.advance()
    rows_t[...] = jnp.zeros_like(rows_t)
    rows_t[:live, :] = time_in[0].astype(F32)
    time_x[...] = rows_t[...].T
    time_all[me] = norm_parts(time_x[...])[0].astype(BF)
    started_t = gather_start((time_all,), sems_p)
    spec_x[...] = spec_in[0].astype(F32).T
    spec_all[me] = norm_parts(spec_x[...])[0].astype(BF)
    started_f = gather_start((spec_all,), sems_q)
    own = Relay(weights, sems_s, (me,))
    own.start()
    own_ffn = Relay(w_ffn, sems_v, (me,))
    own_ffn.start()
    traffic.done(time_x, spec_x)
    traffic.ready(0)
    fold_weights(False, attn_in, small, forward, offsets, backward.at[0])
    bins = lax.broadcasted_iota(jnp.int32, bias.shape, 1) // FRAMES
    bias[...] = jnp.where((bins < limits[0]) | (flags[0] == 0), 0.0, masked_score)
    gather_finish((time_all,), sems_p, started_t)
    chain.advance()
    project_time(live, time_all, forward, offsets, kept)
    time_side, spec_side = (kept[6], kept[2]), (kept[8], kept[5])
    copies = time_attention(time_side, kept, totals, mix_t, all_t, sems_t, score)
    project_spec(me, spec_all, forward, offsets, bias, kept)
    chain.advance()
    fold_weights(True, attn_in, small, forward_two, offsets_two, backward.at[1])
    cols[...] = jnp.concatenate(
        [small[...], jnp.zeros((LANES - small.shape[0], small.shape[1]), F32)], axis=0
    ).T
    own.finish()
    own_ffn.finish()
    traffic.done(time_all, backward, cols)
    gather_near(started_f)
    project_spec(mate, spec_all, forward, offsets, bias, kept)
    block_f = mix_f.shape[2]
    chip, half = me // 2, 2 * block_f

    def keep(step, head, value, peak):
        part_mix[step, head] = value
        part_peak[step, head : head + 1] = peak

    def prior(step, head):
        return part_mix[step, head], part_peak[step, head : head + 1]

    attend_blocks(
        (mate, me), block_f, spec_side[0], kept[3], spec_side[1], score, None, lambda step, n: None,
        span=(chip * half, half), keep=keep,
    )
    gather_finish((spec_all,), sems_q, started_f, near=True)
    chain.advance()
    for n in (across, far):
        project_spec(n, spec_all, forward, offsets, bias, kept)
    traffic.done(spec_all, *kept)

    def between(step):
        if step in (0, 1, 2):
            chain.advance()
        if step == 2:
            chain_ffn.advance()

    copies += spec_attention((across, far), spec_side, kept, totals, mix_f, all_f, sems_f, score, 0, between)
    copies += spec_attention(
        (mate, me), spec_side, kept, totals, mix_f, all_f, sems_f, score, 2, between,
        span=((1 - chip) * half, half), prior=prior,
    )
    chain.complete()
    for copy in copies:
        copy.wait()
    traffic.done(mix_t, mix_f, all_t, all_f, *totals, weights)
    kept, totals = kept_y, totals_y
    time_y[...] = add_branch(joined(all_t), whole_weight(weights, 0, local), cols[:, 14:15], time_x[...])
    time_all_y[me] = norm_parts(time_y[...])[0].astype(BF)
    started_t = gather_start((time_all_y,), sems_p_two)
    spec_y[...] = add_branch(joined(all_f), whole_weight(weights, 1, local), cols[:, 15:16], spec_x[...])
    spec_all_y[me] = norm_parts(spec_y[...])[0].astype(BF)
    started_f = gather_start((spec_all_y,), sems_q_two)
    traffic.done(time_y, spec_y)
    chain_ffn.advance()
    gather_finish((time_all_y,), sems_p_two, started_t)
    project_time(live, time_all_y, forward_two, offsets_two, kept)
    project_spec(me, spec_all_y, forward_two, offsets_two, bias, kept)
    gather_finish((spec_all_y,), sems_q_two, started_f)
    chain_ffn.advance()
    time_side, spec_side = (kept[6], kept[2]), (kept[8], kept[5])
    copies = []
    for step, n in enumerate((across, far, mate, me)):
        if step < 3:
            project_spec(n, spec_all_y, forward_two, offsets_two, bias, kept)
        copies += spec_attention(
            (n,), time_side, kept, totals, mix_f_y, all_f_y, sems_f_two, score, step, lambda step: None
        )
    traffic.done(time_all_y, spec_all_y, *kept)
    chain_ffn.advance()
    copies += time_attention(spec_side, kept, totals, mix_t_y, all_t_y, sems_t_two, score)
    chain_ffn.complete()
    for copy in copies:
        copy.wait()


def whole_weight(weights, index, rows):
    part = weights[:, index * rows : (index + 1) * rows]
    return part.reshape(-1, part.shape[2])


def joined(mixed):
    part = mixed[...]
    return part.reshape(-1, part.shape[2])


def add_branch(mixed, w_out, scale, stream):
    return stream + scale * mul(w_out, mixed, TN)


def gelu_pair(values):
    share = 0.5 * (1.0 + lax.erf(values * (2.0**-0.5)))
    slope = share + values * (jnp.exp(-0.5 * values * values) * ((2.0 * math.pi) ** -0.5))
    return values * share, slope


def mixed_gradients(grad_stream, weights, scales, outgoing):
    for n, lanes in enumerate((slice(0, LANES), slice(LANES, None))):
        grad_mix = mul(weights[n], (scales[n] * grad_stream[:, lanes]).astype(BF), NN).astype(BF)
        group, width = outgoing[n].shape[:2]
        for g in range(group):
            outgoing[n][g] = grad_mix[g * width : (g + 1) * width]


def output_gradients(grad_stream, mixed, grads, start):
    for n, lanes in enumerate((slice(0, LANES), slice(LANES, None))):
        grad_out = mul(joined(mixed[n]), grad_stream[:, lanes].astype(BF), NT).astype(BF)
        group, width = mixed[n].shape[:2]
        for g in range(group):
            grads[g, start + n * width : start + (n + 1) * width] = grad_out[g * width : (g + 1) * width]


def third_kernel(
    live, parts_turn, traffic, in_t, in_f, time_x, spec_x, w_out, w_ffn, cols, time_dy, spec_dy,
    time_all, spec_all, backward, mix_t, mix_f, *rest,
):
    kept, totals = rest[:10], rest[10:12]
    result, grad_stream, turn_part, grads_in, grad_norm = rest[12:17]
    (grads, out_t, out_f, back_t, back_f, rows_t, terms_t, terms_f, held_t, held_f, held_core, turn_in, turn_stage, actives,
     grad_hiddens, ds_t, ds_f, query, upstream_ref, grad_k, grad_v, sems_p, sems_q, sems_t, sems_f, sems_c, sems_h) = rest[17:]
    me, mate, across, far = places()
    greet((mate, across, far), [partner_of(bit)[1] for bit in parts_turn[0][2]])
    group, local, block_t = mix_t.shape
    block_f, width = mix_f.shape[2], w_out.shape[2]
    w_first, w_second = w_ffn.at[:, :width], w_ffn.at[:, width : 2 * width]
    gain, shift, scale = cols[:, 12:13], cols[:, 13:14], cols[:, 18:19]
    weights = (whole_weight(w_out, 2, local), whole_weight(w_out, 3, local))
    scales = (cols[:, 16:17], cols[:, 17:18])
    stream = jnp.concatenate(
        [
            add_branch(joined(in_t), weights[0], scales[0], time_x[...]),
            add_branch(joined(in_f), weights[1], scales[1], spec_x[...]),
        ],
        axis=1,
    )
    traffic.ready(0)
    rows_t[...] = jnp.zeros_like(rows_t)
    rows_t[:live, :] = time_dy[0].astype(F32)
    upstream = jnp.concatenate([rows_t[...].T, spec_dy[0].astype(F32).T], axis=1)
    unit, scale_inv = norm_parts(stream)
    normed = (unit * gain + shift).astype(BF)
    grad_branch = (scale * upstream).astype(BF)
    branch = grad_normed = None
    for g in range(group):
        hidden = mul(w_first[g], normed, TN)
        active, slope = gelu_pair(hidden)
        actives[g] = active.astype(BF)
        made = mul(w_second[g], actives[g], TN)
        branch = made if branch is None else branch + made
        grad_hiddens[g] = (mul(w_second[g], grad_branch, NN) * slope).astype(BF)
        made = mul(w_first[g], grad_hiddens[g], NN)
        grad_normed = made if grad_normed is None else grad_normed + made
    value = upstream + norm_back(unit, scale_inv, grad_normed * gain)
    mixed_gradients(value, weights, scales, (out_t, out_f))
    copies_t = send_blocks(out_t, back_t, sems_t)
    copies_f = send_blocks(out_f, back_f, sems_f)
    last = 2 * width + 2 * local
    for g in range(group):
        grads[g, :width] = mul(normed, grad_hiddens[g], NT).astype(BF)
        grads[g, width : 2 * width] = mul(actives[g], grad_branch, NT).astype(BF)
    output_gradients(value, (in_t, in_f), grads, 2 * width)
    sums = jnp.concatenate(
        [
            jnp.sum(item, axis=1, keepdims=True)
            for item in (grad_normed * unit, grad_normed, upstream * branch)
        ] + [jnp.zeros((width, LANES - 3), F32)],
        axis=1,
    ).T[:16].astype(BF)
    for g in range(group):
        grads[g, last : last + 16] = sums if g == 0 else jnp.zeros_like(sums)
    core = lax.rem(me, 2)
    rows_turn, rows_half = grads.shape[1], turn_in.shape[0] // 2
    copies = [
        push(grads.at[2 * n + 1 - core], held_core.at[n], sems_c.at[0, n], sems_c.at[1, n], mate) for n in range(2)
    ]
    result[...] = stream + scale * branch
    grad_stream[...] = value
    traffic.done(result, grad_stream)
    traffic.ready(1)
    for copy in copies_t:
        copy.wait()
    time_side, spec_side = (kept[6], kept[1], kept[7]), (kept[8], kept[4], kept[9])
    back_time(spec_side, kept, totals, back_t, mix_t, ds_t, query, upstream_ref, grad_k, grad_v)
    keep_keys(False, ds_f, grad_k, grad_v, (0, LANES), grad_k.shape[1], group, block_f)
    for n, copy in enumerate(copies):
        copy.wait()
        made = grads[2 * n + core].astype(F32) + held_core[n].astype(F32)
        first = n * rows_half
        turn_in[first : first + rows_turn] = made.astype(BF)
        if rows_half > rows_turn:
            turn_in[first + rows_turn : first + rows_half] = jnp.zeros((rows_half - rows_turn, width), BF)
    halving = Halving(turn_in, turn_stage, turn_in, sems_h, parts_turn)
    halving.start()
    prepare_queries(kept[3], totals[1], query)
    scatter = Scatter(terms_f, held_f, sems_q)
    size_t = kept[6].shape[0]
    for step, n in enumerate((across, far, mate, me)):
        lanes = lanes_of(n, block_f)
        if step < 3:
            copies_f[step].wait()
        prepare_upstream(back_f[n], mix_f[n], upstream_ref, lanes)
        if step == 2:
            scatter.middle()
        for head in range(2):
            back_unit(head, lanes, step == 0, time_side, query, upstream_ref, ds_f, grad_k, grad_v)
        terms_f[n] = mul(backward[1, 1], ds_f[:, lanes], NN).astype(BF)
        if step == 1:
            scatter.start_far()
        if step == 2:
            scatter.start_mate()
    keep_keys(True, ds_t, grad_k, grad_v, (0, LANES), size_t, group, block_t)
    for g in range(group):
        terms_t[g] = mul(backward[1, 0], ds_t[:, g * block_t : (g + 1) * block_t], NN).astype(BF)
    scatter_t = Scatter(terms_t, held_t, sems_p)
    scatter_t.start()
    halving.finish()
    halving.start()
    scatter_t.middle()
    store_rows(grads_in, ((ds_t, time_all), (ds_f, spec_all)))
    grad_norm[:, :LANES] = scatter_t.finish()
    grad_norm[:, LANES:] = scatter.finish()
    halving.finish()
    while halving.at < halving.steps - 1:
        halving.start()
        halving.finish()
    for n, (first, rows) in enumerate(halving.state):
        turn_part[n * rows : (n + 1) * rows] = turn_in[rows_of(first, rows), :]


def store_rows(target, streams):
    start = 0
    for n, (ds, whole) in enumerate(streams):
        for block in range(3):
            total = row_gradients(ds, whole, slice(block * LANES, (block + 1) * LANES))
            for head in range(2):
                target[start : start + HD] = total[head * HP : head * HP + HD].astype(BF)
                start += HD
        made = row_sums(ds, n)
        sums = made if n == 0 else sums + made
    target[start : start + 16] = sums.astype(BF)


def row_sums(ds, n):
    row = lax.broadcasted_iota(jnp.int32, (16, ds.shape[1]), 0)
    return mul((row == n).astype(BF), ds[...], NT)


def store_head(target, head, ds, whole):
    tiles = whole.shape[1] // LANES
    count = 3 * HD + 16
    for block in range(3):
        base = block * LANES + head * HP
        total = row_gradients(ds, whole, slice(base, base + HP))[:HD].astype(BF)
        for n in range(tiles):
            start = n * count + block * HD
            target[start : start + HD] = total[:, n * LANES : (n + 1) * LANES]
    sums = row_sums(ds, 0).astype(BF)
    for n in range(tiles):
        target[n * count + 3 * HD : (n + 1) * count] = sums[:, n * LANES : (n + 1) * LANES]
    if target.shape[0] > tiles * count:
        target[tiles * count :] = jnp.zeros_like(target[tiles * count :])


def load_head(target, tiles):
    count = 3 * HD + 16
    return jnp.concatenate([target[n * count : (n + 1) * count] for n in range(tiles)], axis=1)


def fourth_kernel(
    parts_turn, parts_in, parts_out, traffic, grad_norm, grad_in, time_y, spec_y, time_x, spec_x, in_t, in_f,
    w_out, cols, time_all, spec_all, backward, mix_t, mix_f, *rest,
):
    kept, totals = rest[:10], rest[10:12]
    turn_part, cross_in, attn_in, attn_out, small = rest[12:17]
    stream_grad, grad_a, grad_b, grad_c, grad_d, packed, scalars = rest[17:24]
    (turn_in, turn_stage, turn_out, turn_far, turn, cross, late_a, late_b, out, cross_one, late_a_one, late_b_one, out_one,
     cross_two, out_two, late_a_two, late_b_two, grads, out_t, out_f, back_t, back_f, terms_t, terms_f, held_t, held_f, held_two,
     ds_t, ds_f, query, upstream_ref, grad_k, grad_v, pieces, sems_q, sems_two, sems_three, sems_t, sems_f, sems_p, sems_y, sems_s,
     sems_turn, sems_cross, sems_a, sems_b, sems_out) = rest[24:]
    me, mate, across, far = places()
    size = lax.axis_size("dp")
    greet((mate, across, far), [lax.rem(lax.axis_index("dp") + n, size) for n in range(1, size)])
    group, local, block_t = mix_t.shape
    block_f, width = mix_f.shape[2], w_out.shape[2]

    def both(first, stage, last, sems, cut):
        return Chain(Halving(first, stage, last, sems.at[0], cut), Doubling(last, sems.at[1], cut))

    rest_parts = [segment_after(part) for part in parts_turn]
    rows = turn_part.shape[0] // len(parts_turn)
    for n, (first, count, _) in enumerate(rest_parts):
        turn_in[rows_of(first, rows), :] = turn_part[n * rows : (n + 1) * rows]
    rows_cross, rows_out = cross_in.shape[0], grads.shape[1]
    cross_one[:rows_cross] = cross_in[...]
    if cross_one.shape[0] > rows_cross:
        cross_one[rows_cross:] = jnp.zeros_like(cross_one[rows_cross:])
    chain_turn = Chain(
        Halving(turn_in, turn_stage, turn_out, sems_s, rest_parts),
        Chips(turn_out, turn_far, turn, sems_y, parts_turn), Doubling(turn, sems_turn, parts_turn[: len(parts_turn) // 2]),
    )
    chain_cross = both(cross_one, cross_two, cross, sems_cross, parts_in)
    chain_out = both(out_one, out_two, out, sems_out, parts_out)
    chain_a = Chain(Direct(late_a_one, late_a_two, late_a, sems_a))
    chain_b = Chain(Direct(late_b_one, late_b_two, late_b, sems_b))
    chain_turn.advance()
    chain_cross.advance()
    unit, scale_inv = norm_parts(jnp.concatenate([time_y[...], spec_y[...]], axis=1))
    value = grad_in[...] + norm_back(unit, scale_inv, grad_norm[...])
    traffic.ready(0)
    weights = (whole_weight(w_out, 0, local), whole_weight(w_out, 1, local))
    mixed_gradients(value, weights, (cols[:, 14:15], cols[:, 15:16]), (out_t, out_f))
    copies_t = send_blocks(out_t, back_t, sems_t)
    copies_f = send_blocks(out_f, back_f, sems_f)
    output_gradients(value, (in_t, in_f), grads, 0)
    scatter = Scatter(grads, held_two, sems_two)
    scatter.start()
    stream_grad[...] = value
    traffic.ready(1)
    for copy in copies_t:
        copy.wait()
    scatter.middle()
    time_side, spec_side = (kept[6], kept[1], kept[7]), (kept[8], kept[4], kept[9])
    size_t, size_f = kept[6].shape[0], kept[8].shape[0]
    back_time(time_side, kept, totals, back_t, mix_t, ds_t, query, upstream_ref, grad_k, grad_v)
    keep_keys(True, ds_t, grad_k, grad_v, (0, LANES), size_t, group, block_t)
    for g in range(group):
        terms_t[g] = mul(backward[0, 0], ds_t[:, g * block_t : (g + 1) * block_t], NN).astype(BF)
    chain_cross.advance()
    out_one[:rows_out] = scatter.finish().astype(BF)
    store_rows(out_one.at[rows_out:], ((ds_t, time_all),))
    rows_used = rows_out + 6 * HD + 16
    if out_one.shape[0] > rows_used:
        out_one[rows_used:] = jnp.zeros_like(out_one[rows_used:])
    chain_out.advance()
    prepare_queries(kept[3], totals[1], query)
    order = ((me, None), (mate, 2), (across, 0), (far, 1))
    moves = (
        (chain_turn, (0, 2, 4, 6)), (chain_cross, (1, 3, 5, 7)), (chain_out, (1, 3, 5, 7)), (chain_a, (6,)),
    )
    for head in range(2):
        for step, (n, arrival) in enumerate(order):
            lanes = lanes_of(n, block_f)
            if head == 0:
                if arrival is not None:
                    copies_f[arrival].wait()
                prepare_upstream(back_f[n], mix_f[n], upstream_ref, lanes)
            back_unit(head, lanes, step == 0, spec_side, query, upstream_ref, ds_f, grad_k, grad_v)
            for chain, when in moves:
                if head * 4 + step in when:
                    chain.advance()
        keep_keys(False, ds_f, grad_k, grad_v, (head * HP, (head + 1) * HP), size_f, group, block_f)
        if head == 0:
            store_head(late_a_one, 0, ds_f, spec_all)
            chain_a.advance()
    scatter_t = Scatter(terms_t, held_t, sems_three)
    scatter = Scatter(terms_f, held_f, sems_q)
    store_head(late_b_one, 1, ds_f, spec_all)
    chain_b.advance()
    for step, n in enumerate((far, across, mate, me)):
        terms_f[n] = mul(backward[0, 1], ds_f[:, lanes_of(n, block_f)], NN).astype(BF)
        if step == 0:
            scatter.start_far()
    scatter.middle()
    scatter.start_mate()
    scatter_t.start()
    scatter_t.middle()
    chains = (chain_turn, chain_cross, chain_out, chain_a)
    for chain in chains:
        chain.advance()
    traffic.ready(2)
    unit, scale_inv = norm_parts(jnp.concatenate([time_x[...], spec_x[...]], axis=1))
    chain_b.advance()
    for chain in chains:
        chain.complete()
    squares = jnp.zeros((1, width), F32)
    packed_rows = [jnp.zeros((1, width), F32) for _ in range(19)]
    tiles = width // LANES

    def add_squares(total, gradient):
        return total + jnp.sum(gradient * gradient, axis=0, keepdims=True)

    def turned(sums):
        return jnp.concatenate([sums, jnp.zeros((LANES - 16, width), F32)], axis=0).T

    def rows_done(squares, pick, plain, sums, lane, block):
        index, group = pick
        column = jnp.concatenate(
            [
                sums[head][block * LANES + head * HP : block * LANES + head * HP + HD, lane : lane + 1]
                for head in range(2)
            ],
            axis=0,
        )
        row = norm_rows[index][group]
        gradient = plain * small[row : row + 1, :] + column * small[row + 1 : row + 2, :]
        grad_a[index, group] = gradient.astype(BF)
        weight = attn_in[index, group]
        packed_rows[row] += jnp.sum(weight * plain, axis=0, keepdims=True)
        packed_rows[row + 1] += jnp.sum(weight * column, axis=0, keepdims=True)
        return add_squares(squares, gradient)

    rows = cross[: 12 * HD + 16].astype(F32)
    sums = (turned(rows[12 * HD :]),) * 2
    for stream, picks in enumerate(picks_of(True)):
        for block, pick in enumerate(picks):
            start = (stream * 6 + block * 2) * HD
            squares = rows_done(squares, pick, rows[start : start + local], sums, stream, block)
    rows = out[rows_out : rows_out + 6 * HD + 16].astype(F32)
    sums = (turned(rows[6 * HD :]),) * 2
    for block, pick in enumerate(picks_of(False)[0]):
        squares = rows_done(squares, pick, rows[block * local : (block + 1) * local], sums, 0, block)
    for index in range(4):
        if index < 2:
            plain = out[index * local : (index + 1) * local].astype(F32)
        else:
            start = 2 * width + (index - 2) * local
            plain = turn[start : start + local].astype(F32)
        gradient = plain * small[14 + index : 15 + index, :]
        grad_b[index] = gradient.astype(BF)
        squares = add_squares(squares, gradient)
        packed_rows[14 + index] += jnp.sum(attn_out[index] * plain, axis=0, keepdims=True)
    for target, start in ((grad_c, 0), (grad_d, width)):
        target[...] = turn[start : start + width]
        squares = add_squares(squares, turn[start : start + width].astype(F32))
    smalls = turn[2 * width + 2 * local : 2 * width + 2 * local + 16].astype(F32)
    for n, row in enumerate((12, 13, 18)):
        packed_rows[row] += smalls[n : n + 1]
    traffic.done(grad_b, grad_c, grad_d)
    chain_b.advance()
    halves = [load_head(late, tiles).astype(F32) for late in (late_a, late_b)]
    sums = [turned(half[3 * HD :]) for half in halves]
    for block, pick in enumerate(picks_of(False)[1]):
        plain = jnp.concatenate([half[block * HD : (block + 1) * HD] for half in halves], axis=0)
        squares = rows_done(squares, pick, plain, sums, 0, block)
    pieces[me] = jnp.concatenate(packed_rows + [squares] + [jnp.zeros((4, width), F32)], axis=0)
    copies = [
        push(pieces.at[me], pieces.at[me], sems_p.at[0, n], sems_p.at[1, n], other)
        for n, other in enumerate((across, far, mate))
    ]
    traffic.done(grad_a)
    scaled = jnp.concatenate([scatter_t.finish(), scatter.finish()], axis=1)
    stream_grad[...] = stream_grad[...] + norm_back(unit, scale_inv, scaled)
    traffic.done(stream_grad)
    for copy in copies:
        copy.wait()
    total = pieces[0]
    for n in range(1, pieces.shape[0]):
        total = total + pieces[n]
    packed[...] = total
    row = lax.broadcasted_iota(jnp.int32, total.shape, 0)
    every = jnp.where(row < 19, total * total, jnp.where(row == 19, total, 0.0))
    norm = jnp.sqrt(jnp.sum(jnp.sum(every, axis=0, keepdims=True), axis=1, keepdims=True))
    factor = jnp.minimum(1.0, clip_level / norm)
    lane = lax.broadcasted_iota(jnp.int32, scalars.shape, 1)
    scalars[...] = jnp.where(lane == 0, norm, factor)


def adam_parts(weight, first_moment, second_moment, gradient, step_rate, decay_rate):
    first_new = beta_first * first_moment + (1.0 - beta_first) * gradient
    second_new = beta_second * second_moment + (1.0 - beta_second) * gradient * gradient
    first_fix = 1.0 - beta_first**STEP
    second_fix = 1.0 - beta_second**STEP
    direction = (first_new * (1.0 / first_fix)) / (jnp.sqrt(second_new * (1.0 / second_fix)) + adam_eps)
    return (weight - step_rate * (direction + decay_rate * weight), first_new, second_new)


def last_kernel(live, traffic, scalars, packed, small, small_m, small_v, result, stream_grad, *refs):
    held, outs = refs[:16], refs[16:28]
    small_outs, (time_out, spec_out, time_grad, spec_grad, shift_gradient, norm) = refs[28:31], refs[31:37]
    sems_out = refs[37]
    rates = (rate_matrix, rate_output, rate_matrix, rate_matrix)
    factor = scalars[:, 1:2]
    gradient = packed[: small.shape[0]] * factor
    made = adam_parts(small[...], small_m[...], small_v[...], gradient, rate_small, 0.0)
    for target, value in zip(small_outs, made):
        target[...] = value
    shift_gradient[...] = gradient[13:14].reshape(-1)
    norm[...] = scalars[:, 0:1]
    leaving = []
    for n, rate in enumerate(rates):
        traffic.ready(n)
        gradient, weight, first_moment, second_moment = held[4 * n : 4 * n + 4]
        rows = weight.shape[0] // 3
        for piece in range(3):
            part = slice(piece * rows, (piece + 1) * rows)
            made = adam_parts(
                weight[part], first_moment[part], second_moment[part], gradient[part].astype(F32) * factor, rate, decay_matrix
            )
            for m, (target, value) in enumerate(zip((weight, first_moment, second_moment), made)):
                target[part] = value
                copy = pltpu.make_async_copy(
                    target.at[part], outs[3 * n + m].at[part], sems_out.at[9 * n + 3 * piece + m]
                )
                copy.start()
                leaving.append(copy)
        if n == 1:
            traffic.ready(4)
            for source, one, two in ((result, time_out, spec_out), (stream_grad, time_grad, spec_grad)):
                one[...] = source[:, :LANES].T[:live].reshape(live, 1, -1)
                two[0] = source[:, LANES:].T
                traffic.done(one, two)
    for copy in leaving:
        copy.wait()


def shards(
    time_in, spec_in, rate_flags, band_limits, time_cot, spec_cot, attn_in, attn_out, ffn_in, ffn_out, small,
    attn_in_m, attn_in_v, attn_out_m, attn_out_v, ffn_in_m, ffn_in_v, ffn_out_m, ffn_out_v, small_m, small_v,
):
    group, size = lax.axis_size("mp"), lax.axis_size("dp")
    live = time_in.shape[1]
    count = -(-live // 16) * 16
    block_t, block_f = LANES, spec_in.shape[1]
    width, local, part = time_in.shape[2], attn_in.shape[2], ffn_in.shape[1]
    lanes = block_t + block_f
    size_t, size_f, rows_t = group * block_t, group * block_f, group * count

    whole = (shape_of((group, width, block_t), BF), shape_of((group, width, block_f), BF))
    stream = (shape_of((width, block_t), F32), shape_of((width, block_f), F32))
    mix = (shape_of((group, local, block_t), BF), shape_of((group, local, block_f), BF))
    kept_shapes = tuple(
        shape_of(s, BF)
        for s in [(LANES, size_t)] + [(LANES, rows_t)] * 2 + [(LANES, size_f)] * 3 + [(rows_t, LANES)] * 2
        + [(size_f, LANES)] * 2
    ) + (shape_of((2, size_t), F32), shape_of((2, size_f), F32))
    packed_weights = (2, 3 * LANES, width)
    score = pltpu.VMEM((2, size_f, max(size_t, block_f)), F32)
    smem = pl.BlockSpec(memory_space=pltpu.SMEM)

    rows_w, parts_w = cut_parts(width, size, 3)
    rows_ffn, parts_ffn = cut_parts(2 * width, size, 6)
    bits = len(parts_w[0][2])
    count_w, count_ffn = len(parts_w), len(parts_ffn)
    made = call(
        functools.partial(forward_kernel, live, parts_w, parts_ffn), "forward",
        (stream + whole + mix + mix + kept_shapes) * 2 + (
            shape_of((2, 2, width, 3 * LANES), BF), shape_of((group, rows_w, width), BF),
            shape_of((group, rows_ffn, width), BF), shape_of((width, LANES), F32),
        ),
        (time_in, spec_in, rate_flags, band_limits, attn_in, attn_out, ffn_in, ffn_out, small),
        [
            pltpu.VMEM(packed_weights, BF), pltpu.VMEM((2, 3 * LANES, 1), F32),
            pltpu.VMEM(packed_weights, BF), pltpu.VMEM((2, 3 * LANES, 1), F32), pltpu.VMEM((1, size_f), F32),
            pltpu.VMEM((LANES, width), F32), score, pltpu.VMEM((2, 2, HP, block_f), F32), pltpu.VMEM((2, 2, block_f), F32),
            dma(6, 1), dma(6, 1), dma(2, 3), dma(2, 3), dma(2, count_w), dma(2, count_w, bits), dma(2, 1), dma(2, 1),
            dma(2, count_ffn), dma(6, 1), dma(6, 1), dma(2, 3), dma(2, 3), dma(2, count_ffn, bits), dma(2, 1), dma(2, 1),
        ],
        0, specs={2: smem, 3: smem}, late=((4,),),
        early=tuple(range(24)) + tuple(range(28, 38)) + (40, 41, 43),
    )
    (time_x, spec_x, time_all, spec_all, mix_t, mix_f, all_t, all_f), kept = made[:8], made[8:20]
    (time_y, spec_y, time_all_y, spec_all_y, mix_t_y, mix_f_y, all_t_y, all_f_y), kept_y = made[20:28], made[28:40]
    backward, w_out, w_ffn, cols = made[40:]

    rows_turn, rows_in = width + part + 2 * local + 16, 6 * local + 16
    back_scratch = [
        pltpu.VMEM((3 * LANES, size_t), BF), pltpu.VMEM((3 * LANES, size_f), BF),
        pltpu.VMEM((2, LANES, size_f), BF), pltpu.VMEM((2, LANES, size_f), BF),
        pltpu.VMEM((LANES, size_f), F32), pltpu.VMEM((LANES, size_f), F32),
    ]
    mixes = [pltpu.VMEM(m.shape, BF) for m in mix + mix]
    rows_pair, parts_turn = cut_parts(rows_turn, size, 2)
    parts_turn = parts_turn + [(first + rows_pair, rows, order) for first, rows, order in parts_turn]
    pair = pltpu.VMEM((2 * rows_pair, width), BF)
    terms = [pltpu.VMEM((group, width, block_t), BF), pltpu.VMEM((group, width, block_f), BF)]
    result, grad_stream, turn_part, cross_in, grad_norm = call(
        functools.partial(third_kernel, live, parts_turn), "third",
        (
            shape_of((width, lanes), F32), shape_of((width, lanes), F32), shape_of((4 * rows_pair // size, width), BF),
            shape_of((rows_in, width), BF), shape_of((width, lanes), F32),
        ),
        (
            all_t_y, all_f_y, time_y, spec_y, w_out, w_ffn, cols, time_cot, spec_cot,
            time_all_y, spec_all_y, backward, mix_t_y, mix_f_y,
        ) + tuple(kept_y),
        [pltpu.VMEM((group, rows_turn, width), BF)] + mixes + [pltpu.VMEM((LANES, width), F32)] + terms + terms + [
            pltpu.VMEM((2, rows_turn, width), BF), pair, pair,
            pltpu.VMEM((group, part, lanes), BF), pltpu.VMEM((group, part, lanes), BF),
        ] + back_scratch + [dma(2, 3), dma(2, 3), dma(2, 3), dma(2, 3), dma(2, 2), dma(2, 4, bits)], 2,
        late=((5, 7, 8), tuple(range(9, 26))), early=(0, 1),
    )

    rows_sum, parts_in = cut_parts(rows_in, size, 5)
    rows_out, parts_out = cut_parts(5 * local + 16, size, 4)
    rows_late, _ = cut_parts((width // LANES) * (3 * HD + 16), size, 1)
    sums, late, outs = (
        pltpu.VMEM(shape, BF) for shape in ((rows_sum, width), (rows_late, LANES), (rows_out, width))
    )
    pieces = pltpu.VMEM((size - 1, rows_late // size, LANES), BF)
    stream_grad, grad_a, grad_b, grad_c, grad_d, packed, scalars = call(
        functools.partial(fourth_kernel, parts_turn, parts_in, parts_out), "fourth",
        (
            shape_of((width, lanes), F32), shape_of(attn_in.shape, BF), shape_of(attn_out.shape, BF),
            shape_of(ffn_in.shape, BF), shape_of(ffn_out.shape, BF), shape_of((24, width), F32), shape_of((1, LANES), F32),
        ),
        (
            grad_norm, grad_stream, time_y, spec_y, time_x, spec_x, all_t, all_f, w_out, cols,
            time_all, spec_all, backward, mix_t, mix_f,
        ) + tuple(kept) + (turn_part, cross_in, attn_in, attn_out, small),
        [pair, pair, pair, pltpu.VMEM((rows_pair // size, width), BF), pltpu.VMEM((rows_pair, width), BF)] + [sums, late, late, outs] * 2 + [
            sums, outs, pieces, pieces, pltpu.VMEM((group, 2 * local, width), BF)] + mixes + terms + terms + [pltpu.VMEM((4, 2 * local, width), BF)]
        + back_scratch + [
            pltpu.VMEM((group, 24, width), F32), dma(2, 3), dma(2, 3), dma(2, 3), dma(2, 3), dma(2, 3), dma(2, 3), dma(2, 2), dma(2, 4, 1),
            dma(2, 2, bits), dma(2, 2, 5, bits), dma(2, 2, size - 1), dma(2, 2, size - 1), dma(2, 2, 4, bits),
        ], 3,
        late=((8, 6, 7), tuple(range(10, 27)), (4, 5, 29, 30, 31)), early=(0, 1, 2, 3, 4),
    )

    ins, outs = [], []
    for gradient, weight, first_moment, second_moment in (
        (grad_a, attn_in, attn_in_m, attn_in_v), (grad_b, attn_out, attn_out_m, attn_out_v),
        (grad_c, ffn_in, ffn_in_m, ffn_in_v), (grad_d, ffn_out, ffn_out_m, ffn_out_v),
    ):
        flat = (weight.size // width, width)
        ins += [value.reshape(flat) for value in (gradient, weight, first_moment, second_moment)]
        outs += [shape_of(flat, F32)] * 3
    outs += [shape_of(small.shape, F32)] * 3
    outs += [shape_of((live, 1, width), F32), shape_of((1, block_f, width), F32)] * 2
    outs += [shape_of((width,), F32), shape_of((1, 1), F32)]
    made = call(
        functools.partial(last_kernel, live), "last", outs, (scalars, packed, small, small_m, small_v, result, stream_grad, *ins),
        [dma(36)], None, late=tuple(tuple(range(7 + 4 * n, 11 + 4 * n)) for n in range(4)) + ((5, 6),),
        early=tuple(range(15, 19)), direct=tuple(range(12)),
    )
    updated = [
        value.reshape(weight.shape)
        for value, weight in zip(made[:15], [w for w in (attn_in, attn_out, ffn_in, ffn_out, small) for _ in range(3)])
    ]
    time_out, spec_out, time_grad, spec_grad, shift_gradient, norm = made[15:]
    time_out, time_grad = (jnp.swapaxes(value, 0, 1) for value in (time_out, time_grad))
    return (time_out, spec_out, time_grad, spec_grad, norm[0, 0], *updated, shift_gradient)


def solution(mesh):
    tokens, copied = P("dp", "mp", None), P()
    a, b, c, d = P(None, None, "mp", None), P(None, "mp", None), P(None, "mp"), P("mp", None)
    return jax.shard_map(
        shards,
        mesh=mesh,
        in_specs=(
            tokens, tokens, P("dp"), P("dp"), tokens, tokens, a, b, c, d, copied,
            a, a, b, b, c, c, d, d, copied, copied,
        ),
        out_specs=(
            tokens, tokens, tokens, tokens, copied,
            a, a, a, b, b, b, c, c, c, d, d, d, copied, copied, copied, copied,
        ),
        check_vma=False,
    )
```

```python
import functools
import math

import jax
import jax.numpy as jnp
from jax import lax
from jax.experimental import pallas as pl
from jax.experimental.pallas import tpu as pltpu
from jax.sharding import PartitionSpec as P

HD = 48
HP = 64
LANES = 128
FRAMES = 256
STEP = 10
BF = jnp.bfloat16
F32 = jnp.float32
NN = ((1,), (0,))
NT = ((1,), (1,))
TN = ((0,), (0,))
MESH = pl.DeviceIdType.MESH

norm_eps = 1e-05
clip_level = 100.0
beta_first = 0.9
beta_second = 0.95
adam_eps = 1e-08
decay_matrix = 0.1
rate_matrix = 0.05
rate_output = 0.5
rate_small = 0.5
masked_score = -1000000000.0
score_scale = HD ** (-0.5)
log_two = math.log(2.0)
query_scale = score_scale / log_two
vmem_limit = 58 * 2**20
AUX = HD
MASK_ROW = HD + 3
norm_rows = ((0, 0, 0), (2, 2, 2), (4, 6, 6), (8, 10, 10))


def mul(left, right, dims):
    return lax.dot_general(left, right, (dims, ((), ())), preferred_element_type=F32)


def dma(*shape):
    return pltpu.SemaphoreType.DMA(shape)


def vmem():
    return pl.BlockSpec(memory_space=pltpu.VMEM)


def shape_of(shape, kind):
    return jax.ShapeDtypeStruct(shape, kind)


class Traffic:
    def __init__(self):
        self.loads, self.stores, self.leaving = [], {}, []

    def ready(self, group):
        for copy in self.loads[group]:
            copy.wait()

    def done(self, *refs):
        for ref in refs:
            copy = self.stores.pop(id(ref))
            copy.start()
            self.leaving.append(copy)

    def finish(self):
        for copy in list(self.stores.values()):
            copy.start()
            self.leaving.append(copy)
        for copy in self.leaving:
            copy.wait()


def call(kernel, name, outs, args, scratch, collective, specs=None, late=(), early=(), direct=()):
    ins, count = len(args), len(args) + len(outs) + len(scratch)
    flat = [n for group in late for n in group]
    extra = [pltpu.VMEM(args[n].shape, args[n].dtype) for n in flat]
    extra += [pltpu.VMEM(outs[n].shape, outs[n].dtype) for n in early]
    extra += [dma(max(len(flat), 1)), dma(max(len(early), 1))]

    def body(*refs):
        refs, held = list(refs[:count]), refs[count:]
        traffic = Traffic()
        place = 0
        for group in late:
            copies = []
            for n in group:
                copies.append(pltpu.make_async_copy(refs[n], held[place], held[-2].at[place]))
                copies[-1].start()
                refs[n] = held[place]
                place += 1
            traffic.loads.append(copies)
        for m, n in enumerate(early):
            ref = held[place + m]
            traffic.stores[id(ref)] = pltpu.make_async_copy(ref, refs[ins + n], held[-1].at[m])
            refs[ins + n] = ref
        kernel(traffic, *refs)
        traffic.finish()

    anywhere = pl.BlockSpec(memory_space=pl.ANY)
    remote = {} if collective is None else {"collective_id": collective, "has_side_effects": True}
    return pl.pallas_call(
        body,
        name=name,
        out_shape=outs,
        in_specs=[anywhere if n in flat else (specs or {}).get(n, vmem()) for n in range(ins)],
        out_specs=tuple(anywhere if n in early or n in direct else vmem() for n in range(len(outs))),
        scratch_shapes=list(scratch) + extra,
        compiler_params=pltpu.CompilerParams(vmem_limit_bytes=vmem_limit, **remote),
    )(*args)


def places():
    me = lax.axis_index("mp")
    mate = me + 1 - 2 * lax.rem(me, 2)
    across = lax.rem(me + 2, 4)
    far = lax.rem(mate + 2, 4)
    return me, mate, across, far


def greet(others, partners=()):
    barrier = pltpu.get_barrier_semaphore()
    for other in others:
        pl.semaphore_signal(barrier, inc=1, device_id={"mp": other}, device_id_type=MESH)
    for partner in partners:
        pl.semaphore_signal(barrier, inc=1, device_id={"dp": partner}, device_id_type=MESH)
    pl.semaphore_wait(barrier, len(others) + len(partners))


def push_to(source, target, send, recv, device):
    copy = pltpu.make_async_remote_copy(
        source, target, send, recv, device_id=device, device_id_type=MESH
    )
    copy.start()
    return copy


def push(source, target, send, recv, device):
    return push_to(source, target, send, recv, {"mp": device})


class Gather:
    def __init__(self, ref, sems, lanes=None):
        self.ref, self.sems, self.lanes = ref, sems, lanes

    def block(self, index):
        return self.ref.at[index] if self.lanes is None else self.ref.at[index, :, self.lanes]

    def start(self):
        me, mate, across, far = places()
        own = self.block(me)
        self.first = push(own, own, self.sems.at[0], self.sems.at[1], across)
        self.second = push(own, own, self.sems.at[2], self.sems.at[3], mate)
        return self

    def near(self):
        self.second.wait_recv()

    def finish(self, near=False):
        self.relay()
        self.end(near)

    def relay(self):
        me, mate, across, far = places()
        self.first.wait_recv()
        other = self.block(across)
        self.third = push(other, other, self.sems.at[4], self.sems.at[5], mate)

    def end(self, near=False):
        self.first.wait_send()
        if near:
            self.second.wait_send()
        else:
            self.second.wait()
        self.third.wait()


def send_block(source, target, sems, n, other):
    me, mate, across, far = places()
    return push(source.at[other], target.at[me], sems.at[0, n], sems.at[1, n], other)


def send_blocks(source, target, sems):
    me, mate, across, far = places()
    copies = [send_block(source, target, sems, n, other) for n, other in enumerate((across, far, mate))]
    target[me] = source[me]
    return copies


class Scatter:
    def __init__(self, source, held, sems):
        self.source, self.held, self.sems = source, held, sems

    def start_far(self):
        me, mate, across, far = places()
        self.one = push(self.source.at[far], self.held.at[0], self.sems.at[0, 0], self.sems.at[1, 0], mate)

    def start_mate(self):
        me, mate, across, far = places()
        self.two = push(self.source.at[mate], self.held.at[1], self.sems.at[0, 1], self.sems.at[1, 1], mate)

    def start(self):
        self.start_far()
        self.start_mate()

    def middle(self):
        me, mate, across, far = places()
        self.one.wait()
        self.held[2] = (self.source[across].astype(F32) + self.held[0].astype(F32)).astype(BF)
        self.cross = push(self.held.at[2], self.held.at[3], self.sems.at[0, 2], self.sems.at[1, 2], across)

    def finish(self):
        me, mate, across, far = places()
        self.two.wait()
        total = self.source[me].astype(F32) + self.held[1].astype(F32)
        self.cross.wait()
        return total + self.held[3].astype(F32)


def norm_parts(stream):
    center = stream - jnp.mean(stream, axis=0, keepdims=True)
    scale_inv = lax.rsqrt(jnp.mean(center * center, axis=0, keepdims=True) + norm_eps)
    return center * scale_inv, scale_inv


def norm_back(unit, scale_inv, scaled):
    return scale_inv * (
        scaled
        - jnp.mean(scaled, axis=0, keepdims=True)
        - unit * jnp.mean(scaled * unit, axis=0, keepdims=True)
    )


def attend_blocks(
    places_in, block, keys, queries, values, score, write, after, span=None, keep=None, prior=None
):
    first, rows_k = span or (0, keys.shape[0])
    here, there = rows_of(first, rows_k), lanes_from(first, rows_k)
    row = lax.broadcasted_iota(jnp.int32, (LANES, block), 0)

    def make(n, head):
        query = queries[:, lanes_of(n, block)]
        own = (row < HP) if head == 0 else (row >= HP)
        score[head, :rows_k, :] = mul(keys[here, :], jnp.where(own, query, jnp.zeros_like(query)), NN)

    def finish(step, n, head):
        held = score[head, :rows_k, :]
        peak = jnp.max(held, axis=0, keepdims=True)
        shares = jnp.exp2(held - peak).astype(BF)
        mixed = mul(values[head * HP : (head + 1) * HP, there], shares, NN)
        if keep is not None:
            keep(step, head, mixed, peak)
            return
        if prior is not None:
            other, other_peak = prior(step, head)
            new_peak = jnp.maximum(peak, other_peak)
            mixed = mixed * jnp.exp2(peak - new_peak) + other * jnp.exp2(other_peak - new_peak)
            peak = new_peak
        total = mixed[AUX : AUX + 1, :]
        write(n, head, (mixed[:HD] * (1.0 / total)).astype(BF), peak + jnp.log2(total))

    make(places_in[0], 0)
    for step, n in enumerate(places_in):
        make(n, 1)
        finish(step, n, 0)
        if step + 1 < len(places_in):
            make(places_in[step + 1], 0)
        finish(step, n, 1)
        after(step, n)


def lanes_from(first, count):
    return pl.ds(first if isinstance(first, int) else pl.multiple_of(first, LANES), count)


def lanes_of(n, block):
    return pl.ds(n * block if isinstance(n, int) else pl.multiple_of(n * block, LANES), block)


def split_three(value):
    high = value.astype(BF)
    rest = value - high.astype(F32)
    middle = rest.astype(BF)
    return high, middle, (rest - middle.astype(F32)).astype(BF)


def with_rows(body, head, parts):
    row = lax.broadcasted_iota(jnp.int32, body.shape, 0) - head * HP
    out = jnp.where((row >= 0) & (row < HP), body.astype(F32), 0.0)
    for n, part in enumerate(parts):
        out = jnp.where(row == AUX + n, part.astype(F32), out)
    return out.astype(BF)


def back_unit(head, lanes, fresh, side, queries, upstream, grad_q, grad_k, grad_v):
    keys_rows, keys, values_rows = side
    rows_k = keys_rows.shape[0]
    own = slice(head * HP, (head + 1) * HP)
    shares = jnp.exp2(mul(keys_rows[...], queries[head, :, lanes], NN))
    inner = mul(values_rows[...], upstream[head, :, lanes], NN)
    grad_score = (shares * inner).astype(BF)
    shares = shares.astype(BF)
    grad_q[own, lanes] = (mul(keys[own, :], grad_score, NN) * score_scale).astype(BF)
    made_k = mul(queries[head, own, lanes], grad_score, NT)
    made_v = mul(upstream[head, own, lanes], shares, NT)
    grad_k[own, :rows_k] = made_k if fresh else grad_k[own, :rows_k] + made_k
    grad_v[own, :rows_k] = made_v if fresh else grad_v[own, :rows_k] + made_v


def prepare_queries(q, total, query):
    size = q.shape[1]
    for head in range(2):
        query[head, :, :size] = with_rows(q[...], head, split_three(-total[head : head + 1, :]))


def prepare_upstream(part, mixed, upstream, lanes):
    block = part.shape[1]
    for head in range(2):
        rows = slice(head * HD, (head + 1) * HD)
        inner = jnp.sum(part[rows].astype(F32) * mixed[rows].astype(F32), axis=0, keepdims=True)
        padded = jnp.concatenate(
            [part[rows], *split_three(-inner), jnp.zeros((HP - HD - 3, block), BF)], axis=0
        )
        other = jnp.zeros((HP, block), BF)
        both = [padded, other] if head == 0 else [other, padded]
        upstream[head, :, lanes] = jnp.concatenate(both, axis=0)


def back_time(side, kept, totals, back_t, mix_t, ds_t, query, upstream, grad_k, grad_v):
    group, _, block = mix_t.shape
    prepare_queries(kept[0], totals[0], query)
    for g in range(group):
        prepare_upstream(back_t[g], mix_t[g], upstream, lanes_of(g, block))
    for head in range(2):
        back_unit(head, slice(0, group * block), True, side, query, upstream, ds_t, grad_k, grad_v)


def spread_keys(ds, base, source, group, block):
    turned = source.T
    count, width = turned.shape[0] // group, turned.shape[1]
    for g in range(group):
        part = turned[g * count : (g + 1) * count]
        part = jnp.concatenate([part, jnp.zeros((block - count, width), F32)], axis=0)
        ds[base : base + width, g * block : (g + 1) * block] = part.T.astype(BF)


def keep_keys(time_keys, ds, grad_k, grad_v, rows, size, group, block):
    start, stop = rows
    key, value = grad_k[start:stop, :size] * log_two, grad_v[start:stop, :size]
    for base, made in ((LANES, key), (2 * LANES, value)):
        if time_keys:
            spread_keys(ds, base + start, made, group, block)
        else:
            ds[base + start : base + stop, :] = made.astype(BF)


def row_gradients(ds, whole, rows):
    group, _, block = whole.shape
    total = None
    for g in range(group):
        made = mul(ds[rows, g * block : (g + 1) * block], whole[g], NT)
        total = made if total is None else total + made
    return total


def bit_orders(size):
    bits = [1 << n for n in range(size.bit_length() - 1)]
    return bits, bits[1:2] + bits[:1] + bits[2:]


def cut_parts(count, size, parts):
    tile = 16 * size
    parts = min(parts, -(-count // tile))
    rows = -(-count // (tile * parts)) * tile
    return rows * parts, [(n * rows, rows, bit_orders(size)[n % 2]) for n in range(parts)]


def partner_of(bit):
    index = lax.axis_index("dp")
    mine = lax.rem(index // bit, 2)
    return mine, index + bit * (1 - 2 * mine)


def segment_of(part):
    first, rows, bits = part
    for bit in bits:
        rows = rows // 2
        first = first + partner_of(bit)[0] * rows
    return first, rows


def rows_of(first, rows):
    return pl.ds(first if isinstance(first, int) else pl.multiple_of(first, 16), rows)


class Halving:
    def __init__(self, source, stage, target, sems, parts):
        self.source, self.stage, self.target, self.sems = source, stage, target, sems
        self.state = [list(part[:2]) for part in parts]
        self.orders = [part[2] for part in parts]
        self.full = [part[1] for part in parts]
        self.steps, self.at, self.copies = len(self.orders[0]), 0, []

    def start(self):
        self.copies = []
        for n, (first, rows) in enumerate(self.state):
            mine, partner = partner_of(self.orders[n][self.at])
            half = rows // 2
            place = self.held(n)
            self.copies.append(
                push_to(
                    self.source.at[rows_of(first + (1 - mine) * half, half)], self.stage.at[rows_of(place, half)],
                    self.sems.at[0, n, self.at], self.sems.at[1, n, self.at], {"dp": partner},
                )
            )

    def held(self, n):
        total = self.full[n]
        return sum(self.full[:n]) + total - (total >> self.at)

    def finish(self):
        into = self.target if self.at == self.steps - 1 else self.source
        for n, copy in enumerate(self.copies):
            first, rows = self.state[n]
            mine, partner = partner_of(self.orders[n][self.at])
            half = rows // 2
            here, there = rows_of(first + mine * half, half), rows_of(self.held(n), half)
            copy.wait()
            into[here, :] = (self.source[here, :].astype(F32) + self.stage[there, :].astype(F32)).astype(BF)
            self.state[n] = [first + mine * half, half]
        self.at += 1


class Doubling:
    def __init__(self, target, sems, parts):
        self.target, self.sems = target, sems
        self.state = [list(segment_of(part)) for part in parts]
        self.orders = [part[2][::-1] for part in parts]
        self.steps, self.at, self.copies = len(self.orders[0]), 0, []

    def start(self):
        self.copies = []
        for n, (first, rows) in enumerate(self.state):
            mine, partner = partner_of(self.orders[n][self.at])
            here = self.target.at[rows_of(first, rows)]
            self.copies.append(
                push_to(here, here, self.sems.at[0, n, self.at], self.sems.at[1, n, self.at], {"dp": partner})
            )

    def finish(self):
        for n, copy in enumerate(self.copies):
            first, rows = self.state[n]
            mine, partner = partner_of(self.orders[n][self.at])
            copy.wait()
            self.state[n] = [first - mine * rows, 2 * rows]
        self.at += 1


class Direct:
    steps = 2

    def __init__(self, source, stage, target, sems):
        self.source, self.stage, self.target, self.sems, self.at = source, stage, target, sems, 0
        self.size = lax.axis_size("dp")
        self.rows = source.shape[0] // self.size

    def piece(self, index):
        return rows_of(index * self.rows, self.rows)

    def start(self):
        index = lax.axis_index("dp")
        self.copies = []
        for n in range(1, self.size):
            other = lax.rem(index + n, self.size)
            if self.at == 0:
                source, target = self.source.at[self.piece(other)], self.stage.at[n - 1]
            else:
                source = target = self.target.at[self.piece(index)]
            self.copies.append(
                push_to(
                    source, target, self.sems.at[self.at, 0, n - 1], self.sems.at[self.at, 1, n - 1], {"dp": other}
                )
            )

    def finish(self):
        for copy in self.copies:
            copy.wait()
        if self.at == 0:
            here = self.piece(lax.axis_index("dp"))
            total = self.source[here, :].astype(F32)
            for n in range(self.size - 1):
                total = total + self.stage[n].astype(F32)
            self.target[here, :] = total.astype(BF)
        self.at += 1


class Across:
    steps = 1

    def __init__(self, source, target, sems, parts):
        self.source, self.target, self.sems, self.parts, self.at = source, target, sems, parts, 0

    def start(self):
        me, mate, across, far = places()
        self.copies = []
        for n, part in enumerate(self.parts):
            rows = rows_of(*segment_of(part))
            self.copies.append(
                push(self.source.at[rows], self.target.at[rows], self.sems.at[0, n], self.sems.at[1, n], across)
            )

    def finish(self):
        for copy in self.copies:
            copy.wait()
        self.at += 1


def segment_after(part):
    first, rows, bits = part
    for bit in bits[:-1]:
        rows = rows // 2
        first = first + partner_of(bit)[0] * rows
    return first, rows, bits[-1:]


class Chips:
    steps = 1

    def __init__(self, source, held, target, sems, parts):
        self.source, self.held, self.target, self.sems, self.at = source, held, target, sems, 0
        self.parts = parts[: len(parts) // 2]
        self.half = sum(part[1] for part in self.parts)

    def start(self):
        me, mate, across, far = places()
        chip = me // 2
        self.copies = []
        for n, part in enumerate(self.parts):
            first, rows = segment_of(part)
            self.copies.append(
                push(
                    self.source.at[rows_of(first + (1 - chip) * self.half, rows)],
                    self.held.at[n * rows : (n + 1) * rows], self.sems.at[0, n], self.sems.at[1, n], across,
                )
            )

    def finish(self):
        chip = places()[0] // 2
        for n, copy in enumerate(self.copies):
            copy.wait()
            first, rows = segment_of(self.parts[n])
            own = self.source[rows_of(first + chip * self.half, rows), :].astype(F32)
            total = own + self.held[n * rows : (n + 1) * rows].astype(F32)
            self.target[rows_of(first, rows), :] = total.astype(BF)
        self.at += 1


class Relay:
    steps = 1

    def __init__(self, whole, sems, blocks):
        self.whole, self.sems, self.blocks, self.at = whole, sems, blocks, 0

    def start(self):
        me, mate, across, far = places()
        self.copies = [
            push(self.whole.at[block], self.whole.at[block], self.sems.at[0, n], self.sems.at[1, n], mate)
            for n, block in enumerate(self.blocks)
        ]

    def finish(self):
        for copy in self.copies:
            copy.wait()
        self.at += 1


class Chain:
    def __init__(self, *stages):
        self.stages, self.now, self.flying = list(stages), 0, False

    def advance(self):
        if self.now == len(self.stages):
            return
        stage = self.stages[self.now]
        if self.flying:
            stage.finish()
            if stage.at == stage.steps:
                self.now += 1
                self.flying = False
                if self.now == len(self.stages):
                    return
                stage = self.stages[self.now]
        stage.start()
        self.flying = True

    def complete(self):
        while self.now < len(self.stages):
            self.advance()


def picks_of(cross):
    if cross:
        return ((2, 0), (3, 1), (3, 2)), ((3, 0), (2, 1), (2, 2))
    return ((0, 0), (0, 1), (0, 2)), ((1, 0), (1, 1), (1, 2))


def fold_weights(cross, attn_in, small, forward, offsets, backward):
    width = attn_in.shape[3]
    for stream, picks in enumerate(picks_of(cross)):
        blocks = []
        for block, (index, group) in enumerate(picks):
            row = norm_rows[index][group]
            weight = attn_in[index, group]
            folded = weight * small[row : row + 1, :]
            offset = jnp.sum(weight * small[row + 1 : row + 2, :], axis=1, keepdims=True)
            factor = query_scale if group == 0 else 1.0
            ones = (MASK_ROW,) if group == 0 else (AUX, AUX + 1, AUX + 2)
            spare = lax.broadcasted_iota(jnp.int32, (HP - HD, 1), 0) + HD
            marks = jnp.zeros((HP - HD, 1), F32)
            for one in ones:
                marks = jnp.where(spare == one, 1.0, marks)
            for head in range(2):
                rows = slice(head * HD, (head + 1) * HD)
                start = block * LANES + head * HP
                forward[stream, start : start + HD, :] = (folded[rows] * factor).astype(BF)
                forward[stream, start + HD : start + HP, :] = jnp.zeros((HP - HD, width), BF)
                offsets[stream, start : start + HD, :] = offset[rows] * factor
                offsets[stream, start + HD : start + HP, :] = marks
                blocks += [folded[rows], jnp.zeros((HP - HD, width), F32)]
        backward[stream] = jnp.concatenate(blocks, axis=0).T.astype(BF)


def project_time(live, time_all, forward, offsets, kept):
    qt, kt, vt, qf, kf, vf, kt_rows, vt_rows, kf_rows, vf_rows = kept
    group, _, block = time_all.shape
    row = lax.broadcasted_iota(jnp.int32, (LANES, block), 0)
    lane = lax.broadcasted_iota(jnp.int32, (LANES, block), 1)
    dead = jnp.where(lane < live, 0.0, masked_score)
    mask = jnp.where((row == MASK_ROW) | (row == MASK_ROW + HP), dead, 0.0)
    count = kt_rows.shape[0] // group
    for n in range(group):
        made = mul(forward[0], time_all[n], NN) + offsets[0]
        qt[:, n * block : (n + 1) * block] = made[:LANES].astype(BF)
        key, value = (made[LANES : 2 * LANES] + mask).astype(BF), made[2 * LANES :].astype(BF)
        lanes = slice(n * count, (n + 1) * count)
        kt_rows[lanes, :], vt_rows[lanes, :] = key.T[:count], value.T[:count]
    kt[...] = kt_rows[...].T
    vt[...] = vt_rows[...].T


def project_spec(n, spec_all, forward, offsets, bias, kept):
    qt, kt, vt, qf, kf, vf, kt_rows, vt_rows, kf_rows, vf_rows = kept
    block = spec_all.shape[2]
    lanes = lanes_of(n, block)
    row = lax.broadcasted_iota(jnp.int32, (LANES, block), 0)
    made = mul(forward[1], spec_all[n], NN) + offsets[1]
    qf[:, lanes] = made[:LANES].astype(BF)
    mask = jnp.where((row == MASK_ROW) | (row == MASK_ROW + HP), bias[:, lanes], 0.0)
    key, value = (made[LANES : 2 * LANES] + mask).astype(BF), made[2 * LANES :].astype(BF)
    kf[:, lanes], vf[:, lanes] = key, value
    kf_rows[lanes, :], vf_rows[lanes, :] = key.T, value.T


def time_attention(side, kept, totals, mix_t, all_t, sems, score):
    group, _, block = mix_t.shape
    copies = []

    def write(n, head, value, total):
        for g in range(group):
            mix_t[g, head * HD : (head + 1) * HD, :] = value[:, g * block : (g + 1) * block]
        totals[0][head : head + 1, :] = total

    def after(step, n):
        copies.extend(send_blocks(mix_t, all_t, sems))

    attend_blocks((0,), group * block, side[0], kept[0], side[1], score, write, after)
    return copies


def spec_attention(blocks, side, kept, totals, mix_f, all_f, sems, score, first, between, **part):
    block = mix_f.shape[2]
    copies = []

    def write(n, head, value, total):
        mix_f[n, head * HD : (head + 1) * HD, :] = value
        totals[1][head : head + 1, lanes_of(n, block)] = total

    def after(step, n):
        step += first
        if step < 3:
            copies.append(send_block(mix_f, all_f, sems, step, n))
        else:
            all_f[n] = mix_f[n]
        between(step)

    attend_blocks(blocks, block, side[0], kept[3], side[1], score, write, after, **part)
    return copies


def forward_kernel(
    live, parts, parts_ffn, traffic, time_in, spec_in, flags, limits, attn_in, attn_out, ffn_in, ffn_out, small,
    time_x, spec_x, time_all, spec_all, mix_t, mix_f, all_t, all_f, *rest,
):
    kept, totals = rest[:10], rest[10:12]
    time_y, spec_y, time_all_y, spec_all_y, mix_t_y, mix_f_y, all_t_y, all_f_y = rest[12:20]
    kept_y, totals_y = rest[20:30], rest[30:32]
    backward, weights, w_ffn, cols = rest[32:36]
    (forward, offsets, forward_two, offsets_two, bias, rows_t, score, part_mix, part_peak, sems_p, sems_q, sems_t, sems_f, sems_a, sems_d,
     sems_r, sems_s, sems_n, sems_p_two, sems_q_two, sems_t_two, sems_f_two, sems_m, sems_u, sems_v) = rest[36:]
    me, mate, across, far = places()
    greet((mate, across, far), [partner_of(bit)[1] for bit in parts[0][2]])
    width, local = ffn_in.shape[0], mix_t.shape[1]
    weights[me, :width] = attn_out[...].reshape(width, width).astype(BF)
    if weights.shape[1] > width:
        weights[me, width:] = jnp.zeros_like(weights[me, width:])
    w_ffn[me, :width] = ffn_in[...].astype(BF)
    w_ffn[me, width : 2 * width] = ffn_out[...].astype(BF)
    if w_ffn.shape[1] > 2 * width:
        w_ffn[me, 2 * width :] = jnp.zeros_like(w_ffn[me, 2 * width :])
    chain = Chain(
        Across(weights.at[me], weights.at[me], sems_a, parts), Doubling(weights.at[across], sems_d, parts),
        Relay(weights, sems_r, (across,)),
    )
    chain.advance()
    chain_ffn = Chain(
        Across(w_ffn.at[me], w_ffn.at[me], sems_n, parts_ffn), Doubling(w_ffn.at[across], sems_m, parts_ffn),
        Relay(w_ffn, sems_u, (across,)),
    )
    chain_ffn.advance()
    rows_t[...] = jnp.zeros_like(rows_t)
    rows_t[:live, :] = time_in[0].astype(F32)
    time_x[...] = rows_t[...].T
    time_all[me] = norm_parts(time_x[...])[0].astype(BF)
    gather_t = Gather(time_all, sems_p).start()
    block_f = mix_f.shape[2]
    halves = (slice(0, block_f // 2), slice(block_f // 2, block_f))
    gathers = []
    for n, part in enumerate(halves):
        spec_x[:, part] = spec_in[0, part, :].astype(F32).T
        spec_all[me, :, part] = norm_parts(spec_x[:, part])[0].astype(BF)
        gathers.append(Gather(spec_all, sems_q.at[n], part).start())
    own = Relay(weights, sems_s, (me,))
    own.start()
    own_ffn = Relay(w_ffn, sems_v, (me,))
    own_ffn.start()
    traffic.done(time_x, spec_x)
    traffic.ready(0)
    fold_weights(False, attn_in, small, forward, offsets, backward.at[0])
    bins = lax.broadcasted_iota(jnp.int32, bias.shape, 1) // FRAMES
    bias[...] = jnp.where((bins < limits[0]) | (flags[0] == 0), 0.0, masked_score)
    gather_t.finish()
    chain.advance()
    project_time(live, time_all, forward, offsets, kept)
    time_side, spec_side = (kept[6], kept[2]), (kept[8], kept[5])
    copies = time_attention(time_side, kept, totals, mix_t, all_t, sems_t, score)
    project_spec(me, spec_all, forward, offsets, bias, kept)
    chain.advance()
    fold_weights(True, attn_in, small, forward_two, offsets_two, backward.at[1])
    cols[...] = jnp.concatenate(
        [small[...], jnp.zeros((LANES - small.shape[0], small.shape[1]), F32)], axis=0
    ).T
    own.finish()
    own_ffn.finish()
    traffic.done(time_all, backward, cols)
    for gather in gathers:
        gather.near()
    project_spec(mate, spec_all, forward, offsets, bias, kept)
    chip, half = me // 2, 2 * block_f

    def keep(step, head, value, peak):
        part_mix[step, head] = value
        part_peak[step, head : head + 1] = peak

    def prior(step, head):
        return part_mix[step, head], part_peak[step, head : head + 1]

    attend_blocks(
        (mate, me), block_f, spec_side[0], kept[3], spec_side[1], score, None, lambda step, n: None,
        span=(chip * half, half), keep=keep,
    )
    for gather in gathers:
        gather.relay()
    for gather in gathers:
        gather.end(near=True)
    chain.advance()
    for n in (across, far):
        project_spec(n, spec_all, forward, offsets, bias, kept)
    traffic.done(spec_all, *kept)

    def between(step):
        if step in (0, 1, 2):
            chain.advance()
        if step == 2:
            chain_ffn.advance()

    copies += spec_attention((across, far), spec_side, kept, totals, mix_f, all_f, sems_f, score, 0, between)
    copies += spec_attention(
        (mate, me), spec_side, kept, totals, mix_f, all_f, sems_f, score, 2, between,
        span=((1 - chip) * half, half), prior=prior,
    )
    chain.complete()
    for copy in copies:
        copy.wait()
    traffic.done(mix_t, mix_f, all_t, all_f, *totals, weights)
    kept, totals = kept_y, totals_y
    time_y[...] = add_branch(joined(all_t), whole_weight(weights, 0, local), cols[:, 14:15], time_x[...])
    time_all_y[me] = norm_parts(time_y[...])[0].astype(BF)
    gather_t = Gather(time_all_y, sems_p_two).start()
    gathers = []
    for n, part in enumerate(halves):
        mixed = all_f[:, :, part].reshape(-1, block_f // 2)
        spec_y[:, part] = add_branch(mixed, whole_weight(weights, 1, local), cols[:, 15:16], spec_x[:, part])
        spec_all_y[me, :, part] = norm_parts(spec_y[:, part])[0].astype(BF)
        gathers.append(Gather(spec_all_y, sems_q_two.at[n], part).start())
    traffic.done(time_y, spec_y)
    chain_ffn.advance()
    gather_t.finish()
    project_time(live, time_all_y, forward_two, offsets_two, kept)
    project_spec(me, spec_all_y, forward_two, offsets_two, bias, kept)
    for gather in gathers:
        gather.relay()
    for gather in gathers:
        gather.end()
    chain_ffn.advance()
    time_side, spec_side = (kept[6], kept[2]), (kept[8], kept[5])
    copies = []
    for step, n in enumerate((across, far, mate, me)):
        if step < 3:
            project_spec(n, spec_all_y, forward_two, offsets_two, bias, kept)
        copies += spec_attention(
            (n,), time_side, kept, totals, mix_f_y, all_f_y, sems_f_two, score, step, lambda step: None
        )
    traffic.done(time_all_y, spec_all_y, *kept)
    chain_ffn.advance()
    copies += time_attention(spec_side, kept, totals, mix_t_y, all_t_y, sems_t_two, score)
    chain_ffn.complete()
    for copy in copies:
        copy.wait()


def whole_weight(weights, index, rows):
    part = weights[:, index * rows : (index + 1) * rows]
    return part.reshape(-1, part.shape[2])


def joined(mixed):
    part = mixed[...]
    return part.reshape(-1, part.shape[2])


def add_branch(mixed, w_out, scale, stream):
    return stream + scale * mul(w_out, mixed, TN)


def gelu_pair(values):
    share = 0.5 * (1.0 + lax.erf(values * (2.0**-0.5)))
    slope = share + values * (jnp.exp(-0.5 * values * values) * ((2.0 * math.pi) ** -0.5))
    return values * share, slope


def mixed_gradients(grad_stream, weights, scales, outgoing):
    for n, lanes in enumerate((slice(0, LANES), slice(LANES, None))):
        grad_mix = mul(weights[n], (scales[n] * grad_stream[:, lanes]).astype(BF), NN).astype(BF)
        group, width = outgoing[n].shape[:2]
        for g in range(group):
            outgoing[n][g] = grad_mix[g * width : (g + 1) * width]


def output_gradients(grad_stream, mixed, grads, start):
    for n, lanes in enumerate((slice(0, LANES), slice(LANES, None))):
        grad_out = mul(joined(mixed[n]), grad_stream[:, lanes].astype(BF), NT).astype(BF)
        group, width = mixed[n].shape[:2]
        for g in range(group):
            grads[g, start + n * width : start + (n + 1) * width] = grad_out[g * width : (g + 1) * width]


def third_kernel(
    live, parts_turn, traffic, in_t, in_f, time_x, spec_x, w_out, w_ffn, cols, time_dy, spec_dy,
    time_all, spec_all, backward, mix_t, mix_f, *rest,
):
    kept, totals = rest[:10], rest[10:12]
    result, grad_stream, turn_part, grads_in, grad_norm = rest[12:17]
    (grads, out_t, out_f, back_t, back_f, rows_t, terms_t, terms_f, held_t, held_f, held_core, turn_in, turn_stage, actives,
     grad_hiddens, ds_t, ds_f, query, upstream_ref, grad_k, grad_v, sems_p, sems_q, sems_t, sems_f, sems_c, sems_h) = rest[17:]
    me, mate, across, far = places()
    greet((mate, across, far), [partner_of(bit)[1] for bit in parts_turn[0][2]])
    group, local, block_t = mix_t.shape
    block_f, width = mix_f.shape[2], w_out.shape[2]
    w_first, w_second = w_ffn.at[:, :width], w_ffn.at[:, width : 2 * width]
    gain, shift, scale = cols[:, 12:13], cols[:, 13:14], cols[:, 18:19]
    weights = (whole_weight(w_out, 2, local), whole_weight(w_out, 3, local))
    scales = (cols[:, 16:17], cols[:, 17:18])
    stream = jnp.concatenate(
        [
            add_branch(joined(in_t), weights[0], scales[0], time_x[...]),
            add_branch(joined(in_f), weights[1], scales[1], spec_x[...]),
        ],
        axis=1,
    )
    traffic.ready(0)
    rows_t[...] = jnp.zeros_like(rows_t)
    rows_t[:live, :] = time_dy[0].astype(F32)
    upstream = jnp.concatenate([rows_t[...].T, spec_dy[0].astype(F32).T], axis=1)
    unit, scale_inv = norm_parts(stream)
    normed = (unit * gain + shift).astype(BF)
    grad_branch = (scale * upstream).astype(BF)
    branch = grad_normed = None
    for g in range(group):
        hidden = mul(w_first[g], normed, TN)
        active, slope = gelu_pair(hidden)
        actives[g] = active.astype(BF)
        made = mul(w_second[g], actives[g], TN)
        branch = made if branch is None else branch + made
        grad_hiddens[g] = (mul(w_second[g], grad_branch, NN) * slope).astype(BF)
        made = mul(w_first[g], grad_hiddens[g], NN)
        grad_normed = made if grad_normed is None else grad_normed + made
    value = upstream + norm_back(unit, scale_inv, grad_normed * gain)
    mixed_gradients(value, weights, scales, (out_t, out_f))
    copies_t = send_blocks(out_t, back_t, sems_t)
    copies_f = send_blocks(out_f, back_f, sems_f)
    last = 2 * width + 2 * local
    for g in range(group):
        grads[g, :width] = mul(normed, grad_hiddens[g], NT).astype(BF)
        grads[g, width : 2 * width] = mul(actives[g], grad_branch, NT).astype(BF)
    output_gradients(value, (in_t, in_f), grads, 2 * width)
    sums = jnp.concatenate(
        [
            jnp.sum(item, axis=1, keepdims=True)
            for item in (grad_normed * unit, grad_normed, upstream * branch)
        ] + [jnp.zeros((width, LANES - 3), F32)],
        axis=1,
    ).T[:16].astype(BF)
    for g in range(group):
        grads[g, last : last + 16] = sums if g == 0 else jnp.zeros_like(sums)
    core = lax.rem(me, 2)
    rows_turn, rows_half = grads.shape[1], turn_in.shape[0] // 2
    copies = [
        push(grads.at[2 * n + 1 - core], held_core.at[n], sems_c.at[0, n], sems_c.at[1, n], mate) for n in range(2)
    ]
    result[...] = stream + scale * branch
    grad_stream[...] = value
    traffic.done(result, grad_stream)
    traffic.ready(1)
    for copy in copies_t:
        copy.wait()
    time_side, spec_side = (kept[6], kept[1], kept[7]), (kept[8], kept[4], kept[9])
    back_time(spec_side, kept, totals, back_t, mix_t, ds_t, query, upstream_ref, grad_k, grad_v)
    keep_keys(False, ds_f, grad_k, grad_v, (0, LANES), grad_k.shape[1], group, block_f)
    for n, copy in enumerate(copies):
        copy.wait()
        made = grads[2 * n + core].astype(F32) + held_core[n].astype(F32)
        first = n * rows_half
        turn_in[first : first + rows_turn] = made.astype(BF)
        if rows_half > rows_turn:
            turn_in[first + rows_turn : first + rows_half] = jnp.zeros((rows_half - rows_turn, width), BF)
    halving = Halving(turn_in, turn_stage, turn_in, sems_h, parts_turn)
    halving.start()
    prepare_queries(kept[3], totals[1], query)
    scatter = Scatter(terms_f, held_f, sems_q)
    size_t = kept[6].shape[0]
    for step, n in enumerate((across, far, mate, me)):
        lanes = lanes_of(n, block_f)
        if step < 3:
            copies_f[step].wait()
        prepare_upstream(back_f[n], mix_f[n], upstream_ref, lanes)
        if step == 2:
            scatter.middle()
        for head in range(2):
            back_unit(head, lanes, step == 0, time_side, query, upstream_ref, ds_f, grad_k, grad_v)
        terms_f[n] = mul(backward[1, 1], ds_f[:, lanes], NN).astype(BF)
        if step == 1:
            scatter.start_far()
        if step == 2:
            scatter.start_mate()
    keep_keys(True, ds_t, grad_k, grad_v, (0, LANES), size_t, group, block_t)
    for g in range(group):
        terms_t[g] = mul(backward[1, 0], ds_t[:, g * block_t : (g + 1) * block_t], NN).astype(BF)
    scatter_t = Scatter(terms_t, held_t, sems_p)
    scatter_t.start()
    halving.finish()
    halving.start()
    scatter_t.middle()
    store_rows(grads_in, ((ds_t, time_all), (ds_f, spec_all)))
    grad_norm[:, :LANES] = scatter_t.finish()
    grad_norm[:, LANES:] = scatter.finish()
    halving.finish()
    while halving.at < halving.steps - 1:
        halving.start()
        halving.finish()
    for n, (first, rows) in enumerate(halving.state):
        turn_part[n * rows : (n + 1) * rows] = turn_in[rows_of(first, rows), :]


def store_rows(target, streams):
    start = 0
    for n, (ds, whole) in enumerate(streams):
        for block in range(3):
            total = row_gradients(ds, whole, slice(block * LANES, (block + 1) * LANES))
            for head in range(2):
                target[start : start + HD] = total[head * HP : head * HP + HD].astype(BF)
                start += HD
        made = row_sums(ds, n)
        sums = made if n == 0 else sums + made
    target[start : start + 16] = sums.astype(BF)


def row_sums(ds, n):
    row = lax.broadcasted_iota(jnp.int32, (16, ds.shape[1]), 0)
    return mul((row == n).astype(BF), ds[...], NT)


def store_head(target, head, ds, whole):
    tiles = whole.shape[1] // LANES
    count = 3 * HD + 16
    for block in range(3):
        base = block * LANES + head * HP
        total = row_gradients(ds, whole, slice(base, base + HP))[:HD].astype(BF)
        for n in range(tiles):
            start = n * count + block * HD
            target[start : start + HD] = total[:, n * LANES : (n + 1) * LANES]
    sums = row_sums(ds, 0).astype(BF)
    for n in range(tiles):
        target[n * count + 3 * HD : (n + 1) * count] = sums[:, n * LANES : (n + 1) * LANES]
    if target.shape[0] > tiles * count:
        target[tiles * count :] = jnp.zeros_like(target[tiles * count :])


def load_head(target, tiles):
    count = 3 * HD + 16
    return jnp.concatenate([target[n * count : (n + 1) * count] for n in range(tiles)], axis=1)


def fourth_kernel(
    parts_turn, parts_in, parts_out, traffic, grad_norm, grad_in, time_y, spec_y, time_x, spec_x, in_t, in_f,
    w_out, cols, time_all, spec_all, backward, mix_t, mix_f, *rest,
):
    kept, totals = rest[:10], rest[10:12]
    turn_part, cross_in, attn_in, attn_out, small = rest[12:17]
    stream_grad, grad_a, grad_b, grad_c, grad_d, packed, scalars = rest[17:24]
    (turn_in, turn_stage, turn_out, turn_far, turn, cross, late_a, late_b, out, cross_one, late_a_one, late_b_one, out_one,
     cross_two, out_two, late_a_two, late_b_two, grads, out_t, out_f, back_t, back_f, terms_t, terms_f, held_t, held_f, held_two,
     ds_t, ds_f, query, upstream_ref, grad_k, grad_v, pieces, sems_q, sems_two, sems_three, sems_t, sems_f, sems_p, sems_y, sems_s,
     sems_turn, sems_cross, sems_a, sems_b, sems_out) = rest[24:]
    me, mate, across, far = places()
    size = lax.axis_size("dp")
    greet((mate, across, far), [lax.rem(lax.axis_index("dp") + n, size) for n in range(1, size)])
    group, local, block_t = mix_t.shape
    block_f, width = mix_f.shape[2], w_out.shape[2]

    def both(first, stage, last, sems, cut):
        return Chain(Halving(first, stage, last, sems.at[0], cut), Doubling(last, sems.at[1], cut))

    rest_parts = [segment_after(part) for part in parts_turn]
    rows = turn_part.shape[0] // len(parts_turn)
    for n, (first, count, _) in enumerate(rest_parts):
        turn_in[rows_of(first, rows), :] = turn_part[n * rows : (n + 1) * rows]
    rows_cross, rows_out = cross_in.shape[0], grads.shape[1]
    cross_one[:rows_cross] = cross_in[...]
    if cross_one.shape[0] > rows_cross:
        cross_one[rows_cross:] = jnp.zeros_like(cross_one[rows_cross:])
    chain_turn = Chain(
        Halving(turn_in, turn_stage, turn_out, sems_s, rest_parts),
        Chips(turn_out, turn_far, turn, sems_y, parts_turn), Doubling(turn, sems_turn, parts_turn[: len(parts_turn) // 2]),
    )
    chain_cross = both(cross_one, cross_two, cross, sems_cross, parts_in)
    chain_out = both(out_one, out_two, out, sems_out, parts_out)
    chain_a = Chain(Direct(late_a_one, late_a_two, late_a, sems_a))
    chain_b = Chain(Direct(late_b_one, late_b_two, late_b, sems_b))
    chain_turn.advance()
    chain_cross.advance()
    unit, scale_inv = norm_parts(jnp.concatenate([time_y[...], spec_y[...]], axis=1))
    value = grad_in[...] + norm_back(unit, scale_inv, grad_norm[...])
    traffic.ready(0)
    weights = (whole_weight(w_out, 0, local), whole_weight(w_out, 1, local))
    mixed_gradients(value, weights, (cols[:, 14:15], cols[:, 15:16]), (out_t, out_f))
    copies_t = send_blocks(out_t, back_t, sems_t)
    copies_f = send_blocks(out_f, back_f, sems_f)
    output_gradients(value, (in_t, in_f), grads, 0)
    scatter = Scatter(grads, held_two, sems_two)
    scatter.start()
    stream_grad[...] = value
    traffic.ready(1)
    for copy in copies_t:
        copy.wait()
    scatter.middle()
    time_side, spec_side = (kept[6], kept[1], kept[7]), (kept[8], kept[4], kept[9])
    size_t, size_f = kept[6].shape[0], kept[8].shape[0]
    back_time(time_side, kept, totals, back_t, mix_t, ds_t, query, upstream_ref, grad_k, grad_v)
    keep_keys(True, ds_t, grad_k, grad_v, (0, LANES), size_t, group, block_t)
    for g in range(group):
        terms_t[g] = mul(backward[0, 0], ds_t[:, g * block_t : (g + 1) * block_t], NN).astype(BF)
    chain_cross.advance()
    out_one[:rows_out] = scatter.finish().astype(BF)
    store_rows(out_one.at[rows_out:], ((ds_t, time_all),))
    rows_used = rows_out + 6 * HD + 16
    if out_one.shape[0] > rows_used:
        out_one[rows_used:] = jnp.zeros_like(out_one[rows_used:])
    chain_out.advance()
    prepare_queries(kept[3], totals[1], query)
    order = ((me, None), (mate, 2), (across, 0), (far, 1))
    moves = (
        (chain_turn, (0, 2, 4, 6)), (chain_cross, (1, 3, 5, 7)), (chain_out, (1, 3, 5, 7)), (chain_a, (6,)),
    )
    for head in range(2):
        for step, (n, arrival) in enumerate(order):
            lanes = lanes_of(n, block_f)
            if head == 0:
                if arrival is not None:
                    copies_f[arrival].wait()
                prepare_upstream(back_f[n], mix_f[n], upstream_ref, lanes)
            back_unit(head, lanes, step == 0, spec_side, query, upstream_ref, ds_f, grad_k, grad_v)
            for chain, when in moves:
                if head * 4 + step in when:
                    chain.advance()
        keep_keys(False, ds_f, grad_k, grad_v, (head * HP, (head + 1) * HP), size_f, group, block_f)
        if head == 0:
            store_head(late_a_one, 0, ds_f, spec_all)
            chain_a.advance()
    scatter_t = Scatter(terms_t, held_t, sems_three)
    scatter = Scatter(terms_f, held_f, sems_q)
    store_head(late_b_one, 1, ds_f, spec_all)
    chain_b.advance()
    for step, n in enumerate((far, across, mate, me)):
        terms_f[n] = mul(backward[0, 1], ds_f[:, lanes_of(n, block_f)], NN).astype(BF)
        if step == 0:
            scatter.start_far()
    scatter.middle()
    scatter.start_mate()
    scatter_t.start()
    scatter_t.middle()
    chains = (chain_turn, chain_cross, chain_out, chain_a)
    for chain in chains:
        chain.advance()
    traffic.ready(2)
    unit, scale_inv = norm_parts(jnp.concatenate([time_x[...], spec_x[...]], axis=1))
    chain_b.advance()
    for chain in chains:
        chain.complete()
    squares = jnp.zeros((1, width), F32)
    packed_rows = [jnp.zeros((1, width), F32) for _ in range(19)]
    tiles = width // LANES

    def add_squares(total, gradient):
        return total + jnp.sum(gradient * gradient, axis=0, keepdims=True)

    def turned(sums):
        return jnp.concatenate([sums, jnp.zeros((LANES - 16, width), F32)], axis=0).T

    def rows_done(squares, pick, plain, sums, lane, block):
        index, group = pick
        column = jnp.concatenate(
            [
                sums[head][block * LANES + head * HP : block * LANES + head * HP + HD, lane : lane + 1]
                for head in range(2)
            ],
            axis=0,
        )
        row = norm_rows[index][group]
        gradient = plain * small[row : row + 1, :] + column * small[row + 1 : row + 2, :]
        grad_a[index, group] = gradient.astype(BF)
        weight = attn_in[index, group]
        packed_rows[row] += jnp.sum(weight * plain, axis=0, keepdims=True)
        packed_rows[row + 1] += jnp.sum(weight * column, axis=0, keepdims=True)
        return add_squares(squares, gradient)

    rows = cross[: 12 * HD + 16].astype(F32)
    sums = (turned(rows[12 * HD :]),) * 2
    for stream, picks in enumerate(picks_of(True)):
        for block, pick in enumerate(picks):
            start = (stream * 6 + block * 2) * HD
            squares = rows_done(squares, pick, rows[start : start + local], sums, stream, block)
    rows = out[rows_out : rows_out + 6 * HD + 16].astype(F32)
    sums = (turned(rows[6 * HD :]),) * 2
    for block, pick in enumerate(picks_of(False)[0]):
        squares = rows_done(squares, pick, rows[block * local : (block + 1) * local], sums, 0, block)
    for index in range(4):
        if index < 2:
            plain = out[index * local : (index + 1) * local].astype(F32)
        else:
            start = 2 * width + (index - 2) * local
            plain = turn[start : start + local].astype(F32)
        gradient = plain * small[14 + index : 15 + index, :]
        grad_b[index] = gradient.astype(BF)
        squares = add_squares(squares, gradient)
        packed_rows[14 + index] += jnp.sum(attn_out[index] * plain, axis=0, keepdims=True)
    for target, start in ((grad_c, 0), (grad_d, width)):
        target[...] = turn[start : start + width]
        squares = add_squares(squares, turn[start : start + width].astype(F32))
    smalls = turn[2 * width + 2 * local : 2 * width + 2 * local + 16].astype(F32)
    for n, row in enumerate((12, 13, 18)):
        packed_rows[row] += smalls[n : n + 1]
    traffic.done(grad_b, grad_c, grad_d)
    chain_b.advance()
    halves = [load_head(late, tiles).astype(F32) for late in (late_a, late_b)]
    sums = [turned(half[3 * HD :]) for half in halves]
    for block, pick in enumerate(picks_of(False)[1]):
        plain = jnp.concatenate([half[block * HD : (block + 1) * HD] for half in halves], axis=0)
        squares = rows_done(squares, pick, plain, sums, 0, block)
    pieces[me] = jnp.concatenate(packed_rows + [squares] + [jnp.zeros((4, width), F32)], axis=0)
    copies = [
        push(pieces.at[me], pieces.at[me], sems_p.at[0, n], sems_p.at[1, n], other)
        for n, other in enumerate((across, far, mate))
    ]
    traffic.done(grad_a)
    scaled = jnp.concatenate([scatter_t.finish(), scatter.finish()], axis=1)
    stream_grad[...] = stream_grad[...] + norm_back(unit, scale_inv, scaled)
    traffic.done(stream_grad)
    for copy in copies:
        copy.wait()
    total = pieces[0]
    for n in range(1, pieces.shape[0]):
        total = total + pieces[n]
    packed[...] = total
    row = lax.broadcasted_iota(jnp.int32, total.shape, 0)
    every = jnp.where(row < 19, total * total, jnp.where(row == 19, total, 0.0))
    norm = jnp.sqrt(jnp.sum(jnp.sum(every, axis=0, keepdims=True), axis=1, keepdims=True))
    factor = jnp.minimum(1.0, clip_level / norm)
    lane = lax.broadcasted_iota(jnp.int32, scalars.shape, 1)
    scalars[...] = jnp.where(lane == 0, norm, factor)


def adam_parts(weight, first_moment, second_moment, gradient, step_rate, decay_rate):
    first_new = beta_first * first_moment + (1.0 - beta_first) * gradient
    second_new = beta_second * second_moment + (1.0 - beta_second) * gradient * gradient
    first_fix = 1.0 - beta_first**STEP
    second_fix = 1.0 - beta_second**STEP
    direction = (first_new * (1.0 / first_fix)) / (jnp.sqrt(second_new * (1.0 / second_fix)) + adam_eps)
    return (weight - step_rate * (direction + decay_rate * weight), first_new, second_new)


last_order = (0, 1, 2, 3)


def last_kernel(live, traffic, scalars, packed, small, small_m, small_v, result, stream_grad, *refs):
    held, outs = refs[:16], refs[16:28]
    small_outs, (time_out, spec_out, time_grad, spec_grad, shift_gradient, norm) = refs[28:31], refs[31:37]
    sems_out = refs[37]
    rates = (rate_matrix, rate_output, rate_matrix, rate_matrix)
    factor = scalars[:, 1:2]
    gradient = packed[: small.shape[0]] * factor
    made = adam_parts(small[...], small_m[...], small_v[...], gradient, rate_small, 0.0)
    for target, value in zip(small_outs, made):
        target[...] = value
    shift_gradient[...] = gradient[13:14].reshape(-1)
    norm[...] = scalars[:, 0:1]
    leaving = []
    for place, n in enumerate(last_order):
        traffic.ready(place)
        gradient, weight, first_moment, second_moment = held[4 * n : 4 * n + 4]
        made = adam_parts(
            weight[...], first_moment[...], second_moment[...], gradient[...].astype(F32) * factor, rates[n], decay_matrix
        )
        for m, (target, value) in enumerate(zip((weight, first_moment, second_moment), made)):
            target[...] = value
            leaving.append(pltpu.make_async_copy(target, outs[3 * n + m], sems_out.at[3 * n + m]))
            leaving[-1].start()
        if place == 2:
            traffic.ready(4)
            for source, one, two in ((result, time_out, spec_out), (stream_grad, time_grad, spec_grad)):
                one[...] = source[:, :LANES].T[:live].reshape(live, 1, -1)
                two[0] = source[:, LANES:].T
                traffic.done(one, two)
    for copy in leaving:
        copy.wait()


def shards(
    time_in, spec_in, rate_flags, band_limits, time_cot, spec_cot, attn_in, attn_out, ffn_in, ffn_out, small,
    attn_in_m, attn_in_v, attn_out_m, attn_out_v, ffn_in_m, ffn_in_v, ffn_out_m, ffn_out_v, small_m, small_v,
):
    group, size = lax.axis_size("mp"), lax.axis_size("dp")
    live = time_in.shape[1]
    count = -(-live // 16) * 16
    block_t, block_f = LANES, spec_in.shape[1]
    width, local, part = time_in.shape[2], attn_in.shape[2], ffn_in.shape[1]
    lanes = block_t + block_f
    size_t, size_f, rows_t = group * block_t, group * block_f, group * count

    whole = (shape_of((group, width, block_t), BF), shape_of((group, width, block_f), BF))
    stream = (shape_of((width, block_t), F32), shape_of((width, block_f), F32))
    mix = (shape_of((group, local, block_t), BF), shape_of((group, local, block_f), BF))
    kept_shapes = tuple(
        shape_of(s, BF)
        for s in [(LANES, size_t)] + [(LANES, rows_t)] * 2 + [(LANES, size_f)] * 3 + [(rows_t, LANES)] * 2
        + [(size_f, LANES)] * 2
    ) + (shape_of((2, size_t), F32), shape_of((2, size_f), F32))
    packed_weights = (2, 3 * LANES, width)
    score = pltpu.VMEM((2, size_f, max(size_t, block_f)), F32)
    smem = pl.BlockSpec(memory_space=pltpu.SMEM)

    rows_w, parts_w = cut_parts(width, size, 3)
    rows_ffn, parts_ffn = cut_parts(2 * width, size, 6)
    bits = len(parts_w[0][2])
    count_w, count_ffn = len(parts_w), len(parts_ffn)
    made = call(
        functools.partial(forward_kernel, live, parts_w, parts_ffn), "forward",
        (stream + whole + mix + mix + kept_shapes) * 2 + (
            shape_of((2, 2, width, 3 * LANES), BF), shape_of((group, rows_w, width), BF),
            shape_of((group, rows_ffn, width), BF), shape_of((width, LANES), F32),
        ),
        (time_in, spec_in, rate_flags, band_limits, attn_in, attn_out, ffn_in, ffn_out, small),
        [
            pltpu.VMEM(packed_weights, BF), pltpu.VMEM((2, 3 * LANES, 1), F32),
            pltpu.VMEM(packed_weights, BF), pltpu.VMEM((2, 3 * LANES, 1), F32), pltpu.VMEM((1, size_f), F32),
            pltpu.VMEM((LANES, width), F32), score, pltpu.VMEM((2, 2, HP, block_f), F32), pltpu.VMEM((2, 2, block_f), F32),
            dma(6), dma(2, 6), dma(2, 3), dma(2, 3), dma(2, count_w), dma(2, count_w, bits), dma(2, 1), dma(2, 1),
            dma(2, count_ffn), dma(6), dma(2, 6), dma(2, 3), dma(2, 3), dma(2, count_ffn, bits), dma(2, 1), dma(2, 1),
        ],
        0, specs={2: smem, 3: smem}, late=((4,),),
        early=tuple(range(24)) + tuple(range(28, 38)) + (40, 41, 43),
    )
    (time_x, spec_x, time_all, spec_all, mix_t, mix_f, all_t, all_f), kept = made[:8], made[8:20]
    (time_y, spec_y, time_all_y, spec_all_y, mix_t_y, mix_f_y, all_t_y, all_f_y), kept_y = made[20:28], made[28:40]
    backward, w_out, w_ffn, cols = made[40:]

    rows_turn, rows_in = width + part + 2 * local + 16, 6 * local + 16
    back_scratch = [
        pltpu.VMEM((3 * LANES, size_t), BF), pltpu.VMEM((3 * LANES, size_f), BF),
        pltpu.VMEM((2, LANES, size_f), BF), pltpu.VMEM((2, LANES, size_f), BF),
        pltpu.VMEM((LANES, size_f), F32), pltpu.VMEM((LANES, size_f), F32),
    ]
    mixes = [pltpu.VMEM(m.shape, BF) for m in mix + mix]
    rows_pair, parts_turn = cut_parts(rows_turn, size, 2)
    parts_turn = parts_turn + [(first + rows_pair, rows, order) for first, rows, order in parts_turn]
    pair = pltpu.VMEM((2 * rows_pair, width), BF)
    terms = [pltpu.VMEM((group, width, block_t), BF), pltpu.VMEM((group, width, block_f), BF)]
    result, grad_stream, turn_part, cross_in, grad_norm = call(
        functools.partial(third_kernel, live, parts_turn), "third",
        (
            shape_of((width, lanes), F32), shape_of((width, lanes), F32), shape_of((4 * rows_pair // size, width), BF),
            shape_of((rows_in, width), BF), shape_of((width, lanes), F32),
        ),
        (
            all_t_y, all_f_y, time_y, spec_y, w_out, w_ffn, cols, time_cot, spec_cot,
            time_all_y, spec_all_y, backward, mix_t_y, mix_f_y,
        ) + tuple(kept_y),
        [pltpu.VMEM((group, rows_turn, width), BF)] + mixes + [pltpu.VMEM((LANES, width), F32)] + terms + terms + [
            pltpu.VMEM((2, rows_turn, width), BF), pair, pair,
            pltpu.VMEM((group, part, lanes), BF), pltpu.VMEM((group, part, lanes), BF),
        ] + back_scratch + [dma(2, 3), dma(2, 3), dma(2, 3), dma(2, 3), dma(2, 2), dma(2, 4, bits)], 2,
        late=((5, 7, 8), tuple(range(9, 26))), early=(0, 1),
    )

    rows_sum, parts_in = cut_parts(rows_in, size, 5)
    rows_out, parts_out = cut_parts(5 * local + 16, size, 4)
    rows_late, _ = cut_parts((width // LANES) * (3 * HD + 16), size, 1)
    sums, late, outs = (
        pltpu.VMEM(shape, BF) for shape in ((rows_sum, width), (rows_late, LANES), (rows_out, width))
    )
    pieces = pltpu.VMEM((size - 1, rows_late // size, LANES), BF)
    stream_grad, grad_a, grad_b, grad_c, grad_d, packed, scalars = call(
        functools.partial(fourth_kernel, parts_turn, parts_in, parts_out), "fourth",
        (
            shape_of((width, lanes), F32), shape_of(attn_in.shape, BF), shape_of(attn_out.shape, BF),
            shape_of(ffn_in.shape, BF), shape_of(ffn_out.shape, BF), shape_of((24, width), F32), shape_of((1, LANES), F32),
        ),
        (
            grad_norm, grad_stream, time_y, spec_y, time_x, spec_x, all_t, all_f, w_out, cols,
            time_all, spec_all, backward, mix_t, mix_f,
        ) + tuple(kept) + (turn_part, cross_in, attn_in, attn_out, small),
        [pair, pair, pair, pltpu.VMEM((rows_pair // size, width), BF), pltpu.VMEM((rows_pair, width), BF)] + [sums, late, late, outs] * 2 + [
            sums, outs, pieces, pieces, pltpu.VMEM((group, 2 * local, width), BF)] + mixes + terms + terms + [pltpu.VMEM((4, 2 * local, width), BF)]
        + back_scratch + [
            pltpu.VMEM((group, 24, width), F32), dma(2, 3), dma(2, 3), dma(2, 3), dma(2, 3), dma(2, 3), dma(2, 3), dma(2, 2), dma(2, 4, 1),
            dma(2, 2, bits), dma(2, 2, 5, bits), dma(2, 2, size - 1), dma(2, 2, size - 1), dma(2, 2, 4, bits),
        ], 3,
        late=((8, 6, 7), tuple(range(10, 27)), (4, 5, 29, 30, 31)), early=(0, 1, 2, 3, 4),
    )

    ins, outs = [], []
    for gradient, weight, first_moment, second_moment in (
        (grad_a, attn_in, attn_in_m, attn_in_v), (grad_b, attn_out, attn_out_m, attn_out_v),
        (grad_c, ffn_in, ffn_in_m, ffn_in_v), (grad_d, ffn_out, ffn_out_m, ffn_out_v),
    ):
        flat = (weight.size // width, width)
        ins += [value.reshape(flat) for value in (gradient, weight, first_moment, second_moment)]
        outs += [shape_of(flat, F32)] * 3
    outs += [shape_of(small.shape, F32)] * 3
    outs += [shape_of((live, 1, width), F32), shape_of((1, block_f, width), F32)] * 2
    outs += [shape_of((width,), F32), shape_of((1, 1), F32)]
    made = call(
        functools.partial(last_kernel, live), "last", outs, (scalars, packed, small, small_m, small_v, result, stream_grad, *ins),
        [dma(12)], None, late=tuple(tuple(range(7 + 4 * n, 11 + 4 * n)) for n in last_order) + ((5, 6),),
        early=tuple(range(15, 19)), direct=tuple(range(12)),
    )
    updated = [
        value.reshape(weight.shape)
        for value, weight in zip(made[:15], [w for w in (attn_in, attn_out, ffn_in, ffn_out, small) for _ in range(3)])
    ]
    time_out, spec_out, time_grad, spec_grad, shift_gradient, norm = made[15:]
    time_out, time_grad = (jnp.swapaxes(value, 0, 1) for value in (time_out, time_grad))
    return (time_out, spec_out, time_grad, spec_grad, norm[0, 0], *updated, shift_gradient)


def solution(mesh):
    tokens, copied = P("dp", "mp", None), P()
    a, b, c, d = P(None, None, "mp", None), P(None, "mp", None), P(None, "mp"), P("mp", None)
    return jax.shard_map(
        shards,
        mesh=mesh,
        in_specs=(
            tokens, tokens, P("dp"), P("dp"), tokens, tokens, a, b, c, d, copied,
            a, a, b, b, c, c, d, d, copied, copied,
        ),
        out_specs=(
            tokens, tokens, tokens, tokens, copied,
            a, a, a, b, b, b, c, c, c, d, d, d, copied, copied, copied, copied,
        ),
        check_vma=False,
    )
```

```python
import functools
import math

import jax
import jax.numpy as jnp
from jax import lax
from jax.experimental import pallas as pl
from jax.experimental.pallas import tpu as pltpu
from jax.sharding import PartitionSpec as P

HD = 48
HP = 64
LANES = 128
FRAMES = 256
STEP = 10
BF = jnp.bfloat16
F32 = jnp.float32
NN = ((1,), (0,))
NT = ((1,), (1,))
TN = ((0,), (0,))
MESH = pl.DeviceIdType.MESH

norm_eps = 1e-05
clip_level = 100.0
beta_first = 0.9
beta_second = 0.95
adam_eps = 1e-08
decay_matrix = 0.1
rate_matrix = 0.05
rate_output = 0.5
rate_small = 0.5
masked_score = -1000000000.0
score_scale = HD ** (-0.5)
log_two = math.log(2.0)
query_scale = score_scale / log_two
vmem_limit = 58 * 2**20
AUX = HD
MASK_ROW = HD + 3
norm_rows = ((0, 0, 0), (2, 2, 2), (4, 6, 6), (8, 10, 10))


def mul(left, right, dims):
    return lax.dot_general(left, right, (dims, ((), ())), preferred_element_type=F32)


def dma(*shape):
    return pltpu.SemaphoreType.DMA(shape)


def vmem():
    return pl.BlockSpec(memory_space=pltpu.VMEM)


def shape_of(shape, kind):
    return jax.ShapeDtypeStruct(shape, kind)


class Traffic:
    def __init__(self):
        self.loads, self.stores, self.leaving = [], {}, []

    def ready(self, group):
        for copy in self.loads[group]:
            copy.wait()

    def done(self, *refs):
        for ref in refs:
            copy = self.stores.pop(id(ref))
            copy.start()
            self.leaving.append(copy)

    def finish(self):
        for copy in list(self.stores.values()):
            copy.start()
            self.leaving.append(copy)
        for copy in self.leaving:
            copy.wait()


def call(kernel, name, outs, args, scratch, collective, specs=None, late=(), early=(), direct=()):
    ins, count = len(args), len(args) + len(outs) + len(scratch)
    flat = [n for group in late for n in group]
    extra = [pltpu.VMEM(args[n].shape, args[n].dtype) for n in flat]
    extra += [pltpu.VMEM(outs[n].shape, outs[n].dtype) for n in early]
    extra += [dma(max(len(flat), 1)), dma(max(len(early), 1))]

    def body(*refs):
        refs, held = list(refs[:count]), refs[count:]
        traffic = Traffic()
        place = 0
        for group in late:
            copies = []
            for n in group:
                copies.append(pltpu.make_async_copy(refs[n], held[place], held[-2].at[place]))
                copies[-1].start()
                refs[n] = held[place]
                place += 1
            traffic.loads.append(copies)
        for m, n in enumerate(early):
            ref = held[place + m]
            traffic.stores[id(ref)] = pltpu.make_async_copy(ref, refs[ins + n], held[-1].at[m])
            refs[ins + n] = ref
        kernel(traffic, *refs)
        traffic.finish()

    anywhere = pl.BlockSpec(memory_space=pl.ANY)
    remote = {} if collective is None else {"collective_id": collective, "has_side_effects": True}
    return pl.pallas_call(
        body,
        name=name,
        out_shape=outs,
        in_specs=[anywhere if n in flat else (specs or {}).get(n, vmem()) for n in range(ins)],
        out_specs=tuple(anywhere if n in early or n in direct else vmem() for n in range(len(outs))),
        scratch_shapes=list(scratch) + extra,
        compiler_params=pltpu.CompilerParams(vmem_limit_bytes=vmem_limit, **remote),
    )(*args)


def places():
    me = lax.axis_index("mp")
    mate = me + 1 - 2 * lax.rem(me, 2)
    across = lax.rem(me + 2, 4)
    far = lax.rem(mate + 2, 4)
    return me, mate, across, far


def greet(others, partners=()):
    barrier = pltpu.get_barrier_semaphore()
    for other in others:
        pl.semaphore_signal(barrier, inc=1, device_id={"mp": other}, device_id_type=MESH)
    for partner in partners:
        pl.semaphore_signal(barrier, inc=1, device_id={"dp": partner}, device_id_type=MESH)
    pl.semaphore_wait(barrier, len(others) + len(partners))


def push_to(source, target, send, recv, device):
    copy = pltpu.make_async_remote_copy(
        source, target, send, recv, device_id=device, device_id_type=MESH
    )
    copy.start()
    return copy


def push(source, target, send, recv, device):
    return push_to(source, target, send, recv, {"mp": device})


class Gather:
    def __init__(self, ref, sems, lanes=None):
        self.ref, self.sems, self.lanes = ref, sems, lanes

    def block(self, index):
        return self.ref.at[index] if self.lanes is None else self.ref.at[index, :, self.lanes]

    def start(self):
        me, mate, across, far = places()
        own = self.block(me)
        self.first = push(own, own, self.sems.at[0], self.sems.at[1], across)
        self.second = push(own, own, self.sems.at[2], self.sems.at[3], mate)
        return self

    def near(self):
        self.second.wait_recv()

    def finish(self, near=False):
        self.relay()
        self.end(near)

    def relay(self):
        me, mate, across, far = places()
        self.first.wait_recv()
        other = self.block(across)
        self.third = push(other, other, self.sems.at[4], self.sems.at[5], mate)

    def end(self, near=False):
        self.first.wait_send()
        if near:
            self.second.wait_send()
        else:
            self.second.wait()
        self.third.wait()


def send_block(source, target, sems, n, other):
    me, mate, across, far = places()
    return push(source.at[other], target.at[me], sems.at[0, n], sems.at[1, n], other)


def send_blocks(source, target, sems):
    me, mate, across, far = places()
    copies = [send_block(source, target, sems, n, other) for n, other in enumerate((across, far, mate))]
    target[me] = source[me]
    return copies


class Scatter:
    def __init__(self, source, held, sems):
        self.source, self.held, self.sems = source, held, sems

    def start_far(self):
        me, mate, across, far = places()
        self.one = push(self.source.at[far], self.held.at[0], self.sems.at[0, 0], self.sems.at[1, 0], mate)

    def start_mate(self):
        me, mate, across, far = places()
        self.two = push(self.source.at[mate], self.held.at[1], self.sems.at[0, 1], self.sems.at[1, 1], mate)

    def start(self):
        self.start_far()
        self.start_mate()

    def middle(self):
        me, mate, across, far = places()
        self.one.wait()
        self.held[2] = (self.source[across].astype(F32) + self.held[0].astype(F32)).astype(BF)
        self.cross = push(self.held.at[2], self.held.at[3], self.sems.at[0, 2], self.sems.at[1, 2], across)

    def finish(self):
        me, mate, across, far = places()
        self.two.wait()
        total = self.source[me].astype(F32) + self.held[1].astype(F32)
        self.cross.wait()
        return total + self.held[3].astype(F32)


def norm_parts(stream):
    center = stream - jnp.mean(stream, axis=0, keepdims=True)
    scale_inv = lax.rsqrt(jnp.mean(center * center, axis=0, keepdims=True) + norm_eps)
    return center * scale_inv, scale_inv


def norm_back(unit, scale_inv, scaled):
    return scale_inv * (
        scaled
        - jnp.mean(scaled, axis=0, keepdims=True)
        - unit * jnp.mean(scaled * unit, axis=0, keepdims=True)
    )


def attend_blocks(
    places_in, block, keys, queries, values, score, write, after, span=None, keep=None, prior=None
):
    first, rows_k = span or (0, keys.shape[0])
    here, there = rows_of(first, rows_k), lanes_from(first, rows_k)
    row = lax.broadcasted_iota(jnp.int32, (LANES, block), 0)

    def make(n, head):
        query = queries[:, lanes_of(n, block)]
        own = (row < HP) if head == 0 else (row >= HP)
        score[head, :rows_k, :] = mul(keys[here, :], jnp.where(own, query, jnp.zeros_like(query)), NN)

    def finish(step, n, head):
        held = score[head, :rows_k, :]
        peak = jnp.max(held, axis=0, keepdims=True)
        shares = jnp.exp2(held - peak).astype(BF)
        mixed = mul(values[head * HP : (head + 1) * HP, there], shares, NN)
        if keep is not None:
            keep(step, head, mixed, peak)
            return
        if prior is not None:
            other, other_peak = prior(step, head)
            new_peak = jnp.maximum(peak, other_peak)
            mixed = mixed * jnp.exp2(peak - new_peak) + other * jnp.exp2(other_peak - new_peak)
            peak = new_peak
        total = mixed[AUX : AUX + 1, :]
        write(n, head, (mixed[:HD] * (1.0 / total)).astype(BF), peak + jnp.log2(total))

    make(places_in[0], 0)
    for step, n in enumerate(places_in):
        make(n, 1)
        finish(step, n, 0)
        if step + 1 < len(places_in):
            make(places_in[step + 1], 0)
        finish(step, n, 1)
        after(step, n)


def lanes_from(first, count):
    return pl.ds(first if isinstance(first, int) else pl.multiple_of(first, LANES), count)


def lanes_of(n, block):
    return pl.ds(n * block if isinstance(n, int) else pl.multiple_of(n * block, LANES), block)


def split_three(value):
    high = value.astype(BF)
    rest = value - high.astype(F32)
    middle = rest.astype(BF)
    return high, middle, (rest - middle.astype(F32)).astype(BF)


def with_rows(body, head, parts):
    row = lax.broadcasted_iota(jnp.int32, body.shape, 0) - head * HP
    out = jnp.where((row >= 0) & (row < HP), body.astype(F32), 0.0)
    for n, part in enumerate(parts):
        out = jnp.where(row == AUX + n, part.astype(F32), out)
    return out.astype(BF)


def back_unit(head, lanes, fresh, side, queries, upstream, grad_q, grad_k, grad_v):
    keys_rows, keys, values_rows = side
    rows_k = keys_rows.shape[0]
    own = slice(head * HP, (head + 1) * HP)
    shares = jnp.exp2(mul(keys_rows[...], queries[head, :, lanes], NN))
    inner = mul(values_rows[...], upstream[head, :, lanes], NN)
    grad_score = (shares * inner).astype(BF)
    shares = shares.astype(BF)
    grad_q[own, lanes] = (mul(keys[own, :], grad_score, NN) * score_scale).astype(BF)
    made_k = mul(queries[head, own, lanes], grad_score, NT)
    made_v = mul(upstream[head, own, lanes], shares, NT)
    grad_k[own, :rows_k] = made_k if fresh else grad_k[own, :rows_k] + made_k
    grad_v[own, :rows_k] = made_v if fresh else grad_v[own, :rows_k] + made_v


def prepare_queries(q, total, query):
    size = q.shape[1]
    for head in range(2):
        query[head, :, :size] = with_rows(q[...], head, split_three(-total[head : head + 1, :]))


def prepare_upstream(part, mixed, upstream, lanes):
    block = part.shape[1]
    for head in range(2):
        rows = slice(head * HD, (head + 1) * HD)
        inner = jnp.sum(part[rows].astype(F32) * mixed[rows].astype(F32), axis=0, keepdims=True)
        padded = jnp.concatenate(
            [part[rows], *split_three(-inner), jnp.zeros((HP - HD - 3, block), BF)], axis=0
        )
        other = jnp.zeros((HP, block), BF)
        both = [padded, other] if head == 0 else [other, padded]
        upstream[head, :, lanes] = jnp.concatenate(both, axis=0)


def back_time(side, kept, totals, back_t, mix_t, ds_t, query, upstream, grad_k, grad_v):
    group, _, block = mix_t.shape
    prepare_queries(kept[0], totals[0], query)
    for g in range(group):
        prepare_upstream(back_t[g], mix_t[g], upstream, lanes_of(g, block))
    for head in range(2):
        back_unit(head, slice(0, group * block), True, side, query, upstream, ds_t, grad_k, grad_v)


def spread_keys(ds, base, source, group, block):
    turned = source.T
    count, width = turned.shape[0] // group, turned.shape[1]
    for g in range(group):
        part = turned[g * count : (g + 1) * count]
        part = jnp.concatenate([part, jnp.zeros((block - count, width), F32)], axis=0)
        ds[base : base + width, g * block : (g + 1) * block] = part.T.astype(BF)


def keep_keys(time_keys, ds, grad_k, grad_v, rows, size, group, block):
    start, stop = rows
    key, value = grad_k[start:stop, :size] * log_two, grad_v[start:stop, :size]
    for base, made in ((LANES, key), (2 * LANES, value)):
        if time_keys:
            spread_keys(ds, base + start, made, group, block)
        else:
            ds[base + start : base + stop, :] = made.astype(BF)


def row_gradients(ds, whole, rows):
    group, _, block = whole.shape
    total = None
    for g in range(group):
        made = mul(ds[rows, g * block : (g + 1) * block], whole[g], NT)
        total = made if total is None else total + made
    return total


def bit_orders(size):
    bits = [1 << n for n in range(size.bit_length() - 1)]
    return bits, bits[1:2] + bits[:1] + bits[2:]


def cut_parts(count, size):
    tile = 16 * size
    tiles = -(-count // tile)
    cut = (tiles + 1) // 2 * tile
    rows = tiles * tile
    one, two = bit_orders(size)
    return rows, [(0, cut, one)] + ([(cut, rows - cut, two)] if rows > cut else [])


def partner_of(bit):
    index = lax.axis_index("dp")
    mine = lax.rem(index // bit, 2)
    return mine, index + bit * (1 - 2 * mine)


def segment_of(part):
    first, rows, bits = part
    for bit in bits:
        rows = rows // 2
        first = first + partner_of(bit)[0] * rows
    return first, rows


def rows_of(first, rows):
    return pl.ds(first if isinstance(first, int) else pl.multiple_of(first, 16), rows)


class Halving:
    def __init__(self, source, stage, target, sems, parts):
        self.source, self.stage, self.target, self.sems = source, stage, target, sems
        self.state = [list(part[:2]) for part in parts]
        self.orders = [part[2] for part in parts]
        self.full = [part[1] for part in parts]
        self.steps, self.at, self.copies = len(self.orders[0]), 0, []

    def start(self):
        self.copies = []
        for n, (first, rows) in enumerate(self.state):
            mine, partner = partner_of(self.orders[n][self.at])
            half = rows // 2
            place = self.held(n)
            self.copies.append(
                push_to(
                    self.source.at[rows_of(first + (1 - mine) * half, half)], self.stage.at[rows_of(place, half)],
                    self.sems.at[0, n, self.at], self.sems.at[1, n, self.at], {"dp": partner},
                )
            )

    def held(self, n):
        total = self.full[n]
        return sum(self.full[:n]) + total - (total >> self.at)

    def finish(self):
        into = self.target if self.at == self.steps - 1 else self.source
        for n, copy in enumerate(self.copies):
            first, rows = self.state[n]
            mine, partner = partner_of(self.orders[n][self.at])
            half = rows // 2
            here, there = rows_of(first + mine * half, half), rows_of(self.held(n), half)
            copy.wait()
            into[here, :] = (self.source[here, :].astype(F32) + self.stage[there, :].astype(F32)).astype(BF)
            self.state[n] = [first + mine * half, half]
        self.at += 1


class Doubling:
    def __init__(self, target, sems, parts):
        self.target, self.sems = target, sems
        self.state = [list(segment_of(part)) for part in parts]
        self.orders = [part[2][::-1] for part in parts]
        self.steps, self.at, self.copies = len(self.orders[0]), 0, []

    def start(self):
        self.copies = []
        for n, (first, rows) in enumerate(self.state):
            mine, partner = partner_of(self.orders[n][self.at])
            here = self.target.at[rows_of(first, rows)]
            self.copies.append(
                push_to(here, here, self.sems.at[0, n, self.at], self.sems.at[1, n, self.at], {"dp": partner})
            )

    def finish(self):
        for n, copy in enumerate(self.copies):
            first, rows = self.state[n]
            mine, partner = partner_of(self.orders[n][self.at])
            copy.wait()
            self.state[n] = [first - mine * rows, 2 * rows]
        self.at += 1


class Direct:
    steps = 2

    def __init__(self, source, stage, target, sems):
        self.source, self.stage, self.target, self.sems, self.at = source, stage, target, sems, 0
        self.size = lax.axis_size("dp")
        self.rows = source.shape[0] // self.size

    def piece(self, index):
        return rows_of(index * self.rows, self.rows)

    def start(self):
        index = lax.axis_index("dp")
        self.copies = []
        for n in range(1, self.size):
            other = lax.rem(index + n, self.size)
            if self.at == 0:
                source, target = self.source.at[self.piece(other)], self.stage.at[n - 1]
            else:
                source = target = self.target.at[self.piece(index)]
            self.copies.append(
                push_to(
                    source, target, self.sems.at[self.at, 0, n - 1], self.sems.at[self.at, 1, n - 1], {"dp": other}
                )
            )

    def finish(self):
        for copy in self.copies:
            copy.wait()
        if self.at == 0:
            here = self.piece(lax.axis_index("dp"))
            total = self.source[here, :].astype(F32)
            for n in range(self.size - 1):
                total = total + self.stage[n].astype(F32)
            self.target[here, :] = total.astype(BF)
        self.at += 1


class Across:
    steps = 1

    def __init__(self, source, target, sems, parts):
        self.source, self.target, self.sems, self.parts, self.at = source, target, sems, parts, 0

    def start(self):
        me, mate, across, far = places()
        self.copies = []
        for n, part in enumerate(self.parts):
            rows = rows_of(*segment_of(part))
            self.copies.append(
                push(self.source.at[rows], self.target.at[rows], self.sems.at[0, n], self.sems.at[1, n], across)
            )

    def finish(self):
        for copy in self.copies:
            copy.wait()
        self.at += 1


def segment_after(part):
    first, rows, bits = part
    for bit in bits[:-1]:
        rows = rows // 2
        first = first + partner_of(bit)[0] * rows
    return first, rows, bits[-1:]


class Chips:
    steps = 1

    def __init__(self, source, held, target, sems, parts):
        self.source, self.held, self.target, self.sems, self.at = source, held, target, sems, 0
        self.parts = parts[: len(parts) // 2]
        self.half = sum(part[1] for part in self.parts)

    def start(self):
        me, mate, across, far = places()
        chip = me // 2
        self.copies = []
        for n, part in enumerate(self.parts):
            first, rows = segment_of(part)
            self.copies.append(
                push(
                    self.source.at[rows_of(first + (1 - chip) * self.half, rows)],
                    self.held.at[n * rows : (n + 1) * rows], self.sems.at[0, n], self.sems.at[1, n], across,
                )
            )

    def finish(self):
        chip = places()[0] // 2
        for n, copy in enumerate(self.copies):
            copy.wait()
            first, rows = segment_of(self.parts[n])
            own = self.source[rows_of(first + chip * self.half, rows), :].astype(F32)
            total = own + self.held[n * rows : (n + 1) * rows].astype(F32)
            self.target[rows_of(first, rows), :] = total.astype(BF)
        self.at += 1


class Relay:
    steps = 1

    def __init__(self, whole, sems, blocks):
        self.whole, self.sems, self.blocks, self.at = whole, sems, blocks, 0

    def start(self):
        me, mate, across, far = places()
        self.copies = [
            push(self.whole.at[block], self.whole.at[block], self.sems.at[0, n], self.sems.at[1, n], mate)
            for n, block in enumerate(self.blocks)
        ]

    def finish(self):
        for copy in self.copies:
            copy.wait()
        self.at += 1


class Chain:
    def __init__(self, *stages):
        self.stages, self.now, self.flying = list(stages), 0, False

    def advance(self):
        if self.now == len(self.stages):
            return
        stage = self.stages[self.now]
        if self.flying:
            stage.finish()
            if stage.at == stage.steps:
                self.now += 1
                self.flying = False
                if self.now == len(self.stages):
                    return
                stage = self.stages[self.now]
        stage.start()
        self.flying = True

    def complete(self):
        while self.now < len(self.stages):
            self.advance()


def picks_of(cross):
    if cross:
        return ((2, 0), (3, 1), (3, 2)), ((3, 0), (2, 1), (2, 2))
    return ((0, 0), (0, 1), (0, 2)), ((1, 0), (1, 1), (1, 2))


def fold_weights(cross, attn_in, small, forward, offsets, backward):
    width = attn_in.shape[3]
    for stream, picks in enumerate(picks_of(cross)):
        blocks = []
        for block, (index, group) in enumerate(picks):
            row = norm_rows[index][group]
            weight = attn_in[index, group]
            folded = weight * small[row : row + 1, :]
            offset = jnp.sum(weight * small[row + 1 : row + 2, :], axis=1, keepdims=True)
            factor = query_scale if group == 0 else 1.0
            ones = (MASK_ROW,) if group == 0 else (AUX, AUX + 1, AUX + 2)
            spare = lax.broadcasted_iota(jnp.int32, (HP - HD, 1), 0) + HD
            marks = jnp.zeros((HP - HD, 1), F32)
            for one in ones:
                marks = jnp.where(spare == one, 1.0, marks)
            for head in range(2):
                rows = slice(head * HD, (head + 1) * HD)
                start = block * LANES + head * HP
                forward[stream, start : start + HD, :] = (folded[rows] * factor).astype(BF)
                forward[stream, start + HD : start + HP, :] = jnp.zeros((HP - HD, width), BF)
                offsets[stream, start : start + HD, :] = offset[rows] * factor
                offsets[stream, start + HD : start + HP, :] = marks
                blocks += [folded[rows], jnp.zeros((HP - HD, width), F32)]
        backward[stream] = jnp.concatenate(blocks, axis=0).T.astype(BF)


def project_time(live, time_all, forward, offsets, kept):
    qt, kt, vt, qf, kf, vf, kt_rows, vt_rows, kf_rows, vf_rows = kept
    group, _, block = time_all.shape
    row = lax.broadcasted_iota(jnp.int32, (LANES, block), 0)
    lane = lax.broadcasted_iota(jnp.int32, (LANES, block), 1)
    dead = jnp.where(lane < live, 0.0, masked_score)
    mask = jnp.where((row == MASK_ROW) | (row == MASK_ROW + HP), dead, 0.0)
    count = kt_rows.shape[0] // group
    for n in range(group):
        made = mul(forward[0], time_all[n], NN) + offsets[0]
        qt[:, n * block : (n + 1) * block] = made[:LANES].astype(BF)
        key, value = (made[LANES : 2 * LANES] + mask).astype(BF), made[2 * LANES :].astype(BF)
        lanes = slice(n * count, (n + 1) * count)
        kt_rows[lanes, :], vt_rows[lanes, :] = key.T[:count], value.T[:count]
    kt[...] = kt_rows[...].T
    vt[...] = vt_rows[...].T


def project_spec(n, spec_all, forward, offsets, bias, kept):
    qt, kt, vt, qf, kf, vf, kt_rows, vt_rows, kf_rows, vf_rows = kept
    block = spec_all.shape[2]
    lanes = lanes_of(n, block)
    row = lax.broadcasted_iota(jnp.int32, (LANES, block), 0)
    made = mul(forward[1], spec_all[n], NN) + offsets[1]
    qf[:, lanes] = made[:LANES].astype(BF)
    mask = jnp.where((row == MASK_ROW) | (row == MASK_ROW + HP), bias[:, lanes], 0.0)
    key, value = (made[LANES : 2 * LANES] + mask).astype(BF), made[2 * LANES :].astype(BF)
    kf[:, lanes], vf[:, lanes] = key, value
    kf_rows[lanes, :], vf_rows[lanes, :] = key.T, value.T


def time_attention(side, kept, totals, mix_t, all_t, sems, score):
    group, _, block = mix_t.shape
    copies = []

    def write(n, head, value, total):
        for g in range(group):
            mix_t[g, head * HD : (head + 1) * HD, :] = value[:, g * block : (g + 1) * block]
        totals[0][head : head + 1, :] = total

    def after(step, n):
        copies.extend(send_blocks(mix_t, all_t, sems))

    attend_blocks((0,), group * block, side[0], kept[0], side[1], score, write, after)
    return copies


def spec_attention(blocks, side, kept, totals, mix_f, all_f, sems, score, first, between, **part):
    block = mix_f.shape[2]
    copies = []

    def write(n, head, value, total):
        mix_f[n, head * HD : (head + 1) * HD, :] = value
        totals[1][head : head + 1, lanes_of(n, block)] = total

    def after(step, n):
        step += first
        if step < 3:
            copies.append(send_block(mix_f, all_f, sems, step, n))
        else:
            all_f[n] = mix_f[n]
        between(step)

    attend_blocks(blocks, block, side[0], kept[3], side[1], score, write, after, **part)
    return copies


def forward_kernel(
    live, parts, parts_ffn, traffic, time_in, spec_in, flags, limits, attn_in, attn_out, ffn_in, ffn_out, small,
    time_x, spec_x, time_all, spec_all, mix_t, mix_f, all_t, all_f, *rest,
):
    kept, totals = rest[:10], rest[10:12]
    time_y, spec_y, time_all_y, spec_all_y, mix_t_y, mix_f_y, all_t_y, all_f_y = rest[12:20]
    kept_y, totals_y = rest[20:30], rest[30:32]
    backward, weights, w_ffn, cols = rest[32:36]
    (forward, offsets, forward_two, offsets_two, bias, rows_t, score, part_mix, part_peak, sems_p, sems_q, sems_t, sems_f, sems_a, sems_d,
     sems_r, sems_s, sems_n, sems_p_two, sems_q_two, sems_t_two, sems_f_two, sems_m, sems_u, sems_v) = rest[36:]
    me, mate, across, far = places()
    greet((mate, across, far), [partner_of(bit)[1] for bit in parts[0][2]])
    width, local = ffn_in.shape[0], mix_t.shape[1]
    weights[me, :width] = attn_out[...].reshape(width, width).astype(BF)
    if weights.shape[1] > width:
        weights[me, width:] = jnp.zeros_like(weights[me, width:])
    w_ffn[me, :width] = ffn_in[...].astype(BF)
    w_ffn[me, width : 2 * width] = ffn_out[...].astype(BF)
    if w_ffn.shape[1] > 2 * width:
        w_ffn[me, 2 * width :] = jnp.zeros_like(w_ffn[me, 2 * width :])
    chain = Chain(
        Across(weights.at[me], weights.at[me], sems_a, parts), Doubling(weights.at[across], sems_d, parts),
        Relay(weights, sems_r, (across,)),
    )
    chain.advance()
    chain_ffn = Chain(
        Across(w_ffn.at[me], w_ffn.at[me], sems_n, parts_ffn), Doubling(w_ffn.at[across], sems_m, parts_ffn),
        Relay(w_ffn, sems_u, (across,)),
    )
    chain_ffn.advance()
    rows_t[...] = jnp.zeros_like(rows_t)
    rows_t[:live, :] = time_in[0].astype(F32)
    time_x[...] = rows_t[...].T
    time_all[me] = norm_parts(time_x[...])[0].astype(BF)
    gather_t = Gather(time_all, sems_p).start()
    block_f = mix_f.shape[2]
    halves = (slice(0, block_f // 2), slice(block_f // 2, block_f))
    gathers = []
    for n, part in enumerate(halves):
        spec_x[:, part] = spec_in[0, part, :].astype(F32).T
        spec_all[me, :, part] = norm_parts(spec_x[:, part])[0].astype(BF)
        gathers.append(Gather(spec_all, sems_q.at[n], part).start())
    own = Relay(weights, sems_s, (me,))
    own.start()
    own_ffn = Relay(w_ffn, sems_v, (me,))
    own_ffn.start()
    traffic.done(time_x, spec_x)
    traffic.ready(0)
    fold_weights(False, attn_in, small, forward, offsets, backward.at[0])
    bins = lax.broadcasted_iota(jnp.int32, bias.shape, 1) // FRAMES
    bias[...] = jnp.where((bins < limits[0]) | (flags[0] == 0), 0.0, masked_score)
    gather_t.finish()
    chain.advance()
    project_time(live, time_all, forward, offsets, kept)
    time_side, spec_side = (kept[6], kept[2]), (kept[8], kept[5])
    copies = time_attention(time_side, kept, totals, mix_t, all_t, sems_t, score)
    project_spec(me, spec_all, forward, offsets, bias, kept)
    chain.advance()
    fold_weights(True, attn_in, small, forward_two, offsets_two, backward.at[1])
    cols[...] = jnp.concatenate(
        [small[...], jnp.zeros((LANES - small.shape[0], small.shape[1]), F32)], axis=0
    ).T
    own.finish()
    own_ffn.finish()
    traffic.done(time_all, backward, cols)
    for gather in gathers:
        gather.near()
    project_spec(mate, spec_all, forward, offsets, bias, kept)
    chip, half = me // 2, 2 * block_f

    def keep(step, head, value, peak):
        part_mix[step, head] = value
        part_peak[step, head : head + 1] = peak

    def prior(step, head):
        return part_mix[step, head], part_peak[step, head : head + 1]

    attend_blocks(
        (mate, me), block_f, spec_side[0], kept[3], spec_side[1], score, None, lambda step, n: None,
        span=(chip * half, half), keep=keep,
    )
    for gather in gathers:
        gather.relay()
    for gather in gathers:
        gather.end(near=True)
    chain.advance()
    for n in (across, far):
        project_spec(n, spec_all, forward, offsets, bias, kept)
    traffic.done(spec_all, *kept)

    def between(step):
        if step in (0, 1, 2):
            chain.advance()
        if step == 2:
            chain_ffn.advance()

    copies += spec_attention((across, far), spec_side, kept, totals, mix_f, all_f, sems_f, score, 0, between)
    copies += spec_attention(
        (mate, me), spec_side, kept, totals, mix_f, all_f, sems_f, score, 2, between,
        span=((1 - chip) * half, half), prior=prior,
    )
    chain.complete()
    for copy in copies:
        copy.wait()
    traffic.done(mix_t, mix_f, all_t, all_f, *totals, weights)
    kept, totals = kept_y, totals_y
    time_y[...] = add_branch(joined(all_t), whole_weight(weights, 0, local), cols[:, 14:15], time_x[...])
    time_all_y[me] = norm_parts(time_y[...])[0].astype(BF)
    gather_t = Gather(time_all_y, sems_p_two).start()
    gathers = []
    for n, part in enumerate(halves):
        mixed = all_f[:, :, part].reshape(-1, block_f // 2)
        spec_y[:, part] = add_branch(mixed, whole_weight(weights, 1, local), cols[:, 15:16], spec_x[:, part])
        spec_all_y[me, :, part] = norm_parts(spec_y[:, part])[0].astype(BF)
        gathers.append(Gather(spec_all_y, sems_q_two.at[n], part).start())
    traffic.done(time_y, spec_y)
    chain_ffn.advance()
    gather_t.finish()
    project_time(live, time_all_y, forward_two, offsets_two, kept)
    project_spec(me, spec_all_y, forward_two, offsets_two, bias, kept)
    for gather in gathers:
        gather.relay()
    for gather in gathers:
        gather.end()
    chain_ffn.advance()
    time_side, spec_side = (kept[6], kept[2]), (kept[8], kept[5])
    copies = []
    for step, n in enumerate((across, far, mate, me)):
        if step < 3:
            project_spec(n, spec_all_y, forward_two, offsets_two, bias, kept)
        copies += spec_attention(
            (n,), time_side, kept, totals, mix_f_y, all_f_y, sems_f_two, score, step, lambda step: None
        )
    traffic.done(time_all_y, spec_all_y, *kept)
    chain_ffn.advance()
    copies += time_attention(spec_side, kept, totals, mix_t_y, all_t_y, sems_t_two, score)
    chain_ffn.complete()
    for copy in copies:
        copy.wait()


def whole_weight(weights, index, rows):
    part = weights[:, index * rows : (index + 1) * rows]
    return part.reshape(-1, part.shape[2])


def joined(mixed):
    part = mixed[...]
    return part.reshape(-1, part.shape[2])


def add_branch(mixed, w_out, scale, stream):
    return stream + scale * mul(w_out, mixed, TN)


def gelu_pair(values):
    share = 0.5 * (1.0 + lax.erf(values * (2.0**-0.5)))
    slope = share + values * (jnp.exp(-0.5 * values * values) * ((2.0 * math.pi) ** -0.5))
    return values * share, slope


def mixed_gradients(grad_stream, weights, scales, outgoing):
    for n, lanes in enumerate((slice(0, LANES), slice(LANES, None))):
        grad_mix = mul(weights[n], (scales[n] * grad_stream[:, lanes]).astype(BF), NN).astype(BF)
        group, width = outgoing[n].shape[:2]
        for g in range(group):
            outgoing[n][g] = grad_mix[g * width : (g + 1) * width]


def output_gradients(grad_stream, mixed, grads, start):
    for n, lanes in enumerate((slice(0, LANES), slice(LANES, None))):
        grad_out = mul(joined(mixed[n]), grad_stream[:, lanes].astype(BF), NT).astype(BF)
        group, width = mixed[n].shape[:2]
        for g in range(group):
            grads[g, start + n * width : start + (n + 1) * width] = grad_out[g * width : (g + 1) * width]


def third_kernel(
    live, parts_turn, traffic, in_t, in_f, time_x, spec_x, w_out, w_ffn, cols, time_dy, spec_dy,
    time_all, spec_all, backward, mix_t, mix_f, *rest,
):
    kept, totals = rest[:10], rest[10:12]
    result, grad_stream, turn_part, grads_in, grad_norm = rest[12:17]
    (grads, out_t, out_f, back_t, back_f, rows_t, terms_t, terms_f, held_t, held_f, held_core, turn_in, turn_stage, actives,
     grad_hiddens, ds_t, ds_f, query, upstream_ref, grad_k, grad_v, sems_p, sems_q, sems_t, sems_f, sems_c, sems_h) = rest[17:]
    me, mate, across, far = places()
    greet((mate, across, far), [partner_of(bit)[1] for bit in parts_turn[0][2]])
    group, local, block_t = mix_t.shape
    block_f, width = mix_f.shape[2], w_out.shape[2]
    w_first, w_second = w_ffn.at[:, :width], w_ffn.at[:, width : 2 * width]
    gain, shift, scale = cols[:, 12:13], cols[:, 13:14], cols[:, 18:19]
    weights = (whole_weight(w_out, 2, local), whole_weight(w_out, 3, local))
    scales = (cols[:, 16:17], cols[:, 17:18])
    stream = jnp.concatenate(
        [
            add_branch(joined(in_t), weights[0], scales[0], time_x[...]),
            add_branch(joined(in_f), weights[1], scales[1], spec_x[...]),
        ],
        axis=1,
    )
    traffic.ready(0)
    rows_t[...] = jnp.zeros_like(rows_t)
    rows_t[:live, :] = time_dy[0].astype(F32)
    upstream = jnp.concatenate([rows_t[...].T, spec_dy[0].astype(F32).T], axis=1)
    unit, scale_inv = norm_parts(stream)
    normed = (unit * gain + shift).astype(BF)
    grad_branch = (scale * upstream).astype(BF)
    branch = grad_normed = None
    for g in range(group):
        hidden = mul(w_first[g], normed, TN)
        active, slope = gelu_pair(hidden)
        actives[g] = active.astype(BF)
        made = mul(w_second[g], actives[g], TN)
        branch = made if branch is None else branch + made
        grad_hiddens[g] = (mul(w_second[g], grad_branch, NN) * slope).astype(BF)
        made = mul(w_first[g], grad_hiddens[g], NN)
        grad_normed = made if grad_normed is None else grad_normed + made
    value = upstream + norm_back(unit, scale_inv, grad_normed * gain)
    mixed_gradients(value, weights, scales, (out_t, out_f))
    copies_t = send_blocks(out_t, back_t, sems_t)
    copies_f = send_blocks(out_f, back_f, sems_f)
    last = 2 * width + 2 * local
    for g in range(group):
        grads[g, :width] = mul(normed, grad_hiddens[g], NT).astype(BF)
        grads[g, width : 2 * width] = mul(actives[g], grad_branch, NT).astype(BF)
    output_gradients(value, (in_t, in_f), grads, 2 * width)
    sums = jnp.concatenate(
        [
            jnp.sum(item, axis=1, keepdims=True)
            for item in (grad_normed * unit, grad_normed, upstream * branch)
        ] + [jnp.zeros((width, LANES - 3), F32)],
        axis=1,
    ).T[:16].astype(BF)
    for g in range(group):
        grads[g, last : last + 16] = sums if g == 0 else jnp.zeros_like(sums)
    core = lax.rem(me, 2)
    rows_turn, rows_half = grads.shape[1], turn_in.shape[0] // 2
    copies = [
        push(grads.at[2 * n + 1 - core], held_core.at[n], sems_c.at[0, n], sems_c.at[1, n], mate) for n in range(2)
    ]
    result[...] = stream + scale * branch
    grad_stream[...] = value
    traffic.done(result, grad_stream)
    traffic.ready(1)
    for copy in copies_t:
        copy.wait()
    time_side, spec_side = (kept[6], kept[1], kept[7]), (kept[8], kept[4], kept[9])
    back_time(spec_side, kept, totals, back_t, mix_t, ds_t, query, upstream_ref, grad_k, grad_v)
    keep_keys(False, ds_f, grad_k, grad_v, (0, LANES), grad_k.shape[1], group, block_f)
    for n, copy in enumerate(copies):
        copy.wait()
        made = grads[2 * n + core].astype(F32) + held_core[n].astype(F32)
        first = n * rows_half
        turn_in[first : first + rows_turn] = made.astype(BF)
        if rows_half > rows_turn:
            turn_in[first + rows_turn : first + rows_half] = jnp.zeros((rows_half - rows_turn, width), BF)
    halving = Halving(turn_in, turn_stage, turn_in, sems_h, parts_turn)
    halving.start()
    prepare_queries(kept[3], totals[1], query)
    scatter = Scatter(terms_f, held_f, sems_q)
    size_t = kept[6].shape[0]
    for step, n in enumerate((across, far, mate, me)):
        lanes = lanes_of(n, block_f)
        if step < 3:
            copies_f[step].wait()
        prepare_upstream(back_f[n], mix_f[n], upstream_ref, lanes)
        if step == 2:
            scatter.middle()
        for head in range(2):
            back_unit(head, lanes, step == 0, time_side, query, upstream_ref, ds_f, grad_k, grad_v)
        terms_f[n] = mul(backward[1, 1], ds_f[:, lanes], NN).astype(BF)
        if step == 1:
            scatter.start_far()
        if step == 2:
            scatter.start_mate()
    keep_keys(True, ds_t, grad_k, grad_v, (0, LANES), size_t, group, block_t)
    for g in range(group):
        terms_t[g] = mul(backward[1, 0], ds_t[:, g * block_t : (g + 1) * block_t], NN).astype(BF)
    scatter_t = Scatter(terms_t, held_t, sems_p)
    scatter_t.start()
    halving.finish()
    halving.start()
    scatter_t.middle()
    store_rows(grads_in, ((ds_t, time_all), (ds_f, spec_all)))
    grad_norm[:, :LANES] = scatter_t.finish()
    grad_norm[:, LANES:] = scatter.finish()
    halving.finish()
    while halving.at < halving.steps - 1:
        halving.start()
        halving.finish()
    for n, (first, rows) in enumerate(halving.state):
        turn_part[n * rows : (n + 1) * rows] = turn_in[rows_of(first, rows), :]


def store_rows(target, streams):
    start = 0
    for n, (ds, whole) in enumerate(streams):
        for block in range(3):
            total = row_gradients(ds, whole, slice(block * LANES, (block + 1) * LANES))
            for head in range(2):
                target[start : start + HD] = total[head * HP : head * HP + HD].astype(BF)
                start += HD
        made = row_sums(ds, n)
        sums = made if n == 0 else sums + made
    target[start : start + 16] = sums.astype(BF)


def row_sums(ds, n):
    row = lax.broadcasted_iota(jnp.int32, (16, ds.shape[1]), 0)
    return mul((row == n).astype(BF), ds[...], NT)


def store_head(target, head, ds, whole):
    tiles = whole.shape[1] // LANES
    count = 3 * HD + 16
    for block in range(3):
        base = block * LANES + head * HP
        total = row_gradients(ds, whole, slice(base, base + HP))[:HD].astype(BF)
        for n in range(tiles):
            start = n * count + block * HD
            target[start : start + HD] = total[:, n * LANES : (n + 1) * LANES]
    sums = row_sums(ds, 0).astype(BF)
    for n in range(tiles):
        target[n * count + 3 * HD : (n + 1) * count] = sums[:, n * LANES : (n + 1) * LANES]
    if target.shape[0] > tiles * count:
        target[tiles * count :] = jnp.zeros_like(target[tiles * count :])


def load_head(target, tiles):
    count = 3 * HD + 16
    return jnp.concatenate([target[n * count : (n + 1) * count] for n in range(tiles)], axis=1)


def fourth_kernel(
    parts_turn, parts_in, parts_out, traffic, grad_norm, grad_in, time_y, spec_y, time_x, spec_x, in_t, in_f,
    w_out, cols, time_all, spec_all, backward, mix_t, mix_f, *rest,
):
    kept, totals = rest[:10], rest[10:12]
    turn_part, cross_in, attn_in, attn_out, small = rest[12:17]
    stream_grad, grad_a, grad_b, grad_c, grad_d, packed, scalars = rest[17:24]
    (turn_in, turn_stage, turn_out, turn_far, turn, cross, late_a, late_b, out, cross_one, late_a_one, late_b_one, out_one,
     cross_two, out_two, late_a_two, late_b_two, grads, out_t, out_f, back_t, back_f, terms_t, terms_f, held_t, held_f, held_two,
     ds_t, ds_f, query, upstream_ref, grad_k, grad_v, pieces, sems_q, sems_two, sems_three, sems_t, sems_f, sems_p, sems_y, sems_s,
     sems_turn, sems_cross, sems_a, sems_b, sems_out) = rest[24:]
    me, mate, across, far = places()
    size = lax.axis_size("dp")
    greet((mate, across, far), [lax.rem(lax.axis_index("dp") + n, size) for n in range(1, size)])
    group, local, block_t = mix_t.shape
    block_f, width = mix_f.shape[2], w_out.shape[2]

    def both(first, stage, last, sems, cut):
        return Chain(Halving(first, stage, last, sems.at[0], cut), Doubling(last, sems.at[1], cut))

    rest_parts = [segment_after(part) for part in parts_turn]
    rows = turn_part.shape[0] // len(parts_turn)
    for n, (first, count, _) in enumerate(rest_parts):
        turn_in[rows_of(first, rows), :] = turn_part[n * rows : (n + 1) * rows]
    rows_cross, rows_out = cross_in.shape[0], grads.shape[1]
    cross_one[:rows_cross] = cross_in[...]
    if cross_one.shape[0] > rows_cross:
        cross_one[rows_cross:] = jnp.zeros_like(cross_one[rows_cross:])
    chain_turn = Chain(
        Halving(turn_in, turn_stage, turn_out, sems_s, rest_parts),
        Chips(turn_out, turn_far, turn, sems_y, parts_turn), Doubling(turn, sems_turn, parts_turn[: len(parts_turn) // 2]),
    )
    chain_cross = both(cross_one, cross_two, cross, sems_cross, parts_in)
    chain_out = both(out_one, out_two, out, sems_out, parts_out)
    chain_a = Chain(Direct(late_a_one, late_a_two, late_a, sems_a))
    chain_b = Chain(Direct(late_b_one, late_b_two, late_b, sems_b))
    chain_turn.advance()
    chain_cross.advance()
    unit, scale_inv = norm_parts(jnp.concatenate([time_y[...], spec_y[...]], axis=1))
    value = grad_in[...] + norm_back(unit, scale_inv, grad_norm[...])
    traffic.ready(0)
    weights = (whole_weight(w_out, 0, local), whole_weight(w_out, 1, local))
    mixed_gradients(value, weights, (cols[:, 14:15], cols[:, 15:16]), (out_t, out_f))
    copies_t = send_blocks(out_t, back_t, sems_t)
    copies_f = send_blocks(out_f, back_f, sems_f)
    output_gradients(value, (in_t, in_f), grads, 0)
    scatter = Scatter(grads, held_two, sems_two)
    scatter.start()
    stream_grad[...] = value
    traffic.ready(1)
    for copy in copies_t:
        copy.wait()
    scatter.middle()
    time_side, spec_side = (kept[6], kept[1], kept[7]), (kept[8], kept[4], kept[9])
    size_t, size_f = kept[6].shape[0], kept[8].shape[0]
    back_time(time_side, kept, totals, back_t, mix_t, ds_t, query, upstream_ref, grad_k, grad_v)
    keep_keys(True, ds_t, grad_k, grad_v, (0, LANES), size_t, group, block_t)
    for g in range(group):
        terms_t[g] = mul(backward[0, 0], ds_t[:, g * block_t : (g + 1) * block_t], NN).astype(BF)
    chain_cross.advance()
    out_one[:rows_out] = scatter.finish().astype(BF)
    store_rows(out_one.at[rows_out:], ((ds_t, time_all),))
    rows_used = rows_out + 6 * HD + 16
    if out_one.shape[0] > rows_used:
        out_one[rows_used:] = jnp.zeros_like(out_one[rows_used:])
    chain_out.advance()
    prepare_queries(kept[3], totals[1], query)
    order = ((me, None), (mate, 2), (across, 0), (far, 1))
    moves = (
        (chain_turn, (0, 2, 4, 6)), (chain_cross, (1, 3, 5, 7)), (chain_out, (1, 3, 5, 7)), (chain_a, (6,)),
    )
    for head in range(2):
        for step, (n, arrival) in enumerate(order):
            lanes = lanes_of(n, block_f)
            if head == 0:
                if arrival is not None:
                    copies_f[arrival].wait()
                prepare_upstream(back_f[n], mix_f[n], upstream_ref, lanes)
            back_unit(head, lanes, step == 0, spec_side, query, upstream_ref, ds_f, grad_k, grad_v)
            for chain, when in moves:
                if head * 4 + step in when:
                    chain.advance()
        keep_keys(False, ds_f, grad_k, grad_v, (head * HP, (head + 1) * HP), size_f, group, block_f)
        if head == 0:
            store_head(late_a_one, 0, ds_f, spec_all)
            chain_a.advance()
    scatter_t = Scatter(terms_t, held_t, sems_three)
    scatter = Scatter(terms_f, held_f, sems_q)
    store_head(late_b_one, 1, ds_f, spec_all)
    chain_b.advance()
    for step, n in enumerate((far, across, mate, me)):
        terms_f[n] = mul(backward[0, 1], ds_f[:, lanes_of(n, block_f)], NN).astype(BF)
        if step == 0:
            scatter.start_far()
    scatter.middle()
    scatter.start_mate()
    scatter_t.start()
    scatter_t.middle()
    chains = (chain_turn, chain_cross, chain_out, chain_a)
    for chain in chains:
        chain.advance()
    traffic.ready(2)
    unit, scale_inv = norm_parts(jnp.concatenate([time_x[...], spec_x[...]], axis=1))
    chain_b.advance()
    for chain in chains:
        chain.complete()
    squares = jnp.zeros((1, width), F32)
    packed_rows = [jnp.zeros((1, width), F32) for _ in range(19)]
    tiles = width // LANES

    def add_squares(total, gradient):
        return total + jnp.sum(gradient * gradient, axis=0, keepdims=True)

    def turned(sums):
        return jnp.concatenate([sums, jnp.zeros((LANES - 16, width), F32)], axis=0).T

    def rows_done(squares, pick, plain, sums, lane, block):
        index, group = pick
        column = jnp.concatenate(
            [
                sums[head][block * LANES + head * HP : block * LANES + head * HP + HD, lane : lane + 1]
                for head in range(2)
            ],
            axis=0,
        )
        row = norm_rows[index][group]
        gradient = plain * small[row : row + 1, :] + column * small[row + 1 : row + 2, :]
        grad_a[index, group] = gradient.astype(BF)
        weight = attn_in[index, group]
        packed_rows[row] += jnp.sum(weight * plain, axis=0, keepdims=True)
        packed_rows[row + 1] += jnp.sum(weight * column, axis=0, keepdims=True)
        return add_squares(squares, gradient)

    rows = cross[: 12 * HD + 16].astype(F32)
    sums = (turned(rows[12 * HD :]),) * 2
    for stream, picks in enumerate(picks_of(True)):
        for block, pick in enumerate(picks):
            start = (stream * 6 + block * 2) * HD
            squares = rows_done(squares, pick, rows[start : start + local], sums, stream, block)
    rows = out[rows_out : rows_out + 6 * HD + 16].astype(F32)
    sums = (turned(rows[6 * HD :]),) * 2
    for block, pick in enumerate(picks_of(False)[0]):
        squares = rows_done(squares, pick, rows[block * local : (block + 1) * local], sums, 0, block)
    for index in range(4):
        if index < 2:
            plain = out[index * local : (index + 1) * local].astype(F32)
        else:
            start = 2 * width + (index - 2) * local
            plain = turn[start : start + local].astype(F32)
        gradient = plain * small[14 + index : 15 + index, :]
        grad_b[index] = gradient.astype(BF)
        squares = add_squares(squares, gradient)
        packed_rows[14 + index] += jnp.sum(attn_out[index] * plain, axis=0, keepdims=True)
    for target, start in ((grad_c, 0), (grad_d, width)):
        target[...] = turn[start : start + width]
        squares = add_squares(squares, turn[start : start + width].astype(F32))
    smalls = turn[2 * width + 2 * local : 2 * width + 2 * local + 16].astype(F32)
    for n, row in enumerate((12, 13, 18)):
        packed_rows[row] += smalls[n : n + 1]
    traffic.done(grad_b, grad_c, grad_d)
    chain_b.advance()
    halves = [load_head(late, tiles).astype(F32) for late in (late_a, late_b)]
    sums = [turned(half[3 * HD :]) for half in halves]
    for block, pick in enumerate(picks_of(False)[1]):
        plain = jnp.concatenate([half[block * HD : (block + 1) * HD] for half in halves], axis=0)
        squares = rows_done(squares, pick, plain, sums, 0, block)
    pieces[me] = jnp.concatenate(packed_rows + [squares] + [jnp.zeros((4, width), F32)], axis=0)
    copies = [
        push(pieces.at[me], pieces.at[me], sems_p.at[0, n], sems_p.at[1, n], other)
        for n, other in enumerate((across, far, mate))
    ]
    traffic.done(grad_a)
    scaled = jnp.concatenate([scatter_t.finish(), scatter.finish()], axis=1)
    stream_grad[...] = stream_grad[...] + norm_back(unit, scale_inv, scaled)
    traffic.done(stream_grad)
    for copy in copies:
        copy.wait()
    total = pieces[0]
    for n in range(1, pieces.shape[0]):
        total = total + pieces[n]
    packed[...] = total
    row = lax.broadcasted_iota(jnp.int32, total.shape, 0)
    every = jnp.where(row < 19, total * total, jnp.where(row == 19, total, 0.0))
    norm = jnp.sqrt(jnp.sum(jnp.sum(every, axis=0, keepdims=True), axis=1, keepdims=True))
    factor = jnp.minimum(1.0, clip_level / norm)
    lane = lax.broadcasted_iota(jnp.int32, scalars.shape, 1)
    scalars[...] = jnp.where(lane == 0, norm, factor)


def adam_parts(weight, first_moment, second_moment, gradient, step_rate, decay_rate):
    first_new = beta_first * first_moment + (1.0 - beta_first) * gradient
    second_new = beta_second * second_moment + (1.0 - beta_second) * gradient * gradient
    first_fix = 1.0 - beta_first**STEP
    second_fix = 1.0 - beta_second**STEP
    direction = (first_new * (1.0 / first_fix)) / (jnp.sqrt(second_new * (1.0 / second_fix)) + adam_eps)
    return (weight - step_rate * (direction + decay_rate * weight), first_new, second_new)


last_order = (0, 1, 2, 3)


def last_kernel(live, traffic, scalars, packed, small, small_m, small_v, result, stream_grad, *refs):
    held, outs = refs[:16], refs[16:28]
    small_outs, (time_out, spec_out, time_grad, spec_grad, shift_gradient, norm) = refs[28:31], refs[31:37]
    sems_out = refs[37]
    rates = (rate_matrix, rate_output, rate_matrix, rate_matrix)
    factor = scalars[:, 1:2]
    gradient = packed[: small.shape[0]] * factor
    made = adam_parts(small[...], small_m[...], small_v[...], gradient, rate_small, 0.0)
    for target, value in zip(small_outs, made):
        target[...] = value
    shift_gradient[...] = gradient[13:14].reshape(-1)
    norm[...] = scalars[:, 0:1]
    leaving = []
    for place, n in enumerate(last_order):
        traffic.ready(place)
        gradient, weight, first_moment, second_moment = held[4 * n : 4 * n + 4]
        made = adam_parts(
            weight[...], first_moment[...], second_moment[...], gradient[...].astype(F32) * factor, rates[n], decay_matrix
        )
        for m, (target, value) in enumerate(zip((weight, first_moment, second_moment), made)):
            target[...] = value
            leaving.append(pltpu.make_async_copy(target, outs[3 * n + m], sems_out.at[3 * n + m]))
            leaving[-1].start()
        if place == 2:
            traffic.ready(4)
            for source, one, two in ((result, time_out, spec_out), (stream_grad, time_grad, spec_grad)):
                one[...] = source[:, :LANES].T[:live].reshape(live, 1, -1)
                two[0] = source[:, LANES:].T
                traffic.done(one, two)
    for copy in leaving:
        copy.wait()


def shards(
    time_in, spec_in, rate_flags, band_limits, time_cot, spec_cot, attn_in, attn_out, ffn_in, ffn_out, small,
    attn_in_m, attn_in_v, attn_out_m, attn_out_v, ffn_in_m, ffn_in_v, ffn_out_m, ffn_out_v, small_m, small_v,
):
    group, size = lax.axis_size("mp"), lax.axis_size("dp")
    live = time_in.shape[1]
    count = -(-live // 16) * 16
    block_t, block_f = LANES, spec_in.shape[1]
    width, local, part = time_in.shape[2], attn_in.shape[2], ffn_in.shape[1]
    lanes = block_t + block_f
    size_t, size_f, rows_t = group * block_t, group * block_f, group * count

    whole = (shape_of((group, width, block_t), BF), shape_of((group, width, block_f), BF))
    stream = (shape_of((width, block_t), F32), shape_of((width, block_f), F32))
    mix = (shape_of((group, local, block_t), BF), shape_of((group, local, block_f), BF))
    kept_shapes = tuple(
        shape_of(s, BF)
        for s in [(LANES, size_t)] + [(LANES, rows_t)] * 2 + [(LANES, size_f)] * 3 + [(rows_t, LANES)] * 2
        + [(size_f, LANES)] * 2
    ) + (shape_of((2, size_t), F32), shape_of((2, size_f), F32))
    packed_weights = (2, 3 * LANES, width)
    score = pltpu.VMEM((2, size_f, max(size_t, block_f)), F32)
    smem = pl.BlockSpec(memory_space=pltpu.SMEM)

    rows_w, parts_w = cut_parts(width, size)
    rows_ffn, parts_ffn = cut_parts(2 * width, size)
    bits = len(parts_w[0][2])
    count_w, count_ffn = len(parts_w), len(parts_ffn)
    made = call(
        functools.partial(forward_kernel, live, parts_w, parts_ffn), "forward",
        (stream + whole + mix + mix + kept_shapes) * 2 + (
            shape_of((2, 2, width, 3 * LANES), BF), shape_of((group, rows_w, width), BF),
            shape_of((group, rows_ffn, width), BF), shape_of((width, LANES), F32),
        ),
        (time_in, spec_in, rate_flags, band_limits, attn_in, attn_out, ffn_in, ffn_out, small),
        [
            pltpu.VMEM(packed_weights, BF), pltpu.VMEM((2, 3 * LANES, 1), F32),
            pltpu.VMEM(packed_weights, BF), pltpu.VMEM((2, 3 * LANES, 1), F32), pltpu.VMEM((1, size_f), F32),
            pltpu.VMEM((LANES, width), F32), score, pltpu.VMEM((2, 2, HP, block_f), F32), pltpu.VMEM((2, 2, block_f), F32),
            dma(6), dma(2, 6), dma(2, 3), dma(2, 3), dma(2, count_w), dma(2, count_w, bits), dma(2, 1), dma(2, 1),
            dma(2, count_ffn), dma(6), dma(2, 6), dma(2, 3), dma(2, 3), dma(2, count_ffn, bits), dma(2, 1), dma(2, 1),
        ],
        0, specs={2: smem, 3: smem}, late=((4,),),
        early=tuple(range(24)) + tuple(range(28, 38)) + (40, 41, 43),
    )
    (time_x, spec_x, time_all, spec_all, mix_t, mix_f, all_t, all_f), kept = made[:8], made[8:20]
    (time_y, spec_y, time_all_y, spec_all_y, mix_t_y, mix_f_y, all_t_y, all_f_y), kept_y = made[20:28], made[28:40]
    backward, w_out, w_ffn, cols = made[40:]

    rows_turn, rows_in = width + part + 2 * local + 16, 6 * local + 16
    back_scratch = [
        pltpu.VMEM((3 * LANES, size_t), BF), pltpu.VMEM((3 * LANES, size_f), BF),
        pltpu.VMEM((2, LANES, size_f), BF), pltpu.VMEM((2, LANES, size_f), BF),
        pltpu.VMEM((LANES, size_f), F32), pltpu.VMEM((LANES, size_f), F32),
    ]
    mixes = [pltpu.VMEM(m.shape, BF) for m in mix + mix]
    rows_pair, parts_turn = cut_parts(rows_turn, size)
    parts_turn = parts_turn + [(first + rows_pair, rows, order) for first, rows, order in parts_turn]
    pair = pltpu.VMEM((2 * rows_pair, width), BF)
    terms = [pltpu.VMEM((group, width, block_t), BF), pltpu.VMEM((group, width, block_f), BF)]
    result, grad_stream, turn_part, cross_in, grad_norm = call(
        functools.partial(third_kernel, live, parts_turn), "third",
        (
            shape_of((width, lanes), F32), shape_of((width, lanes), F32), shape_of((4 * rows_pair // size, width), BF),
            shape_of((rows_in, width), BF), shape_of((width, lanes), F32),
        ),
        (
            all_t_y, all_f_y, time_y, spec_y, w_out, w_ffn, cols, time_cot, spec_cot,
            time_all_y, spec_all_y, backward, mix_t_y, mix_f_y,
        ) + tuple(kept_y),
        [pltpu.VMEM((group, rows_turn, width), BF)] + mixes + [pltpu.VMEM((LANES, width), F32)] + terms + terms + [
            pltpu.VMEM((2, rows_turn, width), BF), pair, pair,
            pltpu.VMEM((group, part, lanes), BF), pltpu.VMEM((group, part, lanes), BF),
        ] + back_scratch + [dma(2, 3), dma(2, 3), dma(2, 3), dma(2, 3), dma(2, 2), dma(2, 4, bits)], 2,
        late=((5, 7, 8), tuple(range(9, 26))), early=(0, 1),
    )

    rows_sum, parts_in = cut_parts(rows_in, size)
    rows_out, parts_out = cut_parts(5 * local + 16, size)
    rows_late, _ = cut_parts((width // LANES) * (3 * HD + 16), size)
    sums, late, outs = (
        pltpu.VMEM(shape, BF) for shape in ((rows_sum, width), (rows_late, LANES), (rows_out, width))
    )
    pieces = pltpu.VMEM((size - 1, rows_late // size, LANES), BF)
    stream_grad, grad_a, grad_b, grad_c, grad_d, packed, scalars = call(
        functools.partial(fourth_kernel, parts_turn, parts_in, parts_out), "fourth",
        (
            shape_of((width, lanes), F32), shape_of(attn_in.shape, BF), shape_of(attn_out.shape, BF),
            shape_of(ffn_in.shape, BF), shape_of(ffn_out.shape, BF), shape_of((24, width), F32), shape_of((1, LANES), F32),
        ),
        (
            grad_norm, grad_stream, time_y, spec_y, time_x, spec_x, all_t, all_f, w_out, cols,
            time_all, spec_all, backward, mix_t, mix_f,
        ) + tuple(kept) + (turn_part, cross_in, attn_in, attn_out, small),
        [pair, pair, pair, pltpu.VMEM((rows_pair // size, width), BF), pltpu.VMEM((rows_pair, width), BF)] + [sums, late, late, outs] * 2 + [
            sums, outs, pieces, pieces, pltpu.VMEM((group, 2 * local, width), BF)] + mixes + terms + terms + [pltpu.VMEM((4, 2 * local, width), BF)]
        + back_scratch + [
            pltpu.VMEM((group, 24, width), F32), dma(2, 3), dma(2, 3), dma(2, 3), dma(2, 3), dma(2, 3), dma(2, 3), dma(2, 2), dma(2, 4, 1),
            dma(2, 2, bits), dma(2, 2, 5, bits), dma(2, 2, size - 1), dma(2, 2, size - 1), dma(2, 2, 4, bits),
        ], 3,
        late=((8, 6, 7), tuple(range(10, 27)), (4, 5, 29, 30, 31)), early=(0, 1, 2, 3, 4),
    )

    ins, outs = [], []
    for gradient, weight, first_moment, second_moment in (
        (grad_a, attn_in, attn_in_m, attn_in_v), (grad_b, attn_out, attn_out_m, attn_out_v),
        (grad_c, ffn_in, ffn_in_m, ffn_in_v), (grad_d, ffn_out, ffn_out_m, ffn_out_v),
    ):
        flat = (weight.size // width, width)
        ins += [value.reshape(flat) for value in (gradient, weight, first_moment, second_moment)]
        outs += [shape_of(flat, F32)] * 3
    outs += [shape_of(small.shape, F32)] * 3
    outs += [shape_of((live, 1, width), F32), shape_of((1, block_f, width), F32)] * 2
    outs += [shape_of((width,), F32), shape_of((1, 1), F32)]
    made = call(
        functools.partial(last_kernel, live), "last", outs, (scalars, packed, small, small_m, small_v, result, stream_grad, *ins),
        [dma(12)], None, late=tuple(tuple(range(7 + 4 * n, 11 + 4 * n)) for n in last_order) + ((5, 6),),
        early=tuple(range(15, 19)), direct=tuple(range(12)),
    )
    updated = [
        value.reshape(weight.shape)
        for value, weight in zip(made[:15], [w for w in (attn_in, attn_out, ffn_in, ffn_out, small) for _ in range(3)])
    ]
    time_out, spec_out, time_grad, spec_grad, shift_gradient, norm = made[15:]
    time_out, time_grad = (jnp.swapaxes(value, 0, 1) for value in (time_out, time_grad))
    return (time_out, spec_out, time_grad, spec_grad, norm[0, 0], *updated, shift_gradient)


def solution(mesh):
    tokens, copied = P("dp", "mp", None), P()
    a, b, c, d = P(None, None, "mp", None), P(None, "mp", None), P(None, "mp"), P("mp", None)
    return jax.shard_map(
        shards,
        mesh=mesh,
        in_specs=(
            tokens, tokens, P("dp"), P("dp"), tokens, tokens, a, b, c, d, copied,
            a, a, b, b, c, c, d, d, copied, copied,
        ),
        out_specs=(
            tokens, tokens, tokens, tokens, copied,
            a, a, a, b, b, b, c, c, c, d, d, d, copied, copied, copied, copied,
        ),
        check_vma=False,
    )
```
